32 devices in a mesh: section: 2 (over x), group: 4 (over z), narrow: 4 (over y, core).
Axes of the slice: x: 2, y: 2, z: 4, core: 2. Of those that a mesh axis runs over, the one named last changes fastest.
Arguments:
- boundary: bfloat16 [2, 8, 1024, 768], P('section', 'group', 'narrow'), may hold values from -6 to 6
- segments: int32 [8, 1024], P('group'), may hold values from 0 to 3, never falling along the last dimension, each value on 1 to 769 neighbouring positions
- qkv_weight: bfloat16 [2, 768, 2304], P('section'), may hold values from -0.21875 to 0.21875
- proj_weight: bfloat16 [2, 768, 768], P('section'), may hold values from -3 to 3
- fc1_weight: bfloat16 [2, 768, 3072], P('section'), may hold values from -0.21875 to 0.21875
- fc2_weight: bfloat16 [2, 3072, 768], P('section'), may hold values from -0.109375 to 0.109375
- gains: float32 [2, 4, 768], P('section'), may hold values from 0.5 to 1.5
- biases: float32 [2, 6, 768], P('section'), may hold values from -1.8 to 1.8
- fc1_bias: float32 [2, 3072], P('section'), may hold values from -1.8 to 1.8
Outputs:
- results: bfloat16 [2, 8, 1024, 768], P('section', 'group', 'narrow')
- grad_qkv: float32 [2, 768, 2304], P('section', 'narrow')
- grad_proj: float32 [2, 768, 768], P('section', 'narrow')
- grad_fc1: float32 [2, 768, 3072], P('section', 'narrow')
- grad_fc2: float32 [2, 3072, 768], P('section', 'narrow')
- grad_gains: float32 [2, 4, 768], P('section', None, 'narrow')
- grad_biases: float32 [2, 6, 768], P('section', None, 'narrow')
- grad_fc1_bias: float32 [2, 3072], P('section', 'narrow')
The draws below stay inside these ranges and needn't reach their ends.
Inputs may be any that keep to these rules, and one draw needn't show every extreme that they name: `segments`: along each sequence the segment numbers never fall, every number 0 to 3 occurs, each image has 1 to 769 tokens and one image of every sequence has exactly 769.
All inputs are finite; a program needn't handle non-finite values.
Results may differ from the reference program's by a relative error of at most 0.014.
Values may be sent and summed in bfloat16 or wider, within the bound.
A program may use at most 256 MiB of HBM per device.

```python
import math
import jax
import jax.numpy as jnp
import numpy as np
from jax import lax

D = 768
HEADS = 12
HDIM = 64
FF = 3072
LEN = 1024
IMAGES = 4
SEQS = 8
BIG = 769


def level_of(rng, shape, pieces, least, high):
    factor_of = 1.0
    for dim, shards_of in pieces:
        draws = jax.random.uniform(jax.random.fold_in(jax.random.fold_in(rng, 6), dim), (shards_of,), jnp.float32, least / len(pieces), high / len(pieces))
        factor_of = factor_of * jnp.repeat(jnp.exp(draws), shape[dim] // shards_of).reshape((-1,) + (1,) * (len(shape) - 1 - dim))
    return factor_of


def length_profile(number_of, total, reach, lean):
    portions = [(1 << 20) // math.isqrt(standing ** lean) + 1 for standing in range(2, number_of + 1)]
    rest, given = total - reach - (number_of - 1), [1] * (number_of - 1)
    while rest > 0:
        movable = [i for i in range(number_of - 1) if given[i] < reach]
        mass, budget = sum([portions[i] for i in movable]), rest
        for i in movable:
            addition = min(reach - given[i], max(1, budget * portions[i] // mass), rest)
            given[i] = given[i] + addition
            rest = rest - addition
    return np.array([reach] + given)


def uneven(rng, number_of, total, reach, lean):
    if number_of == 2:
        one = jax.random.randint(rng, (), max(1, total - reach), min(reach, total - 1) + 1)
        return jnp.stack([one, total - one])
    tallies = jnp.asarray(length_profile(number_of, total, reach, lean), jnp.int32)
    twos = (number_of - 1) // 2
    donor, sink = tallies[1:1 + 2 * twos:2], tallies[2:2 + 2 * twos:2]
    room = jnp.minimum(donor - 1, reach - sink)
    passed = jax.random.randint(jax.random.fold_in(rng, 1), (twos,), 0, 1 << 20) % (room + 1)
    tallies = tallies.at[1:1 + 2 * twos:2].set(donor - passed).at[2:2 + 2 * twos:2].set(sink + passed)
    return tallies[jax.random.permutation(jax.random.fold_in(rng, 2), number_of)]


def normal_values(rng, dims, width, reach, shards=(), dtype=jnp.bfloat16):
    entries = jax.random.normal(rng, dims, jnp.float32) * width
    if len(shards) > 0:
        entries = level_of(rng, dims, shards, -0.22, 0.18) * entries
    return jnp.clip(entries, min=-reach, max=reach).astype(dtype)


def setup_inputs(seed: int = 0) -> dict:
    keys = jax.random.split(jax.random.key(seed), 10)
    boundary = normal_values(keys[0], (2, SEQS, LEN, D), 1.0, 6.0, ((0, 2), (1, 4), (2, 4)))
    segments = jax.vmap(lambda own: jnp.searchsorted(jnp.cumsum(uneven(own, IMAGES, LEN, BIG, 0)), jnp.arange(LEN), side="right"))(jax.random.split(keys[1], SEQS)).reshape((SEQS, LEN)).astype(jnp.int32)
    qkv_weight = normal_values(keys[2], (2, D, 3 * D), D ** -0.5, 0.21875, ((0, 2),))
    proj_weight = normal_values(keys[3], (2, D, D), 4 ** -0.5, 3.0, ((0, 2),))
    fc1_weight = normal_values(keys[4], (2, D, FF), D ** -0.5, 0.21875, ((0, 2),))
    fc2_weight = normal_values(keys[5], (2, FF, D), FF ** -0.5, 0.109375, ((0, 2),))
    gains = jnp.clip(0.5 + 1.0 * jax.random.uniform(keys[6], (2, 4, D), jnp.float32) ** level_of(keys[6], (2, 4, D), ((0, 2),), -0.2, 0.2), 0.5, 1.5)
    biases = normal_values(keys[7], (2, 6, D), 0.3, 1.8, ((0, 2),), jnp.float32)
    fc1_bias = normal_values(keys[8], (2, FF), 0.3, 1.8, ((0, 2),), jnp.float32)
    return {"boundary": boundary, "segments": segments, "qkv_weight": qkv_weight, "proj_weight": proj_weight, "fc1_weight": fc1_weight, "fc2_weight": fc2_weight, "gains": gains, "biases": biases, "fc1_bias": fc1_bias}


@jax.custom_vjp
def low(v):
    return lax.optimization_barrier(v.astype(jnp.bfloat16)).astype(jnp.float32)

@jax.custom_vjp
def low_back(v):
    return v

def low_keep(v):
    return (low(v), None)

def low_pass(kept, grad):
    return (grad,)

def back_keep(v):
    return (v, None)

def back_low(kept, grad):
    return (low(grad),)
low.defvjp(low_keep, low_pass)
low_back.defvjp(back_keep, back_low)

def normalize(values, scale_vec, shift_vec):
    row_mean = lax.optimization_barrier(jnp.mean(values, -1, keepdims=True))
    centered = values - row_mean
    variance = lax.optimization_barrier(jnp.mean(centered * centered, -1, keepdims=True))
    return centered * lax.rsqrt(variance + 1e-06) * scale_vec + shift_vec

def attend_heads(query, key_rows, value_rows, seg_row):
    count = query.shape[0]
    query_h = query.reshape(count, HEADS, HDIM)
    key_h = key_rows.reshape(count, HEADS, HDIM)
    value_h = value_rows.reshape(count, HEADS, HDIM)
    raw = jnp.einsum('qhd,khd->hqk', query_h, key_h, precision=lax.Precision.HIGHEST)
    scores = low_back(raw * 0.125)
    same = seg_row[:, None] == seg_row[None, :]
    scores = jnp.where(same[None], scores, -1e+30)
    peak = lax.optimization_barrier(jnp.max(scores, -1, keepdims=True))
    expo = jnp.exp(scores - peak)
    probs = low(expo / lax.optimization_barrier(jnp.sum(expo, -1, keepdims=True)))
    mixed = jnp.einsum('hqk,khd->qhd', probs, value_h, precision=lax.Precision.HIGHEST)
    return mixed.reshape(count, D)
attend_saved = jax.checkpoint(attend_heads)

def one_layer(hidden, seg_row, qkv_w, proj_w, fc1_w, fc2_w, gain_rows, bias_rows, fc1_b):
    high = lax.Precision.HIGHEST
    normed = low(normalize(hidden, gain_rows[0], bias_rows[0]))
    qkv = jnp.dot(normed, qkv_w, precision=high)
    query = low_back(low(qkv[:, :D] + bias_rows[1]))
    key_rows = low_back(low(qkv[:, D:2 * D]))
    value_rows = low_back(low(qkv[:, 2 * D:] + bias_rows[2]))
    attended = low_back(low(attend_saved(query, key_rows, value_rows, seg_row)))
    branch = low_back(jnp.dot(attended, proj_w, precision=high) + bias_rows[3])
    middle = hidden + gain_rows[1] * branch
    normed_two = low(normalize(middle, gain_rows[2], bias_rows[4]))
    hidden_pre = low_back(jnp.dot(normed_two, fc1_w, precision=high) + fc1_b)
    activated = low(jax.nn.gelu(hidden_pre, approximate=False))
    mlp_out = low_back(jnp.dot(activated, fc2_w, precision=high) + bias_rows[5])
    return middle + gain_rows[3] * mlp_out

def both_layers(inputs, weights, seg_row):
    first_out = one_layer(inputs, seg_row, *[w[0] for w in weights])
    second_in = low_back(low(first_out))
    return one_layer(second_in, seg_row, *[w[1] for w in weights])

def reference(boundary, segments, qkv_weight, proj_weight, fc1_weight, fc2_weight, gains, biases, fc1_bias):
    weights = (qkv_weight.astype(jnp.float32), proj_weight.astype(jnp.float32), fc1_weight.astype(jnp.float32), fc2_weight.astype(jnp.float32), gains.astype(jnp.float32), biases.astype(jnp.float32), fc1_bias.astype(jnp.float32))
    inputs = boundary[0].astype(jnp.float32)
    cotangent = boundary[1].astype(jnp.float32)

    def per_sequence(totals, item):
        seq_in, seq_cot, seg_row = item
        output, pullback = jax.vjp(lambda arg_in, arg_w: both_layers(arg_in, arg_w, seg_row), seq_in, weights)
        grad_in, grad_w = pullback(seq_cot)
        totals = tuple((acc + part for acc, part in zip(totals, grad_w)))
        return (totals, (grad_in.astype(jnp.bfloat16), output.astype(jnp.bfloat16)))
    zeros = tuple((jnp.zeros(w.shape, jnp.float32) for w in weights))
    sums, (grads_in, outputs) = lax.scan(per_sequence, zeros, (inputs, cotangent, segments))
    results = jnp.stack([grads_in, outputs])
    return (results, sums[0], sums[1], sums[2], sums[3], sums[4], sums[5], sums[6])
```

```python
import functools

import jax
import jax.numpy as jnp
from jax import lax
from jax.experimental import pallas as pl
from jax.experimental.pallas import tpu as pltpu
from jax.sharding import PartitionSpec as P

SECTION, GROUP, NARROW = "section", "group", "narrow"
HALVES = 2
BIG = 1e30
SLOT_ROWS = 192
SLOT_COLS = 256
RING = 6
ZRING = 12
HOP = 2
BF = jnp.bfloat16
F32 = jnp.float32
MESH = pl.DeviceIdType.MESH


def dot_nn(left, right):
    return lax.dot_general(left, right, (((1,), (0,)), ((), ())), preferred_element_type=F32)


def dot_nt(left, right):
    return lax.dot_general(left, right, (((1,), (1,)), ((), ())), preferred_element_type=F32)


def dot_tn(left, right):
    return lax.dot_general(left, right, (((0,), (0,)), ((), ())), preferred_element_type=F32)


def aligned(start, size, unit=128):
    return pl.ds(pl.multiple_of(start, unit), size)


def norm_stats(values):
    mean = jnp.mean(values, -1, keepdims=True)
    centered = values - mean
    var = jnp.mean(centered * centered, -1, keepdims=True)
    rstd = lax.rsqrt(var + 1e-06)
    return centered * rstd, rstd


def norm_back(grad, hat, rstd, gain):
    scaled = grad * gain
    mean_one = jnp.mean(scaled, -1, keepdims=True)
    mean_two = jnp.mean(scaled * hat, -1, keepdims=True)
    return rstd * (scaled - mean_one - hat * mean_two)


def three_parts(column, lane, base):
    high = column.astype(BF).astype(F32)
    rest = column - high
    mid = rest.astype(BF).astype(F32)
    low = rest - mid
    return jnp.where(
        lane == base, high, jnp.where(lane == base + 1, mid, jnp.where(lane == base + 2, low, 0.0))
    )


def kernel(groups, *refs):
    (
        boundary, segf, wqkv_h, wproj_h, wfc1_h, wfc2_h, gains, biases, fc1b,
        results, g_qkv, g_proj, g_fc1, g_fc2, vec_out,
        wqkv, wproj, wfc1, wfc2,
        hin, cot, n1, qaug, kall, vall, ob, zb, rb, n2, gp, act, mb, fout,
        dmb, du, drb, dzb, doaug, dqkv, dkv_send, dkv_recv, dout,
        unit, ckeep, csend, crecv, ysend, yrecv, rown, zsend, zrecv, ostage,
        vec, dcf, vsend, vrecv,
        w_sem, b_sem, bx_sem, kv_ssem, kv_rsem, x_ssem, x_rsem, xb_ssem, xb_rsem,
        dkv_ssem, dkv_rsem, res_sem,
        c_ssem, c_rsem, y_ssem, y_rsem, z_ssem, z_rsem, o_sem,
        v_ssem, v_rsem, credit,
    ) = refs
    sec = lax.axis_index(SECTION)
    grp = lax.axis_index(GROUP)
    nar = lax.axis_index(NARROW)
    yy = nar // 2
    cc = nar % 2
    sib = (sec, grp, nar + 1 - 2 * cc)
    ynb = (sec, grp, (nar + 2) % 4)
    xnb = (1 - sec, grp, nar)
    zright = (sec, grp + 1, nar)
    zleft = (sec, grp - 1, nar)
    has_right = grp < groups - 1
    has_left = grp > 0
    is_first = sec == 0
    is_second = sec == 1

    blk = boundary.shape[2]
    rows = 2 * blk
    width = boundary.shape[3]
    ff = wfc1.shape[1]
    pairs = width // 128
    chunks = rows // blk

    weight_copies = [
        pltpu.make_async_copy(src.at[0], dst, w_sem.at[i])
        for i, (src, dst) in enumerate(
            ((wqkv_h, wqkv), (wproj_h, wproj), (wfc1_h, wfc1), (wfc2_h, wfc2))
        )
    ]
    for copy in weight_copies:
        copy.start()

    def own_block(dst):
        return pltpu.make_async_copy(boundary.at[0, yy], dst.at[aligned(yy * blk, blk)], b_sem)

    def swap_block(dst):
        return pltpu.make_async_remote_copy(
            src_ref=boundary.at[0, 1 - yy],
            dst_ref=dst.at[aligned(yy * blk, blk)],
            send_sem=bx_sem.at[0],
            recv_sem=bx_sem.at[1],
            device_id=ynb,
            device_id_type=MESH,
        )

    @pl.when(is_first)
    def _():
        own_block(hin).start()

    @pl.when(is_second)
    def _():
        own_block(cot).start()

    barrier = pltpu.get_barrier_semaphore()
    for peer in (sib, ynb, xnb):
        pl.semaphore_signal(barrier, inc=1, device_id=peer, device_id_type=MESH)

    @pl.when(has_right)
    def _():
        pl.semaphore_signal(barrier, inc=1, device_id=zright, device_id_type=MESH)

    @pl.when(has_left)
    def _():
        pl.semaphore_signal(barrier, inc=1, device_id=zleft, device_id_type=MESH)

    pl.semaphore_wait(barrier, 3 + has_right.astype(jnp.int32) + has_left.astype(jnp.int32))

    @pl.when(is_first)
    def _():
        swap_block(hin).start()

    @pl.when(is_second)
    def _():
        swap_block(cot).start()

    vec[...] = jnp.zeros_like(vec)
    dcf[...] = jnp.zeros_like(dcf)

    lane_row = lax.broadcasted_iota(jnp.int32, (1, 128), 1)
    first_row = jnp.where(lane_row < 64, 1.0, 0.0).astype(BF)
    second_row = jnp.where(lane_row < 64, 0.0, 1.0).astype(BF)
    half_lane = lax.rem(lane_row, 64)
    penalty_row = jnp.where(half_lane < 4, BIG, 0.0)

    def x_send(dst, src, j, ssem, rsem):
        part = pl.ds(j * blk, blk)
        return pltpu.make_async_remote_copy(
            src_ref=src.at[part],
            dst_ref=dst.at[part],
            send_sem=ssem.at[j],
            recv_sem=rsem.at[j],
            device_id=xnb,
            device_id_type=MESH,
        )

    def kv_copy(which, j):
        ref = (kall, vall)[which]
        start = pl.multiple_of(j * blk, blk)
        return pltpu.make_async_remote_copy(
            src_ref=ref.at[pl.ds(start, blk)],
            dst_ref=ref.at[pl.ds(start + rows, blk)],
            send_sem=kv_ssem.at[which, j],
            recv_sem=kv_rsem.at[which, j],
            device_id=sib,
            device_id_type=MESH,
        )

    for j in range(chunks):
        @pl.when(is_first)
        def _():
            if j == 0:
                own_block(hin).wait()
            else:
                swap_block(hin).wait()

        @pl.when(is_second)
        def _():
            x_send(hin, fout, j, x_ssem, x_rsem).wait_recv()

        block = jnp.where(is_first, (yy + j) % 2, j)
        part = aligned(block * blk, blk)
        hat, _ = norm_stats(hin[part, :].astype(F32))
        n1[part, :] = (hat * gains[0, 0:1, :] + biases[0, 0:1, :]).astype(BF)
        if j == 0:
            weight_copies[0].wait()

        def project(t, carry, part=part):
            cols = aligned(t * 256, 256)
            got = dot_nn(n1[part, :], wqkv[:, cols])

            @pl.when(t < 3)
            def _():
                low = ((got + biases[0, 1:2, cols]).astype(BF) * 0.125).astype(F32)
                penalty = (segf[part, :].astype(F32) - 1.0) * penalty_row
                for i in range(2):
                    pair = low[:, i * 128 : (i + 1) * 128]
                    qaug[t * 4 + 2 * i, part, :] = jnp.where(lane_row < 64, pair, penalty).astype(BF)
                    qaug[t * 4 + 2 * i + 1, part, :] = jnp.where(lane_row < 64, penalty, pair).astype(BF)

            @pl.when((t >= 3) & (t < 6))
            def _():
                kall[part, aligned(t * 256 - width, 256)] = got.astype(BF)

            @pl.when(t >= 6)
            def _():
                at = aligned(t * 256 - 2 * width, 256)
                vall[part, at] = (got + biases[0, 2:3, at]).astype(BF)

            return carry

        lax.fori_loop(3, 9, project, 0)
        kv_copy(0, block).start()
        kv_copy(1, block).start()
        lax.fori_loop(0, 3, project, 0)

    for j in range(chunks):
        kv_copy(0, j).wait()
        kv_copy(1, j).wait()

    def aug_pair(pair):
        cols = aligned(pair * 128, 128)
        keys, values, feats = kall[:, cols], vall[:, cols], segf[...]
        feat_a, feat_b = feats * second_row, feats * first_row
        return (
            (keys * first_row + feat_a, values * first_row + feat_a),
            (keys * second_row + feat_b, values * second_row + feat_b),
        )

    def forward_block(j, carry):
        part = aligned(j * blk, blk)

        def attend(pair, carry):
            outs = []
            for i, (keys, values) in enumerate(aug_pair(pair)):
                base = 64 * (1 - i)
                query = qaug[2 * pair + i, part, :]
                scores = dot_nt(query, keys)
                peak = jnp.max(scores, -1, keepdims=True)
                expo = jnp.exp(scores - peak).astype(BF)
                mixed = dot_nn(expo, values)
                total = mixed[:, base + 4 : base + 5]
                outs.append(mixed / total)
                log_total = peak + jnp.log(total)
                extra = three_parts(-log_total, lane_row, base + 4)
                qaug[2 * pair + i, part, :] = (query.astype(F32) + extra).astype(BF)
            ob[part, aligned(pair * 128, 128)] = jnp.where(lane_row < 64, outs[0], outs[1]).astype(BF)
            return carry

        lax.fori_loop(0, pairs, attend, 0)

        if j == 0:
            for copy in weight_copies[1:]:
                copy.wait()

        branch = dot_nn(ob[part, :], wproj[...]) + biases[0, 3:4, :]
        zb[part, :] = branch.astype(BF)
        middle = hin[part, :].astype(F32) + gains[0, 1:2, :] * branch
        rb[part, :] = middle
        hat, _ = norm_stats(middle)
        n2[part, :] = (hat * gains[0, 2:3, :] + biases[0, 4:5, :]).astype(BF)

        def expand(t, carry):
            cols = aligned(t * 256, 256)
            pre = dot_nn(n2[part, :], wfc1[:, cols]) + fc1b[0:1, cols]
            phi = 0.5 + 0.5 * lax.erf(pre * 0.7071067811865476)
            act[part, cols] = (pre * phi).astype(BF)
            slope = phi + pre * (jnp.exp(-0.5 * pre * pre) * 0.3989422804014327)
            gp[part, cols] = slope.astype(BF)
            return carry

        lax.fori_loop(0, ff // 256, expand, 0)
        mlp = dot_nn(act[part, :], wfc2[...]) + biases[0, 5:6, :]
        mb[part, :] = mlp.astype(BF)
        fout[part, :] = (rb[part, :] + gains[0, 3:4, :] * mlp).astype(BF)
        return carry

    for j in range(chunks):
        forward_block(j, 0)

        @pl.when(is_first)
        def _():
            x_send(hin, fout, j, x_ssem, x_rsem).start()

    @pl.when(is_second)
    def _():
        own_block(cot).wait()
        swap_block(cot).wait()

    for j in range(chunks):
        part = pl.ds(j * blk, blk)

        @pl.when(is_first)
        def _():
            x_send(cot, dout, j, xb_ssem, xb_rsem).wait_recv()

        grad = cot[part, :].astype(F32)
        vec[3:4, :] += jnp.sum(grad * mb[part, :].astype(F32), 0, keepdims=True)
        low = (gains[0, 3:4, :] * grad).astype(BF)
        dmb[part, :] = low
        vec[9:10, :] += jnp.sum(low.astype(F32), 0, keepdims=True)

    def shrink(t, carry):
        cols = aligned(t * 256, 256)
        back = dot_nt(dmb[...], wfc2[cols, :])
        low = (gp[:, cols].astype(F32) * back).astype(BF)
        du[:, cols] = low
        dcf[pl.ds(t, 1), :] = jnp.sum(low.astype(F32), 0, keepdims=True)
        return carry

    lax.fori_loop(0, ff // 256, shrink, 0)

    for j in range(chunks):
        part = pl.ds(j * blk, blk)
        grad_two = dot_nt(du[part, :], wfc1[...])
        hat, rstd = norm_stats(rb[part, :])
        vec[2:3, :] += jnp.sum(grad_two * hat, 0, keepdims=True)
        vec[8:9, :] += jnp.sum(grad_two, 0, keepdims=True)
        middle = cot[part, :].astype(F32) + norm_back(grad_two, hat, rstd, gains[0, 2:3, :])
        drb[part, :] = middle
        vec[1:2, :] += jnp.sum(middle * zb[part, :].astype(F32), 0, keepdims=True)
        low = (gains[0, 1:2, :] * middle).astype(BF)
        dzb[part, :] = low
        vec[7:8, :] += jnp.sum(low.astype(F32), 0, keepdims=True)

        def heads(t, carry, part=part):
            cols = aligned(t * 256, 256)
            grad_o = dot_nt(dzb[part, :], wproj[cols, :]).astype(BF)
            prod = grad_o.astype(F32) * ob[part, cols].astype(F32)
            for i in range(2):
                pair = grad_o[:, i * 128 : (i + 1) * 128].astype(F32)
                both = prod[:, i * 128 : (i + 1) * 128]
                inner_a = jnp.sum(jnp.where(lane_row < 64, both, 0.0), -1, keepdims=True)
                inner_b = jnp.sum(jnp.where(lane_row < 64, 0.0, both), -1, keepdims=True)
                extra_a = three_parts(-inner_a, lane_row, 68)
                extra_b = three_parts(-inner_b, lane_row, 4)
                doaug[t * 4 + 2 * i, part, :] = jnp.where(lane_row < 64, pair, extra_a).astype(BF)
                doaug[t * 4 + 2 * i + 1, part, :] = jnp.where(lane_row < 64, extra_b, pair).astype(BF)
            return carry

        lax.fori_loop(0, width // 256, heads, 0)

    def dkv_copy(index):
        return pltpu.make_async_remote_copy(
            src_ref=dkv_send.at[index],
            dst_ref=dkv_recv.at[index],
            send_sem=dkv_ssem.at[index],
            recv_sem=dkv_rsem.at[index],
            device_id=sib,
            device_id_type=MESH,
        )

    def attend_back(pair, carry):
        sides = aug_pair(pair)
        grads = {}
        for i, (keys, values) in enumerate(sides):
            query = qaug[2 * pair + i]
            outer = doaug[2 * pair + i]
            for half in (1, 0):
                span = slice(half * rows, (half + 1) * rows)
                prob = jnp.exp(dot_nt(keys[span], query))
                diff = dot_nt(values[span], outer)
                slope = (prob * diff).astype(BF)
                grads["v", i, half] = dot_nn(prob.astype(BF), outer)
                grads["k", i, half] = dot_nn(slope, query)
                grads["q", i, half] = dot_tn(slope, keys[span])
        cols = aligned(pair * 128, 128)

        def merged(name, half):
            return jnp.where(lane_row < 64, grads[name, 0, half], grads[name, 1, half])

        dkv_send[pair] = merged("k", 1).astype(BF)
        dkv_send[pairs + pair] = merged("v", 1).astype(BF)
        dkv_copy(pair).start()
        dkv_copy(pairs + pair).start()
        dqkv[:, cols] = ((merged("q", 0) + merged("q", 1)) * 0.125).astype(BF)
        dqkv[:, aligned(width + pair * 128, 128)] = merged("k", 0).astype(BF)
        dqkv[:, aligned(2 * width + pair * 128, 128)] = merged("v", 0).astype(BF)
        return carry

    lax.fori_loop(0, pairs, attend_back, 0)

    def collect(index, carry):
        dkv_copy(index).wait()
        cols = aligned(width + index * 128, 128)
        dqkv[:, cols] = (dqkv[:, cols].astype(F32) + dkv_recv[index].astype(F32)).astype(BF)
        return carry

    lax.fori_loop(0, 2 * pairs, collect, 0)

    for j in range(chunks):
        part = pl.ds(j * blk, blk)
        vec[5:6, :] += jnp.sum(dqkv[part, 0:width].astype(F32), 0, keepdims=True)
        vec[6:7, :] += jnp.sum(dqkv[part, 2 * width : 3 * width].astype(F32), 0, keepdims=True)
        grad_one = dot_nt(dqkv[part, :], wqkv[...])
        hat, rstd = norm_stats(hin[part, :].astype(F32))
        vec[0:1, :] += jnp.sum(grad_one * hat, 0, keepdims=True)
        vec[4:5, :] += jnp.sum(grad_one, 0, keepdims=True)
        total = drb[part, :] + norm_back(grad_one, hat, rstd, gains[0, 0:1, :])
        dout[part, :] = total.astype(BF)

        @pl.when(is_second)
        def _():
            x_send(cot, dout, j, xb_ssem, xb_rsem).start()

    n_fc2 = 2 * (width // 128)
    n_fc1 = ff // SLOT_COLS
    n_proj = width // SLOT_COLS
    n_qkv = 3 * width // SLOT_COLS
    lo_fc1 = n_fc2
    lo_proj = lo_fc1 + n_fc1
    lo_qkv = lo_proj + n_proj
    slots = lo_qkv + n_qkv
    vslot = slots - 6
    d_core = 1
    d_y = 3
    d_z = d_y + 1

    def core_copy(t):
        at = t % RING
        return pltpu.make_async_remote_copy(
            src_ref=csend.at[at], dst_ref=crecv.at[at],
            send_sem=c_ssem.at[at], recv_sem=c_rsem.at[at],
            device_id=sib, device_id_type=MESH,
        )

    def y_copy(t):
        at = t % RING
        return pltpu.make_async_remote_copy(
            src_ref=ysend.at[at], dst_ref=yrecv.at[at],
            send_sem=y_ssem.at[at], recv_sem=y_rsem.at[at],
            device_id=ynb, device_id_type=MESH,
        )

    def z_copy(way, t):
        return pltpu.make_async_remote_copy(
            src_ref=zsend.at[way, t % RING], dst_ref=zrecv.at[way, t % ZRING],
            send_sem=z_ssem.at[way, t % RING], recv_sem=z_rsem.at[way, t % ZRING],
            device_id=(zright, zleft)[way], device_id_type=MESH,
        )

    def v_copy(stage, peer):
        return pltpu.make_async_remote_copy(
            src_ref=vsend.at[stage], dst_ref=vrecv.at[stage],
            send_sem=v_ssem.at[stage], recv_sem=v_rsem.at[stage],
            device_id=peer, device_id_type=MESH,
        )

    def give(which, t, depth, peer):
        @pl.when(t + depth < slots)
        def _():
            pl.semaphore_signal(credit.at[which], inc=1, device_id=peer, device_id_type=MESH)

    def take(which, t, depth):
        @pl.when(t >= depth)
        def _():
            pl.semaphore_wait(credit.at[which], 1)

    def out_copies(t, action):
        src = ostage.at[t % 4]

        @pl.when(t < lo_fc1)
        def _():
            row = (t // (width // 128)) * (2 * SLOT_ROWS)
            cols = aligned((t % (width // 128)) * 128, 128)
            for i in range(2):
                action(pltpu.make_async_copy(
                    src.at[:, i * 128 : (i + 1) * 128],
                    g_fc2.at[pl.ds(pl.multiple_of(row + i * SLOT_ROWS, SLOT_ROWS), SLOT_ROWS), cols],
                    o_sem.at[t % 4, i],
                ))

        for lo, count, ref in ((lo_fc1, n_fc1, g_fc1), (lo_proj, n_proj, g_proj), (lo_qkv, n_qkv, g_qkv)):
            @pl.when((t >= lo) & (t < lo + count))
            def _():
                action(pltpu.make_async_copy(src, ref.at[:, aligned((t - lo) * SLOT_COLS, SLOT_COLS)], o_sem.at[t % 4, 0]))

    def result_copies(action):
        for flag, src in ((is_first, dout), (is_second, fout)):
            @pl.when(flag)
            def _():
                action(pltpu.make_async_copy(
                    src.at[aligned(yy * blk, blk)], results.at[yy], res_sem.at[0]
                ))
                action(pltpu.make_async_remote_copy(
                    src_ref=src.at[aligned((1 - yy) * blk, blk)], dst_ref=results.at[yy],
                    send_sem=res_sem.at[1], recv_sem=res_sem.at[2],
                    device_id=ynb, device_id_type=MESH,
                ))

    def step(s, carry):
        @pl.when(s < slots)
        def _():
            take(0, s, RING)

            @pl.when(s >= RING)
            def _():
                core_copy(s - RING).wait_send()

            at = s % RING
            keep = s % 2

            @pl.when(s < lo_fc1)
            def _():
                row = (s // (width // 128)) * (2 * SLOT_ROWS)
                cols = aligned((s % (width // 128)) * 128, 128)
                for side in range(2):
                    for core in range(2):
                        first = (2 * side + core) * width + row
                        got = dot_tn(act[:, aligned(first, 2 * SLOT_ROWS)], dmb[:, cols])

                        @pl.when(cc == core)
                        def _():
                            for i in range(2):
                                ckeep[keep, side, :, i * 128 : (i + 1) * 128] = got[i * SLOT_ROWS : (i + 1) * SLOT_ROWS]

                        @pl.when(cc != core)
                        def _():
                            for i in range(2):
                                csend[at, side, :, i * 128 : (i + 1) * 128] = got[i * SLOT_ROWS : (i + 1) * SLOT_ROWS].astype(BF)

            for lo, count, left, right in (
                (lo_fc1, n_fc1, n2, du), (lo_proj, n_proj, ob, dzb), (lo_qkv, n_qkv, n1, dqkv)
            ):
                @pl.when((s >= lo) & (s < lo + count))
                def _():
                    cols = aligned((s - lo) * SLOT_COLS, SLOT_COLS)
                    for side in range(2):
                        unit[...] = dot_tn(left[:, side * 2 * SLOT_ROWS : (side + 1) * 2 * SLOT_ROWS], right[:, cols])
                        ckeep[keep, side] = unit[pl.ds(pl.multiple_of(cc * SLOT_ROWS, SLOT_ROWS), SLOT_ROWS), :]
                        csend[at, side] = unit[pl.ds(pl.multiple_of((1 - cc) * SLOT_ROWS, SLOT_ROWS), SLOT_ROWS), :].astype(BF)

            core_copy(s).start()

            @pl.when(s == vslot)
            def _():
                vsend[0, :, 0:width] = vec[...]
                vsend[0, :, width : width + 256] = dcf[...]
                v_copy(0, sib).start()

        t = s - d_core

        @pl.when((t >= 0) & (t < slots))
        def _():
            core_copy(t).wait_recv()
            at = t % RING
            keep = t % 2
            take(1, t, RING)

            @pl.when(t >= RING)
            def _():
                y_copy(t - RING).wait_send()

            away = 1 - yy
            ysend[at] = (ckeep[keep, away] + crecv[at, away].astype(F32)).astype(BF)
            y_copy(t).start()
            rown[t % ZRING] = ckeep[keep, yy] + crecv[at, yy].astype(F32)
            give(0, t, RING, sib)

            @pl.when(t == vslot)
            def _():
                v_copy(0, sib).wait()
                vsend[1] = vsend[0] + vrecv[0]
                v_copy(1, ynb).start()

        t = s - d_y

        @pl.when((t >= 0) & (t < slots))
        def _():
            y_copy(t).wait_recv()
            at = t % ZRING
            rown[at] = rown[at] + yrecv[t % RING].astype(F32)
            give(1, t, RING, ynb)

            @pl.when(t == vslot)
            def _():
                v_copy(1, ynb).wait()
                vsend[2] = vsend[1] + vrecv[1]

        for way in range(2):
            place = grp if way == 0 else groups - 1 - grp
            has_before = place > 0
            has_after = place < groups - 1
            behind = (zleft, zright)[way]
            ahead = (zright, zleft)[way]
            t = s - d_z - place * HOP
            inside = (t >= 0) & (t < slots)

            @pl.when(inside & has_before)
            def _():
                z_copy(way, t).wait_recv()

            @pl.when(inside & has_after)
            def _():
                take(2 + way, t, ZRING)

                @pl.when(t >= RING)
                def _():
                    z_copy(way, t - RING).wait_send()

                @pl.when(has_before)
                def _():
                    zsend[way, t % RING] = (rown[t % ZRING] + zrecv[way, t % ZRING].astype(F32)).astype(BF)

                @pl.when(jnp.logical_not(has_before))
                def _():
                    zsend[way, t % RING] = rown[t % ZRING].astype(BF)

                z_copy(way, t).start()

            @pl.when(t == vslot)
            def _():
                @pl.when(has_before)
                def _():
                    v_copy(2 + way, behind).wait_recv()

                @pl.when(has_after)
                def _():
                    @pl.when(has_before)
                    def _():
                        vsend[3 + way] = vsend[2] + vrecv[2 + way]

                    @pl.when(jnp.logical_not(has_before))
                    def _():
                        vsend[3 + way] = vsend[2]

                    v_send(way, ahead).start()

        late = jnp.maximum(grp, groups - 1 - grp)
        t = s - d_z - late * HOP

        @pl.when((t >= 0) & (t < slots))
        def _():
            at = t % ZRING

            @pl.when(t >= 4)
            def _():
                out_copies(t - 4, lambda copy: copy.wait())

            @pl.when(has_left & has_right)
            def _():
                ostage[t % 4] = (rown[at] + zrecv[0, at].astype(F32) + zrecv[1, at].astype(F32)).astype(BF)

            @pl.when(has_left & jnp.logical_not(has_right))
            def _():
                ostage[t % 4] = (rown[at] + zrecv[0, at].astype(F32)).astype(BF)

            @pl.when(has_right & jnp.logical_not(has_left))
            def _():
                ostage[t % 4] = (rown[at] + zrecv[1, at].astype(F32)).astype(BF)

            out_copies(t, lambda copy: copy.start())

            @pl.when(has_left)
            def _():
                give(2, t, ZRING, zleft)

            @pl.when(has_right)
            def _():
                give(3, t, ZRING, zright)

        @pl.when(s == slots + d_core)
        def _():
            result_copies(lambda copy: copy.start())

        return carry

    def v_send(way, peer):
        return pltpu.make_async_remote_copy(
            src_ref=vsend.at[3 + way], dst_ref=vrecv.at[2 + way],
            send_sem=v_ssem.at[2 + way], recv_sem=v_rsem.at[2 + way],
            device_id=peer, device_id_type=MESH,
        )

    steps = slots + d_z + (groups - 1) * HOP
    lax.fori_loop(0, steps, step, 0)

    for t in range(slots - 4, slots):
        out_copies(t, lambda copy: copy.wait())
    for t in range(slots - RING, slots):
        core_copy(t).wait_send()
        y_copy(t).wait_send()

        @pl.when(has_right)
        def _():
            z_copy(0, t).wait_send()

        @pl.when(has_left)
        def _():
            z_copy(1, t).wait_send()

    @pl.when(has_right)
    def _():
        v_send(0, zright).wait_send()

    @pl.when(has_left)
    def _():
        v_send(1, zleft).wait_send()

    total = vsend[2]
    vec_out[...] = total

    @pl.when(has_left)
    def _():
        vec_out[...] = vec_out[...] + vrecv[2]

    @pl.when(has_right)
    def _():
        vec_out[...] = vec_out[...] + vrecv[3]

    for j in range(chunks):
        @pl.when(is_first)
        def _():
            x_send(hin, fout, j, x_ssem, x_rsem).wait_send()

        @pl.when(is_second)
        def _():
            x_send(cot, dout, j, xb_ssem, xb_rsem).wait_send()

    result_copies(lambda copy: copy.wait())

HEADS = 12
HDIM = 64


def from_behind(block, axis, distance):
    devices = range(lax.axis_size(axis))
    route = [(i - distance, i) for i in devices if i - distance in devices]
    return lax.ppermute(block, axis, route)


def normalize(values, scale_vec, shift_vec):
    row_mean = jnp.mean(values, -1, keepdims=True)
    centered = values - row_mean
    variance = jnp.mean(centered * centered, -1, keepdims=True)
    return centered * lax.rsqrt(variance + 1e-06) * scale_vec + shift_vec


def gelu_exact(values):
    return jax.nn.gelu(values, approximate=False)


def back_dot(left, weight):
    return lax.dot_general(
        left, weight, (((1,), (1,)), ((), ())), preferred_element_type=jnp.float32
    )


def row_contract(left, right):
    return lax.dot_general(
        left, right, (((0,), (0,)), ((), ())), preferred_element_type=jnp.float32
    )


def masked_scores(query, keys_all, seg_row):
    row_count = query.shape[0]
    length = keys_all.shape[0]
    start = lax.axis_index("narrow") * row_count
    own_seg = lax.dynamic_slice_in_dim(seg_row, start, row_count)
    same = own_seg[:, None] == seg_row[None, :]
    raw = (
        jnp.einsum(
            "qhd,khd->hqk",
            query.reshape(row_count, HEADS, HDIM),
            keys_all.reshape(length, HEADS, HDIM),
            preferred_element_type=jnp.float32,
        )
        * 0.125
    )
    return jnp.where(same[None], raw, -1e30)


def forward_layer(inputs, seg_row, weights):
    qkv_w, proj_w, fc1_w, fc2_w, gain_rows, bias_rows, fc1_b = weights
    row_count, model_width = inputs.shape
    normed = normalize(inputs, gain_rows[0], bias_rows[0]).astype(jnp.bfloat16)
    qkv = jnp.dot(normed, qkv_w, preferred_element_type=jnp.float32)
    query = (qkv[:, :model_width] + bias_rows[1]).astype(jnp.bfloat16)
    key_rows = qkv[:, model_width : 2 * model_width].astype(jnp.bfloat16)
    value_rows = (qkv[:, 2 * model_width :] + bias_rows[2]).astype(jnp.bfloat16)
    keys_all, values_all = (
        lax.all_gather(key_rows, "narrow", axis=0, tiled=True),
        lax.all_gather(value_rows, "narrow", axis=0, tiled=True),
    )
    length = keys_all.shape[0]
    scores = masked_scores(query, keys_all, seg_row)
    peak = jnp.max(scores, -1, keepdims=True)
    log_total = peak + jnp.log(jnp.sum(jnp.exp(scores - peak), -1, keepdims=True))
    probs = jnp.exp(scores - log_total).astype(jnp.bfloat16)
    mixed = jnp.einsum(
        "hqk,khd->qhd",
        probs,
        values_all.reshape(length, HEADS, HDIM),
        preferred_element_type=jnp.float32,
    )
    attended = mixed.reshape(row_count, model_width).astype(jnp.bfloat16)
    branch = jnp.dot(attended, proj_w, preferred_element_type=jnp.float32) + bias_rows[3]
    middle = inputs + gain_rows[1] * branch
    normed_two = normalize(middle, gain_rows[2], bias_rows[4]).astype(jnp.bfloat16)
    hidden_pre = jnp.dot(normed_two, fc1_w, preferred_element_type=jnp.float32) + fc1_b
    activated = gelu_exact(hidden_pre).astype(jnp.bfloat16)
    mlp_out = jnp.dot(activated, fc2_w, preferred_element_type=jnp.float32) + bias_rows[5]
    output = middle + gain_rows[3] * mlp_out
    saved = (
        inputs,
        query,
        keys_all,
        values_all,
        log_total,
        attended,
        branch,
        middle,
        hidden_pre,
        mlp_out,
    )
    return (output, saved)


def backward_layer(grad_out, saved, seg_row, weights):
    qkv_w, proj_w, fc1_w, fc2_w, gain_rows, bias_rows, fc1_b = weights
    (
        inputs,
        query,
        keys_all,
        values_all,
        log_total,
        attended,
        branch,
        middle,
        hidden_pre,
        mlp_out,
    ) = saved
    row_count, model_width = inputs.shape
    length = keys_all.shape[0]
    scale_two = jnp.sum(grad_out * mlp_out, 0)
    mlp_grad = (gain_rows[3] * grad_out).astype(jnp.bfloat16)
    activated, gelu_pull = jax.vjp(gelu_exact, hidden_pre)
    grad_fc2 = row_contract(activated.astype(jnp.bfloat16), mlp_grad)
    shift_five = jnp.sum(mlp_grad.astype(jnp.float32), 0)
    pre_grad = gelu_pull(back_dot(mlp_grad, fc2_w))[0].astype(jnp.bfloat16)
    normed_two, norm_pull_two = jax.vjp(normalize, middle, gain_rows[2], bias_rows[4])
    grad_fc1 = row_contract(normed_two.astype(jnp.bfloat16), pre_grad)
    grad_fc1b = jnp.sum(pre_grad.astype(jnp.float32), 0)
    middle_part, gain_two, shift_four = norm_pull_two(back_dot(pre_grad, fc1_w))
    middle_grad = grad_out + middle_part
    scale_one = jnp.sum(middle_grad * branch, 0)
    branch_grad = (gain_rows[1] * middle_grad).astype(jnp.bfloat16)
    grad_proj = row_contract(attended, branch_grad)
    shift_three = jnp.sum(branch_grad.astype(jnp.float32), 0)
    heads_grad = back_dot(branch_grad, proj_w).astype(jnp.bfloat16).reshape(row_count, HEADS, HDIM)
    scores = masked_scores(query, keys_all, seg_row)
    probs = jnp.exp(scores - log_total)
    keys_heads = keys_all.reshape(length, HEADS, HDIM)
    prob_grad = jnp.einsum(
        "qhd,khd->hqk",
        heads_grad,
        values_all.reshape(length, HEADS, HDIM),
        preferred_element_type=jnp.float32,
    )
    inner = jnp.sum(probs * prob_grad, -1, keepdims=True)
    score_grad = (probs * (prob_grad - inner)).astype(jnp.bfloat16)
    query_grad = (
        (
            jnp.einsum("hqk,khd->qhd", score_grad, keys_heads, preferred_element_type=jnp.float32)
            * 0.125
        )
        .reshape(row_count, model_width)
        .astype(jnp.bfloat16)
    )
    key_part = (
        jnp.einsum(
            "hqk,qhd->khd",
            score_grad,
            query.reshape(row_count, HEADS, HDIM),
            preferred_element_type=jnp.float32,
        )
        * 0.125
    ).reshape(length, model_width)
    value_part = jnp.einsum(
        "hqk,qhd->khd", probs.astype(jnp.bfloat16), heads_grad, preferred_element_type=jnp.float32
    ).reshape(length, model_width)
    key_sum, value_sum = (
        lax.psum_scatter(
            key_part.astype(jnp.bfloat16), "narrow", scatter_dimension=0, tiled=True
        ).astype(jnp.float32),
        lax.psum_scatter(
            value_part.astype(jnp.bfloat16), "narrow", scatter_dimension=0, tiled=True
        ).astype(jnp.float32),
    )
    key_grad = key_sum.astype(jnp.bfloat16)
    value_grad = value_sum.astype(jnp.bfloat16)
    qkv_grad = jnp.concatenate([query_grad, key_grad, value_grad], 1)
    normed, norm_pull_one = jax.vjp(normalize, inputs, gain_rows[0], bias_rows[0])
    grad_qkv = row_contract(normed.astype(jnp.bfloat16), qkv_grad)
    input_part, gain_one, shift_zero = norm_pull_one(back_dot(qkv_grad, qkv_w))
    input_grad = middle_grad + input_part
    gain_grads = jnp.stack([gain_one, scale_one, gain_two, scale_two])
    shift_grads = jnp.stack(
        [
            shift_zero,
            jnp.sum(query_grad.astype(jnp.float32), 0),
            jnp.sum(value_grad.astype(jnp.float32), 0),
            shift_three,
            shift_four,
            shift_five,
        ]
    )
    return (
        input_grad,
        (grad_qkv, grad_proj, grad_fc1, grad_fc2, gain_grads, shift_grads, grad_fc1b),
    )


def general_body(
    boundary, segments, qkv_weight, proj_weight, fc1_weight, fc2_weight, gains, biases, fc1_bias
):
    weights = (
        qkv_weight[0],
        proj_weight[0],
        fc1_weight[0],
        fc2_weight[0],
        gains[0],
        biases[0],
        fc1_bias[0],
    )
    local_ends = boundary[0]
    micro_count = local_ends.shape[0]
    first_section = lax.axis_index("section") == 0
    arrived = jnp.zeros(local_ends.shape[1:], jnp.bfloat16)
    stored = []
    outputs = []
    for step_index in range(micro_count + 1):
        lower = min(step_index, micro_count - 1)
        upper = max(step_index - 1, 0)
        inputs = jnp.where(
            first_section, local_ends[lower].astype(jnp.float32), arrived.astype(jnp.float32)
        )
        seg_row = jnp.where(first_section, segments[lower], segments[upper])
        output, saved = forward_layer(inputs, seg_row, weights)
        stored.append((saved, seg_row))
        outputs.append(output)
        if step_index < micro_count:
            arrived = from_behind(output.astype(jnp.bfloat16), "section", 1)
    totals = tuple((jnp.zeros(w.shape, jnp.float32) for w in weights))
    returned = jnp.zeros(local_ends.shape[1:], jnp.bfloat16)
    input_grads = []
    for step_index in range(micro_count + 1):
        lower = min(step_index, micro_count - 1)
        upper = max(step_index - 1, 0)
        picked = jax.tree.map(
            lambda early, later: jnp.where(first_section, early, later),
            stored[upper],
            stored[lower + 1],
        )
        cotangent = jnp.where(
            first_section, returned.astype(jnp.float32), local_ends[lower].astype(jnp.float32)
        )
        is_valid = jnp.where(first_section, step_index >= 1, step_index < micro_count)
        cotangent = jnp.where(is_valid, cotangent, 0.0)
        grad_in, pieces = backward_layer(cotangent, picked[0], picked[1], weights)
        totals = tuple((acc + part for acc, part in zip(totals, pieces)))
        input_grads.append(grad_in)
        if step_index < micro_count:
            returned = from_behind(grad_in.astype(jnp.bfloat16), "section", -1)
    results = jnp.stack(
        [jnp.where(first_section, input_grads[j + 1], outputs[j + 1]) for j in range(micro_count)]
    )
    results = results.astype(jnp.bfloat16)
    within = (
        lax.psum_scatter(
            totals[0].astype(jnp.bfloat16), "narrow", scatter_dimension=0, tiled=True
        ).astype(jnp.float32),
        lax.psum_scatter(
            totals[1].astype(jnp.bfloat16), "narrow", scatter_dimension=0, tiled=True
        ).astype(jnp.float32),
        lax.psum_scatter(
            totals[2].astype(jnp.bfloat16), "narrow", scatter_dimension=0, tiled=True
        ).astype(jnp.float32),
        lax.psum_scatter(
            totals[3].astype(jnp.bfloat16), "narrow", scatter_dimension=0, tiled=True
        ).astype(jnp.float32),
        lax.psum_scatter(
            totals[4].astype(jnp.bfloat16), "narrow", scatter_dimension=1, tiled=True
        ).astype(jnp.float32),
        lax.psum_scatter(
            totals[5].astype(jnp.bfloat16), "narrow", scatter_dimension=1, tiled=True
        ).astype(jnp.float32),
        lax.psum_scatter(
            totals[6].astype(jnp.bfloat16), "narrow", scatter_dimension=0, tiled=True
        ).astype(jnp.float32),
    )
    final = (
        lax.psum(within[0].astype(jnp.bfloat16), "group").astype(jnp.float32),
        lax.psum(within[1].astype(jnp.bfloat16), "group").astype(jnp.float32),
        lax.psum(within[2].astype(jnp.bfloat16), "group").astype(jnp.float32),
        lax.psum(within[3].astype(jnp.bfloat16), "group").astype(jnp.float32),
        lax.psum(within[4].astype(jnp.bfloat16), "group").astype(jnp.float32),
        lax.psum(within[5].astype(jnp.bfloat16), "group").astype(jnp.float32),
        lax.psum(within[6].astype(jnp.bfloat16), "group").astype(jnp.float32),
    )
    return (
        results[None],
        final[0][None],
        final[1][None],
        final[2][None],
        final[3][None],
        final[4][None],
        final[5][None],
        final[6][None],
    )


def segment_features(seg_row, blk, core):
    parts = seg_row.reshape(HALVES, 2, blk)
    ordered = jnp.concatenate([parts[:, core].reshape(-1), parts[:, 1 - core].reshape(-1)])
    lane = jnp.arange(128) % 64
    hot = (ordered[:, None] == lane[None, :]) & (lane < 4)[None, :]
    ones = (lane >= 4) & (lane < 7)
    return (hot | ones[None, :]).astype(BF)


def fused_body(
    groups, boundary, segments, qkv_weight, proj_weight, fc1_weight, fc2_weight, gains, biases, fc1_bias
):
    blk, width = boundary.shape[2:]
    rows, keys = 2 * blk, 4 * blk
    ff = fc1_weight.shape[2]
    heads = width // HDIM
    nar = lax.axis_index(NARROW)
    seg_row = lax.dynamic_index_in_dim(segments, nar // 2, 0, keepdims=False)
    feats = segment_features(seg_row, blk, nar % 2)

    def bf(*shape):
        return pltpu.VMEM(shape, BF)

    def f32(*shape):
        return pltpu.VMEM(shape, F32)

    dma = pltpu.SemaphoreType.DMA
    slot = (SLOT_ROWS, SLOT_COLS)
    scratch = [
        bf(width, 3 * width), bf(width, width), bf(width, ff), bf(ff, width),
        bf(rows, width), bf(rows, width), bf(rows, width), bf(heads, rows, 128),
        bf(keys, width), bf(keys, width), bf(rows, width), bf(rows, width),
        f32(rows, width), bf(rows, width), bf(rows, ff), bf(rows, ff), bf(rows, width), bf(rows, width),
        bf(rows, width), bf(rows, ff), f32(rows, width), bf(rows, width), bf(heads, rows, 128),
        bf(rows, 3 * width), bf(heads, rows, 128), bf(heads, rows, 128), bf(rows, width),
        f32(2 * SLOT_ROWS, SLOT_COLS), f32(2, 2, *slot), bf(RING, 2, *slot), bf(RING, 2, *slot),
        bf(RING, *slot), bf(RING, *slot), f32(ZRING, *slot), bf(2, RING, *slot), bf(2, ZRING, *slot), bf(4, *slot),
        f32(16, width), f32(16, 256), f32(5, 16, width + 256), f32(4, 16, width + 256),
        dma((4,)), dma(()), dma((2,)), dma((2, 2)), dma((2, 2)), dma((2,)), dma((2,)), dma((2,)), dma((2,)),
        dma((heads,)), dma((heads,)), dma((3,)),
        dma((RING,)), dma((RING,)), dma((RING,)), dma((RING,)), dma((2, RING)), dma((2, ZRING)), dma((4, 2)),
        dma((4,)), dma((4,)), pltpu.SemaphoreType.REGULAR((4,)),
    ]
    hbm = pl.BlockSpec(memory_space=pl.ANY)
    vmem = pl.BlockSpec(memory_space=pltpu.VMEM)
    out = pl.pallas_call(
        functools.partial(kernel, groups),
        out_shape=(
            jax.ShapeDtypeStruct((2, blk, width), BF),
            jax.ShapeDtypeStruct((width // 4, 3 * width), BF),
            jax.ShapeDtypeStruct((width // 4, width), BF),
            jax.ShapeDtypeStruct((width // 4, ff), BF),
            jax.ShapeDtypeStruct((ff // 4, width), BF),
            jax.ShapeDtypeStruct((16, width + 256), F32),
        ),
        in_specs=[hbm, vmem, hbm, hbm, hbm, hbm, vmem, vmem, vmem],
        out_specs=(hbm, hbm, hbm, hbm, hbm, vmem),
        scratch_shapes=scratch,
        compiler_params=pltpu.CompilerParams(
            collective_id=0, has_side_effects=True, vmem_limit_bytes=63 * 2**20
        ),
        name="two_layers",
    )(boundary, feats, qkv_weight, proj_weight, fc1_weight, fc2_weight, gains, biases, fc1_bias)
    results, qkv, proj, fc1, fc2, vecs = out
    share = lax.dynamic_slice_in_dim(vecs[:, :width], nar * (width // 4), width // 4, 1)
    fc1_share = lax.dynamic_slice_in_dim(vecs[: ff // 256, width:].reshape(-1), nar * (ff // 4), ff // 4, 0)
    return (
        results[None],
        qkv.astype(F32)[None],
        proj.astype(F32)[None],
        fc1.astype(F32)[None],
        fc2.astype(F32)[None],
        share[:4][None],
        share[4:10][None],
        fc1_share[None],
    )


def solution(mesh):
    sections, groups, narrow = (mesh.shape[name] for name in (SECTION, GROUP, NARROW))
    placed = (
        P("section", "group", "narrow", None),
        P("group", None),
        P("section", None, None),
        P("section", None, None),
        P("section", None, None),
        P("section", None, None),
        P("section", None, None),
        P("section", None, None),
        P("section", None),
    )
    fused = sections == 2 and narrow == 4 and groups > 1
    body = functools.partial(fused_body, groups) if fused else general_body
    return jax.shard_map(
        body,
        mesh=mesh,
        in_specs=placed,
        out_specs=(
            P("section", "group", "narrow", None),
            P("section", "narrow", None),
            P("section", "narrow", None),
            P("section", "narrow", None),
            P("section", "narrow", None),
            P("section", None, "narrow"),
            P("section", None, "narrow"),
            P("section", "narrow"),
        ),
        check_vma=False,
    )
```

```python
import functools

import jax
import jax.numpy as jnp
from jax import lax
from jax.experimental import pallas as pl
from jax.experimental.pallas import tpu as pltpu
from jax.sharding import PartitionSpec as P

SECTION, GROUP, NARROW = "section", "group", "narrow"
HALVES = 2
BIG = 1e30
SLOT_ROWS = 192
SLOT_COLS = 256
RING = 6
ZRING = 8
OWN_RING = 12
HOP = 2
BF = jnp.bfloat16
F32 = jnp.float32
MESH = pl.DeviceIdType.MESH


def dot_nn(left, right):
    return lax.dot_general(left, right, (((1,), (0,)), ((), ())), preferred_element_type=F32)


def dot_nt(left, right):
    return lax.dot_general(left, right, (((1,), (1,)), ((), ())), preferred_element_type=F32)


def dot_tn(left, right):
    return lax.dot_general(left, right, (((0,), (0,)), ((), ())), preferred_element_type=F32)


def aligned(start, size, unit=128):
    return pl.ds(pl.multiple_of(start, unit), size)


def norm_stats(values):
    mean = jnp.mean(values, -1, keepdims=True)
    centered = values - mean
    var = jnp.mean(centered * centered, -1, keepdims=True)
    rstd = lax.rsqrt(var + 1e-06)
    return centered * rstd, rstd


def norm_back(grad, hat, rstd, gain):
    scaled = grad * gain
    mean_one = jnp.mean(scaled, -1, keepdims=True)
    mean_two = jnp.mean(scaled * hat, -1, keepdims=True)
    return rstd * (scaled - mean_one - hat * mean_two)


def three_parts(column, lane, base):
    high = column.astype(BF).astype(F32)
    rest = column - high
    mid = rest.astype(BF).astype(F32)
    low = rest - mid
    return jnp.where(
        lane == base, high, jnp.where(lane == base + 1, mid, jnp.where(lane == base + 2, low, 0.0))
    )


def kernel(groups, *refs):
    (
        boundary, segments, wqkv_h, wproj_h, wfc1_h, wfc2_h, gains, biases, fc1b,
        results, g_qkv, g_proj, g_fc1, g_fc2, vec_out,
        wqkv, wproj, wfc1, wfc2,
        hin, cot, n1, qaug, kall, vall, ob, zb, rb, n2, gp, act, mb, fout,
        dmb, dzb, doaug, dqkv, dkv_send, dkv_recv, dout,
        segf, ckeep, csend, crecv, ysend, yrecv, rown, zsend, zrecv, ostage,
        vec, dcf, vsend, vrecv,
        w_sem, b_sem, bx_sem, kv_ssem, kv_rsem, x_ssem, x_rsem, xb_ssem, xb_rsem,
        dkv_ssem, dkv_rsem, res_sem,
        c_ssem, c_rsem, y_ssem, y_rsem, z_ssem, z_rsem, o_sem,
        v_ssem, v_rsem, credit,
    ) = refs
    du, drb = gp, rb
    sec = lax.axis_index(SECTION)
    grp = lax.axis_index(GROUP)
    nar = lax.axis_index(NARROW)
    yy = nar // 2
    cc = nar % 2
    sib = (sec, grp, nar + 1 - 2 * cc)
    ynb = (sec, grp, (nar + 2) % 4)
    xnb = (1 - sec, grp, nar)
    zright = (sec, grp + 1, nar)
    zleft = (sec, grp - 1, nar)
    has_right = grp < groups - 1
    has_left = grp > 0
    is_first = sec == 0
    is_second = sec == 1

    blk = boundary.shape[2]
    rows = 2 * blk
    width = boundary.shape[3]
    ff = wfc1.shape[1]
    pairs = width // 128
    chunks = rows // blk

    def bias(row):
        return biases[0:1, row * width : (row + 1) * width]

    weight_copies = [
        pltpu.make_async_copy(src.at[0], dst, w_sem.at[i])
        for i, (src, dst) in enumerate(
            ((wqkv_h, wqkv), (wproj_h, wproj), (wfc1_h, wfc1), (wfc2_h, wfc2))
        )
    ]
    for copy in weight_copies:
        copy.start()

    def own_block(dst):
        return pltpu.make_async_copy(boundary.at[0, yy], dst.at[aligned(yy * blk, blk)], b_sem)

    def swap_block(dst):
        return pltpu.make_async_remote_copy(
            src_ref=boundary.at[0, 1 - yy],
            dst_ref=dst.at[aligned(yy * blk, blk)],
            send_sem=bx_sem.at[0],
            recv_sem=bx_sem.at[1],
            device_id=ynb,
            device_id_type=MESH,
        )

    @pl.when(is_first)
    def _():
        own_block(hin).start()

    @pl.when(is_second)
    def _():
        own_block(cot).start()

    barrier = pltpu.get_barrier_semaphore()
    for peer in (sib, ynb, xnb):
        pl.semaphore_signal(barrier, inc=1, device_id=peer, device_id_type=MESH)

    @pl.when(has_right)
    def _():
        pl.semaphore_signal(barrier, inc=1, device_id=zright, device_id_type=MESH)

    @pl.when(has_left)
    def _():
        pl.semaphore_signal(barrier, inc=1, device_id=zleft, device_id_type=MESH)

    pl.semaphore_wait(barrier, 3 + has_right.astype(jnp.int32) + has_left.astype(jnp.int32))

    @pl.when(is_first)
    def _():
        swap_block(hin).start()

    @pl.when(is_second)
    def _():
        swap_block(cot).start()

    keys_seg = jnp.concatenate(
        [
            segments[pl.ds(yy, 1), aligned((half * 2 + core) * blk, blk)]
            for core in (cc, 1 - cc)
            for half in range(2)
        ],
        1,
    )
    feature = lax.rem(lax.broadcasted_iota(jnp.int32, (128, 1), 0), 64)
    hot = jnp.where(keys_seg == feature, 1.0, 0.0)
    ones = jnp.where((feature >= 4) & (feature < 7), 1.0, 0.0)
    segf[...] = jnp.where(feature < 4, hot, ones).T.astype(BF)
    vec[...] = jnp.zeros_like(vec)
    dcf[...] = jnp.zeros_like(dcf)

    lane_row = lax.broadcasted_iota(jnp.int32, (1, 128), 1)
    first_row = jnp.where(lane_row < 64, 1.0, 0.0).astype(BF)
    second_row = jnp.where(lane_row < 64, 0.0, 1.0).astype(BF)
    half_lane = lax.rem(lane_row, 64)
    penalty_row = jnp.where(half_lane < 4, BIG, 0.0)

    def x_send(dst, src, j, ssem, rsem):
        part = aligned(j * blk, blk)
        return pltpu.make_async_remote_copy(
            src_ref=src.at[part],
            dst_ref=dst.at[part],
            send_sem=ssem.at[j],
            recv_sem=rsem.at[j],
            device_id=xnb,
            device_id_type=MESH,
        )

    def kv_copy(which, j):
        ref = (kall, vall)[which]
        start = pl.multiple_of(j * blk, blk)
        return pltpu.make_async_remote_copy(
            src_ref=ref.at[pl.ds(start, blk)],
            dst_ref=ref.at[pl.ds(start + rows, blk)],
            send_sem=kv_ssem.at[which, j],
            recv_sem=kv_rsem.at[which, j],
            device_id=sib,
            device_id_type=MESH,
        )

    for j in range(chunks):
        @pl.when(is_first)
        def _():
            if j == 0:
                own_block(hin).wait()
            else:
                swap_block(hin).wait()

        @pl.when(is_second)
        def _():
            x_send(hin, fout, j, x_ssem, x_rsem).wait_recv()

        block = jnp.where(is_first, (yy + j) % 2, j)
        part = aligned(block * blk, blk)
        hat, _ = norm_stats(hin[part, :].astype(F32))
        n1[part, :] = (hat * gains[0, 0:1, :] + bias(0)).astype(BF)
        if j == 0:
            weight_copies[0].wait()

        normed = n1[part, :]
        kall[part, :] = dot_nn(normed, wqkv[:, width : 2 * width]).astype(BF)
        kv_copy(0, block).start()
        vall[part, :] = (dot_nn(normed, wqkv[:, 2 * width :]) + bias(2)).astype(BF)
        kv_copy(1, block).start()
        low = ((dot_nn(normed, wqkv[:, 0:width]) + bias(1)).astype(BF) * 0.125).astype(F32)
        penalty = (segf[part, :].astype(F32) - 1.0) * penalty_row
        for i in range(pairs):
            pair = low[:, i * 128 : (i + 1) * 128]
            qaug[2 * i, part, :] = jnp.where(lane_row < 64, pair, penalty).astype(BF)
            qaug[2 * i + 1, part, :] = jnp.where(lane_row < 64, penalty, pair).astype(BF)

    for j in range(chunks):
        kv_copy(0, j).wait()
        kv_copy(1, j).wait()

    def aug_pair(pair):
        cols = aligned(pair * 128, 128)
        keys, values, feats = kall[:, cols], vall[:, cols], segf[...]
        feat_a, feat_b = feats * second_row, feats * first_row
        return (
            (keys * first_row + feat_a, values * first_row + feat_a),
            (keys * second_row + feat_b, values * second_row + feat_b),
        )

    def forward_block(j, carry):
        part = aligned(j * blk, blk)

        feats = segf[...]
        own_pen = ((segf[part, :].astype(F32) - 1.0) * penalty_row).astype(BF) * first_row
        scores, sums = {}, {}

        def score(pair):
            cols = slice(pair * 128, (pair + 1) * 128)
            keys = jnp.concatenate([kall[:, cols], feats], 1)
            query = jnp.concatenate(
                [
                    jnp.concatenate([qaug[2 * pair, part, :] * first_row, own_pen], 1),
                    jnp.concatenate([qaug[2 * pair + 1, part, :] * second_row, own_pen], 1),
                ],
                0,
            )
            scores[pair] = dot_nt(query, keys)

        ahead = 2
        for pair in range(ahead):
            score(pair)
        for pair in range(pairs):
            if pair + ahead < pairs:
                score(pair + ahead)
            cols = slice(pair * 128, (pair + 1) * 128)
            peak = jnp.max(scores[pair], -1, keepdims=True)
            expo = jnp.exp(scores.pop(pair) - peak).astype(BF)
            mixed = dot_nn(expo, jnp.concatenate([vall[:, cols], feats], 1))
            total = mixed[:, 132:133]
            outs = mixed[:, 0:128] / total
            log_total = peak + jnp.log(total)
            for i in range(2):
                base = 64 * (1 - i)
                extra = three_parts(-log_total[i * blk : (i + 1) * blk], lane_row, base + 4)
                query = qaug[2 * pair + i, part, :]
                qaug[2 * pair + i, part, :] = (query.astype(F32) + extra).astype(BF)
            ob[part, cols] = jnp.where(lane_row < 64, outs[:blk], outs[blk:]).astype(BF)

        @pl.when(j == 0)
        def _():
            for copy in weight_copies[1:]:
                copy.wait()

        branch = dot_nn(ob[part, :], wproj[...]) + bias(3)
        zb[part, :] = branch.astype(BF)
        middle = hin[part, :].astype(F32) + gains[0, 1:2, :] * branch
        rb[part, :] = middle
        hat, _ = norm_stats(middle)
        n2[part, :] = (hat * gains[0, 2:3, :] + bias(4)).astype(BF)

        def expand(t, carry):
            cols = aligned(t * width, width)
            pre = dot_nn(n2[part, :], wfc1[:, cols]) + fc1b[0:1, cols]
            phi = 0.5 + 0.5 * lax.erf(pre * 0.7071067811865476)
            act[part, cols] = (pre * phi).astype(BF)
            slope = phi + pre * (jnp.exp(-0.5 * pre * pre) * 0.3989422804014327)
            gp[part, cols] = slope.astype(BF)
            return carry

        lax.fori_loop(0, ff // width, expand, 0)
        mlp = dot_nn(act[part, :], wfc2[...]) + bias(5)
        mb[part, :] = mlp.astype(BF)
        fout[part, :] = (rb[part, :] + gains[0, 3:4, :] * mlp).astype(BF)

        @pl.when(is_first)
        def _():
            x_send(hin, fout, j, x_ssem, x_rsem).start()

        return carry

    lax.fori_loop(0, chunks, forward_block, 0)

    n_fc2 = 2 * (width // 128)
    n_fc1 = ff // SLOT_COLS
    n_proj = width // SLOT_COLS
    n_qkv = 3 * width // SLOT_COLS
    lo_fc1 = n_fc2
    lo_proj = lo_fc1 + n_fc1
    lo_qkv = lo_proj + n_proj
    slots = lo_qkv + n_qkv
    vslot = slots - 6
    early = 11 + 2 * pairs
    d_core = 2
    d_y = 4
    d_z = d_y + 1

    def core_copy(t):
        at = t % RING
        return pltpu.make_async_remote_copy(
            src_ref=csend.at[at], dst_ref=crecv.at[at],
            send_sem=c_ssem.at[at], recv_sem=c_rsem.at[at],
            device_id=sib, device_id_type=MESH,
        )

    def y_copy(t):
        at = t % RING
        return pltpu.make_async_remote_copy(
            src_ref=ysend.at[at], dst_ref=yrecv.at[at],
            send_sem=y_ssem.at[at], recv_sem=y_rsem.at[at],
            device_id=ynb, device_id_type=MESH,
        )

    def z_copy(way, t):
        return pltpu.make_async_remote_copy(
            src_ref=zsend.at[way, t % RING], dst_ref=zrecv.at[way, t % ZRING],
            send_sem=z_ssem.at[way, t % RING], recv_sem=z_rsem.at[way, t % ZRING],
            device_id=(zright, zleft)[way], device_id_type=MESH,
        )

    def v_copy(stage, peer):
        return pltpu.make_async_remote_copy(
            src_ref=vsend.at[stage], dst_ref=vrecv.at[stage],
            send_sem=v_ssem.at[stage], recv_sem=v_rsem.at[stage],
            device_id=peer, device_id_type=MESH,
        )

    def give(which, t, depth, peer):
        @pl.when(t + depth < slots)
        def _():
            pl.semaphore_signal(credit.at[which], inc=1, device_id=peer, device_id_type=MESH)

    def take(which, t, depth):
        @pl.when(t >= depth)
        def _():
            pl.semaphore_wait(credit.at[which], 1)

    def out_copies(t, action):
        src = ostage.at[t % 4]

        @pl.when(t < lo_fc1)
        def _():
            row = (t // (width // 128)) * (2 * SLOT_ROWS)
            cols = aligned((t % (width // 128)) * 128, 128)
            for i in range(2):
                action(pltpu.make_async_copy(
                    src.at[:, i * 128 : (i + 1) * 128],
                    g_fc2.at[pl.ds(pl.multiple_of(row + i * SLOT_ROWS, SLOT_ROWS), SLOT_ROWS), cols],
                    o_sem.at[t % 4, i],
                ))

        for lo, count, ref in ((lo_fc1, n_fc1, g_fc1), (lo_proj, n_proj, g_proj), (lo_qkv, n_qkv, g_qkv)):
            @pl.when((t >= lo) & (t < lo + count))
            def _():
                action(pltpu.make_async_copy(src, ref.at[:, aligned((t - lo) * SLOT_COLS, SLOT_COLS)], o_sem.at[t % 4, 0]))

    def result_copies(action):
        for flag, src in ((is_first, dout), (is_second, fout)):
            @pl.when(flag)
            def _():
                action(pltpu.make_async_copy(
                    src.at[aligned(yy * blk, blk)], results.at[yy], res_sem.at[0]
                ))
                action(pltpu.make_async_remote_copy(
                    src_ref=src.at[aligned((1 - yy) * blk, blk)], dst_ref=results.at[yy],
                    send_sem=res_sem.at[1], recv_sem=res_sem.at[2],
                    device_id=ynb, device_id_type=MESH,
                ))

    def own_terms(q, kinds):
        @pl.when(q * 3 >= RING)
        def _():
            for i in range(3):
                core_copy(q * 3 + i - RING).wait_send()

        def place(at, side, rows_of, cols_of, got, core):
            @pl.when(cc == core)
            def _():
                ckeep[at, side, rows_of, cols_of] = got

            @pl.when(cc != core)
            def _():
                csend[at, side, rows_of, cols_of] = got.astype(BF)

        every = slice(None)
        if "fc2" in kinds:
            @pl.when(q < lo_fc1 // 3)
            def _():
                row = (q // 2) * (2 * SLOT_ROWS)
                cols = aligned((q % 2) * 384, 384)
                for side in range(2):
                    for core in range(2):
                        first = (2 * side + core) * width + row
                        got = dot_tn(act[:, aligned(first, 2 * SLOT_ROWS)], dmb[:, cols])
                        for i in range(3):
                            for half in range(2):
                                place(
                                    (q % 2) * 3 + i, side, every, slice(half * 128, half * 128 + 128),
                                    got[half * SLOT_ROWS : (half + 1) * SLOT_ROWS, i * 128 : (i + 1) * 128], core,
                                )

        for name, lo, count, left, right in (
            ("fc1", lo_fc1, n_fc1, n2, du), ("proj", lo_proj, n_proj, ob, dzb), ("qkv", lo_qkv, n_qkv, n1, dqkv)
        ):
            if name in kinds:
                @pl.when((q * 3 >= lo) & (q * 3 < lo + count))
                def _():
                    cols = aligned((q * 3 - lo) * SLOT_COLS, 3 * SLOT_COLS)
                    for side in range(2):
                        got = dot_tn(left[:, side * 2 * SLOT_ROWS : (side + 1) * 2 * SLOT_ROWS], right[:, cols])
                        for i in range(3):
                            for core in range(2):
                                place(
                                    (q % 2) * 3 + i, side, every, every,
                                    got[core * SLOT_ROWS : (core + 1) * SLOT_ROWS, i * SLOT_COLS : (i + 1) * SLOT_COLS], core,
                                )

    def step(s, carry, kinds=("fc2", "fc1", "proj", "qkv")):
        @pl.when(s < slots)
        def _():
            @pl.when(s % 3 == 0)
            def _():
                own_terms(s // 3, kinds)

            take(0, s, RING)
            core_copy(s).start()

            @pl.when(s == vslot)
            def _():
                vsend[0, :, 0:width] = vec[...]
                vsend[0, :, width : width + 256] = dcf[...]
                v_copy(0, sib).start()

        t = s - d_core

        @pl.when((t >= 0) & (t < slots))
        def _():
            core_copy(t).wait_recv()
            at = t % RING
            keep = t % RING
            take(1, t, RING)

            @pl.when(t >= RING)
            def _():
                y_copy(t - RING).wait_send()

            away = 1 - yy
            ysend[at] = (ckeep[keep, away] + crecv[at, away].astype(F32)).astype(BF)
            y_copy(t).start()
            rown[t % OWN_RING] = ckeep[keep, yy] + crecv[at, yy].astype(F32)
            give(0, t, RING, sib)

            @pl.when(t == vslot)
            def _():
                v_copy(0, sib).wait()
                vsend[1] = vsend[0] + vrecv[0]
                v_copy(1, ynb).start()

        t = s - d_y

        @pl.when((t >= 0) & (t < slots))
        def _():
            y_copy(t).wait_recv()
            at = t % OWN_RING
            rown[at] = rown[at] + yrecv[t % RING].astype(F32)
            give(1, t, RING, ynb)

            @pl.when(t == vslot)
            def _():
                v_copy(1, ynb).wait()
                vsend[2] = vsend[1] + vrecv[1]

        for way in range(2):
            place = grp if way == 0 else groups - 1 - grp
            has_before = place > 0
            has_after = place < groups - 1
            behind = (zleft, zright)[way]
            ahead = (zright, zleft)[way]
            t = s - d_z - place * HOP
            inside = (t >= 0) & (t < slots)

            @pl.when(inside & has_before)
            def _():
                z_copy(way, t).wait_recv()

            @pl.when(inside & has_after)
            def _():
                take(2 + way, t, ZRING)

                @pl.when(t >= RING)
                def _():
                    z_copy(way, t - RING).wait_send()

                @pl.when(has_before)
                def _():
                    zsend[way, t % RING] = (rown[t % OWN_RING] + zrecv[way, t % ZRING].astype(F32)).astype(BF)

                @pl.when(jnp.logical_not(has_before))
                def _():
                    zsend[way, t % RING] = rown[t % OWN_RING].astype(BF)

                z_copy(way, t).start()

            @pl.when(t == vslot)
            def _():
                @pl.when(has_before)
                def _():
                    v_copy(2 + way, behind).wait_recv()

                @pl.when(has_after)
                def _():
                    @pl.when(has_before)
                    def _():
                        vsend[3 + way] = vsend[2] + vrecv[2 + way]

                    @pl.when(jnp.logical_not(has_before))
                    def _():
                        vsend[3 + way] = vsend[2]

                    v_send(way, ahead).start()

        late = jnp.maximum(grp, groups - 1 - grp)
        t = s - d_z - late * HOP

        @pl.when((t >= 0) & (t < slots))
        def _():
            at = t % ZRING
            own = t % OWN_RING

            @pl.when(t >= 4)
            def _():
                out_copies(t - 4, lambda copy: copy.wait())

            @pl.when(has_left & has_right)
            def _():
                ostage[t % 4] = (rown[own] + zrecv[0, at].astype(F32) + zrecv[1, at].astype(F32)).astype(BF)

            @pl.when(has_left & jnp.logical_not(has_right))
            def _():
                ostage[t % 4] = (rown[own] + zrecv[0, at].astype(F32)).astype(BF)

            @pl.when(has_right & jnp.logical_not(has_left))
            def _():
                ostage[t % 4] = (rown[own] + zrecv[1, at].astype(F32)).astype(BF)

            out_copies(t, lambda copy: copy.start())

            @pl.when(has_left)
            def _():
                give(2, t, ZRING, zleft)

            @pl.when(has_right)
            def _():
                give(3, t, ZRING, zright)

        @pl.when(s == slots + d_core)
        def _():
            result_copies(lambda copy: copy.start())

        return carry

    def v_send(way, peer):
        return pltpu.make_async_remote_copy(
            src_ref=vsend.at[3 + way], dst_ref=vrecv.at[2 + way],
            send_sem=v_ssem.at[2 + way], recv_sem=v_rsem.at[2 + way],
            device_id=peer, device_id_type=MESH,
        )

    def pump(lo, hi, kinds):
        @pl.when(is_first)
        def _():
            lax.fori_loop(lo, hi, functools.partial(step, kinds=kinds), 0)

    @pl.when(is_second)
    def _():
        own_block(cot).wait()
        swap_block(cot).wait()

    for j in range(chunks):
        part = pl.ds(j * blk, blk)

        @pl.when(is_first)
        def _():
            x_send(cot, dout, j, xb_ssem, xb_rsem).wait_recv()

        grad = cot[part, :].astype(F32)
        vec[3:4, :] += jnp.sum(grad * mb[part, :].astype(F32), 0, keepdims=True)
        low = (gains[0, 3:4, :] * grad).astype(BF)
        dmb[part, :] = low
        vec[9:10, :] += jnp.sum(low.astype(F32), 0, keepdims=True)

    pump(0, 3, ("fc2",))

    def shrink(t, carry):
        cols = aligned(t * width, width)
        back = dot_nt(dmb[...], wfc2[cols, :])
        low = (gp[:, cols].astype(F32) * back).astype(BF)
        du[:, cols] = low
        sums = jnp.sum(low.astype(F32), 0, keepdims=True)
        for i in range(width // 256):
            dcf[pl.ds(t * (width // 256) + i, 1), :] = sums[:, i * 256 : (i + 1) * 256]
        pump(3 + t, 4 + t, ("fc2",))
        return carry

    lax.fori_loop(0, ff // width, shrink, 0)

    for j in range(chunks):
        part = pl.ds(j * blk, blk)
        grad_two = dot_nt(du[part, :], wfc1[...])
        hat, rstd = norm_stats(rb[part, :])
        vec[2:3, :] += jnp.sum(grad_two * hat, 0, keepdims=True)
        vec[8:9, :] += jnp.sum(grad_two, 0, keepdims=True)
        middle = cot[part, :].astype(F32) + norm_back(grad_two, hat, rstd, gains[0, 2:3, :])
        drb[part, :] = middle
        vec[1:2, :] += jnp.sum(middle * zb[part, :].astype(F32), 0, keepdims=True)
        low = (gains[0, 1:2, :] * middle).astype(BF)
        dzb[part, :] = low
        vec[7:8, :] += jnp.sum(low.astype(F32), 0, keepdims=True)

        grad_o = dot_nt(low, wproj[...]).astype(BF).astype(F32)
        for i in range(pairs):
            cols = slice(i * 128, (i + 1) * 128)
            pair = grad_o[:, cols]
            both = pair * ob[part, cols].astype(F32)
            inner_a = jnp.sum(jnp.where(lane_row < 64, both, 0.0), -1, keepdims=True)
            inner_b = jnp.sum(jnp.where(lane_row < 64, 0.0, both), -1, keepdims=True)
            extra_a = three_parts(-inner_a, lane_row, 68)
            extra_b = three_parts(-inner_b, lane_row, 4)
            doaug[2 * i, part, :] = jnp.where(lane_row < 64, pair, extra_a).astype(BF)
            doaug[2 * i + 1, part, :] = jnp.where(lane_row < 64, extra_b, pair).astype(BF)
        pump(7 + 2 * j, 9 + 2 * j, ("fc2",))

    def dkv_copy(index):
        return pltpu.make_async_remote_copy(
            src_ref=dkv_send.at[index],
            dst_ref=dkv_recv.at[index],
            send_sem=dkv_ssem.at[index],
            recv_sem=dkv_rsem.at[index],
            device_id=sib,
            device_id_type=MESH,
        )

    def attend_back(pair, carry):
        sides = aug_pair(pair)
        grads = {}
        for i, (keys, values) in enumerate(sides):
            query = qaug[2 * pair + i]
            outer = doaug[2 * pair + i]
            for half in (1, 0):
                span = slice(half * rows, (half + 1) * rows)
                prob = jnp.exp(dot_nt(keys[span], query))
                diff = dot_nt(values[span], outer)
                slope = (prob * diff).astype(BF)
                grads["v", i, half] = dot_nn(prob.astype(BF), outer)
                grads["k", i, half] = dot_nn(slope, query)
                grads["q", i, half] = dot_tn(slope, keys[span])
        cols = aligned(pair * 128, 128)

        def merged(name, half):
            return jnp.where(lane_row < 64, grads[name, 0, half], grads[name, 1, half])

        dkv_send[pair] = merged("k", 1).astype(BF)
        dkv_send[pairs + pair] = merged("v", 1).astype(BF)
        dkv_copy(pair).start()
        dkv_copy(pairs + pair).start()
        dqkv[:, cols] = ((merged("q", 0) + merged("q", 1)) * 0.125).astype(BF)
        dqkv[:, aligned(width + pair * 128, 128)] = merged("k", 0).astype(BF)
        dqkv[:, aligned(2 * width + pair * 128, 128)] = merged("v", 0).astype(BF)
        pump(11 + 2 * pair, 13 + 2 * pair, ("fc2", "fc1"))
        return carry

    lax.fori_loop(0, pairs, attend_back, 0)

    def collect(index, carry):
        dkv_copy(index).wait()
        cols = aligned(width + index * 128, 128)
        dqkv[:, cols] = (dqkv[:, cols].astype(F32) + dkv_recv[index].astype(F32)).astype(BF)
        return carry

    lax.fori_loop(0, 2 * pairs, collect, 0)

    for j in range(chunks):
        part = pl.ds(j * blk, blk)
        vec[5:6, :] += jnp.sum(dqkv[part, 0:width].astype(F32), 0, keepdims=True)
        vec[6:7, :] += jnp.sum(dqkv[part, 2 * width : 3 * width].astype(F32), 0, keepdims=True)
        grad_one = dot_nt(dqkv[part, :], wqkv[...])
        hat, rstd = norm_stats(hin[part, :].astype(F32))
        vec[0:1, :] += jnp.sum(grad_one * hat, 0, keepdims=True)
        vec[4:5, :] += jnp.sum(grad_one, 0, keepdims=True)
        total = drb[part, :] + norm_back(grad_one, hat, rstd, gains[0, 0:1, :])
        dout[part, :] = total.astype(BF)

        @pl.when(is_second)
        def _():
            x_send(cot, dout, j, xb_ssem, xb_rsem).start()

    steps = slots + d_z + (groups - 1) * HOP
    lax.fori_loop(jnp.where(is_first, early, 0), steps, step, 0)

    for t in range(slots - 4, slots):
        out_copies(t, lambda copy: copy.wait())
    for t in range(slots - RING, slots):
        core_copy(t).wait_send()
        y_copy(t).wait_send()

        @pl.when(has_right)
        def _():
            z_copy(0, t).wait_send()

        @pl.when(has_left)
        def _():
            z_copy(1, t).wait_send()

    @pl.when(has_right)
    def _():
        v_send(0, zright).wait_send()

    @pl.when(has_left)
    def _():
        v_send(1, zleft).wait_send()

    total = vsend[2]
    vec_out[...] = total

    @pl.when(has_left)
    def _():
        vec_out[...] = vec_out[...] + vrecv[2]

    @pl.when(has_right)
    def _():
        vec_out[...] = vec_out[...] + vrecv[3]

    for j in range(chunks):
        @pl.when(is_first)
        def _():
            x_send(hin, fout, j, x_ssem, x_rsem).wait_send()

        @pl.when(is_second)
        def _():
            x_send(cot, dout, j, xb_ssem, xb_rsem).wait_send()

    result_copies(lambda copy: copy.wait())

HEADS = 12
HDIM = 64


def from_behind(block, axis, distance):
    devices = range(lax.axis_size(axis))
    route = [(i - distance, i) for i in devices if i - distance in devices]
    return lax.ppermute(block, axis, route)


def normalize(values, scale_vec, shift_vec):
    row_mean = jnp.mean(values, -1, keepdims=True)
    centered = values - row_mean
    variance = jnp.mean(centered * centered, -1, keepdims=True)
    return centered * lax.rsqrt(variance + 1e-06) * scale_vec + shift_vec


def gelu_exact(values):
    return jax.nn.gelu(values, approximate=False)


def back_dot(left, weight):
    return lax.dot_general(
        left, weight, (((1,), (1,)), ((), ())), preferred_element_type=jnp.float32
    )


def row_contract(left, right):
    return lax.dot_general(
        left, right, (((0,), (0,)), ((), ())), preferred_element_type=jnp.float32
    )


def masked_scores(query, keys_all, seg_row):
    row_count = query.shape[0]
    length = keys_all.shape[0]
    start = lax.axis_index("narrow") * row_count
    own_seg = lax.dynamic_slice_in_dim(seg_row, start, row_count)
    same = own_seg[:, None] == seg_row[None, :]
    raw = (
        jnp.einsum(
            "qhd,khd->hqk",
            query.reshape(row_count, HEADS, HDIM),
            keys_all.reshape(length, HEADS, HDIM),
            preferred_element_type=jnp.float32,
        )
        * 0.125
    )
    return jnp.where(same[None], raw, -1e30)


def forward_layer(inputs, seg_row, weights):
    qkv_w, proj_w, fc1_w, fc2_w, gain_rows, bias_rows, fc1_b = weights
    row_count, model_width = inputs.shape
    normed = normalize(inputs, gain_rows[0], bias_rows[0]).astype(jnp.bfloat16)
    qkv = jnp.dot(normed, qkv_w, preferred_element_type=jnp.float32)
    query = (qkv[:, :model_width] + bias_rows[1]).astype(jnp.bfloat16)
    key_rows = qkv[:, model_width : 2 * model_width].astype(jnp.bfloat16)
    value_rows = (qkv[:, 2 * model_width :] + bias_rows[2]).astype(jnp.bfloat16)
    keys_all, values_all = (
        lax.all_gather(key_rows, "narrow", axis=0, tiled=True),
        lax.all_gather(value_rows, "narrow", axis=0, tiled=True),
    )
    length = keys_all.shape[0]
    scores = masked_scores(query, keys_all, seg_row)
    peak = jnp.max(scores, -1, keepdims=True)
    log_total = peak + jnp.log(jnp.sum(jnp.exp(scores - peak), -1, keepdims=True))
    probs = jnp.exp(scores - log_total).astype(jnp.bfloat16)
    mixed = jnp.einsum(
        "hqk,khd->qhd",
        probs,
        values_all.reshape(length, HEADS, HDIM),
        preferred_element_type=jnp.float32,
    )
    attended = mixed.reshape(row_count, model_width).astype(jnp.bfloat16)
    branch = jnp.dot(attended, proj_w, preferred_element_type=jnp.float32) + bias_rows[3]
    middle = inputs + gain_rows[1] * branch
    normed_two = normalize(middle, gain_rows[2], bias_rows[4]).astype(jnp.bfloat16)
    hidden_pre = jnp.dot(normed_two, fc1_w, preferred_element_type=jnp.float32) + fc1_b
    activated = gelu_exact(hidden_pre).astype(jnp.bfloat16)
    mlp_out = jnp.dot(activated, fc2_w, preferred_element_type=jnp.float32) + bias_rows[5]
    output = middle + gain_rows[3] * mlp_out
    saved = (
        inputs,
        query,
        keys_all,
        values_all,
        log_total,
        attended,
        branch,
        middle,
        hidden_pre,
        mlp_out,
    )
    return (output, saved)


def backward_layer(grad_out, saved, seg_row, weights):
    qkv_w, proj_w, fc1_w, fc2_w, gain_rows, bias_rows, fc1_b = weights
    (
        inputs,
        query,
        keys_all,
        values_all,
        log_total,
        attended,
        branch,
        middle,
        hidden_pre,
        mlp_out,
    ) = saved
    row_count, model_width = inputs.shape
    length = keys_all.shape[0]
    scale_two = jnp.sum(grad_out * mlp_out, 0)
    mlp_grad = (gain_rows[3] * grad_out).astype(jnp.bfloat16)
    activated, gelu_pull = jax.vjp(gelu_exact, hidden_pre)
    grad_fc2 = row_contract(activated.astype(jnp.bfloat16), mlp_grad)
    shift_five = jnp.sum(mlp_grad.astype(jnp.float32), 0)
    pre_grad = gelu_pull(back_dot(mlp_grad, fc2_w))[0].astype(jnp.bfloat16)
    normed_two, norm_pull_two = jax.vjp(normalize, middle, gain_rows[2], bias_rows[4])
    grad_fc1 = row_contract(normed_two.astype(jnp.bfloat16), pre_grad)
    grad_fc1b = jnp.sum(pre_grad.astype(jnp.float32), 0)
    middle_part, gain_two, shift_four = norm_pull_two(back_dot(pre_grad, fc1_w))
    middle_grad = grad_out + middle_part
    scale_one = jnp.sum(middle_grad * branch, 0)
    branch_grad = (gain_rows[1] * middle_grad).astype(jnp.bfloat16)
    grad_proj = row_contract(attended, branch_grad)
    shift_three = jnp.sum(branch_grad.astype(jnp.float32), 0)
    heads_grad = back_dot(branch_grad, proj_w).astype(jnp.bfloat16).reshape(row_count, HEADS, HDIM)
    scores = masked_scores(query, keys_all, seg_row)
    probs = jnp.exp(scores - log_total)
    keys_heads = keys_all.reshape(length, HEADS, HDIM)
    prob_grad = jnp.einsum(
        "qhd,khd->hqk",
        heads_grad,
        values_all.reshape(length, HEADS, HDIM),
        preferred_element_type=jnp.float32,
    )
    inner = jnp.sum(probs * prob_grad, -1, keepdims=True)
    score_grad = (probs * (prob_grad - inner)).astype(jnp.bfloat16)
    query_grad = (
        (
            jnp.einsum("hqk,khd->qhd", score_grad, keys_heads, preferred_element_type=jnp.float32)
            * 0.125
        )
        .reshape(row_count, model_width)
        .astype(jnp.bfloat16)
    )
    key_part = (
        jnp.einsum(
            "hqk,qhd->khd",
            score_grad,
            query.reshape(row_count, HEADS, HDIM),
            preferred_element_type=jnp.float32,
        )
        * 0.125
    ).reshape(length, model_width)
    value_part = jnp.einsum(
        "hqk,qhd->khd", probs.astype(jnp.bfloat16), heads_grad, preferred_element_type=jnp.float32
    ).reshape(length, model_width)
    key_sum, value_sum = (
        lax.psum_scatter(
            key_part.astype(jnp.bfloat16), "narrow", scatter_dimension=0, tiled=True
        ).astype(jnp.float32),
        lax.psum_scatter(
            value_part.astype(jnp.bfloat16), "narrow", scatter_dimension=0, tiled=True
        ).astype(jnp.float32),
    )
    key_grad = key_sum.astype(jnp.bfloat16)
    value_grad = value_sum.astype(jnp.bfloat16)
    qkv_grad = jnp.concatenate([query_grad, key_grad, value_grad], 1)
    normed, norm_pull_one = jax.vjp(normalize, inputs, gain_rows[0], bias_rows[0])
    grad_qkv = row_contract(normed.astype(jnp.bfloat16), qkv_grad)
    input_part, gain_one, shift_zero = norm_pull_one(back_dot(qkv_grad, qkv_w))
    input_grad = middle_grad + input_part
    gain_grads = jnp.stack([gain_one, scale_one, gain_two, scale_two])
    shift_grads = jnp.stack(
        [
            shift_zero,
            jnp.sum(query_grad.astype(jnp.float32), 0),
            jnp.sum(value_grad.astype(jnp.float32), 0),
            shift_three,
            shift_four,
            shift_five,
        ]
    )
    return (
        input_grad,
        (grad_qkv, grad_proj, grad_fc1, grad_fc2, gain_grads, shift_grads, grad_fc1b),
    )


def general_body(
    boundary, segments, qkv_weight, proj_weight, fc1_weight, fc2_weight, gains, biases, fc1_bias
):
    weights = (
        qkv_weight[0],
        proj_weight[0],
        fc1_weight[0],
        fc2_weight[0],
        gains[0],
        biases[0],
        fc1_bias[0],
    )
    local_ends = boundary[0]
    micro_count = local_ends.shape[0]
    first_section = lax.axis_index("section") == 0
    arrived = jnp.zeros(local_ends.shape[1:], jnp.bfloat16)
    stored = []
    outputs = []
    for step_index in range(micro_count + 1):
        lower = min(step_index, micro_count - 1)
        upper = max(step_index - 1, 0)
        inputs = jnp.where(
            first_section, local_ends[lower].astype(jnp.float32), arrived.astype(jnp.float32)
        )
        seg_row = jnp.where(first_section, segments[lower], segments[upper])
        output, saved = forward_layer(inputs, seg_row, weights)
        stored.append((saved, seg_row))
        outputs.append(output)
        if step_index < micro_count:
            arrived = from_behind(output.astype(jnp.bfloat16), "section", 1)
    totals = tuple((jnp.zeros(w.shape, jnp.float32) for w in weights))
    returned = jnp.zeros(local_ends.shape[1:], jnp.bfloat16)
    input_grads = []
    for step_index in range(micro_count + 1):
        lower = min(step_index, micro_count - 1)
        upper = max(step_index - 1, 0)
        picked = jax.tree.map(
            lambda early, later: jnp.where(first_section, early, later),
            stored[upper],
            stored[lower + 1],
        )
        cotangent = jnp.where(
            first_section, returned.astype(jnp.float32), local_ends[lower].astype(jnp.float32)
        )
        is_valid = jnp.where(first_section, step_index >= 1, step_index < micro_count)
        cotangent = jnp.where(is_valid, cotangent, 0.0)
        grad_in, pieces = backward_layer(cotangent, picked[0], picked[1], weights)
        totals = tuple((acc + part for acc, part in zip(totals, pieces)))
        input_grads.append(grad_in)
        if step_index < micro_count:
            returned = from_behind(grad_in.astype(jnp.bfloat16), "section", -1)
    results = jnp.stack(
        [jnp.where(first_section, input_grads[j + 1], outputs[j + 1]) for j in range(micro_count)]
    )
    results = results.astype(jnp.bfloat16)
    within = (
        lax.psum_scatter(
            totals[0].astype(jnp.bfloat16), "narrow", scatter_dimension=0, tiled=True
        ).astype(jnp.float32),
        lax.psum_scatter(
            totals[1].astype(jnp.bfloat16), "narrow", scatter_dimension=0, tiled=True
        ).astype(jnp.float32),
        lax.psum_scatter(
            totals[2].astype(jnp.bfloat16), "narrow", scatter_dimension=0, tiled=True
        ).astype(jnp.float32),
        lax.psum_scatter(
            totals[3].astype(jnp.bfloat16), "narrow", scatter_dimension=0, tiled=True
        ).astype(jnp.float32),
        lax.psum_scatter(
            totals[4].astype(jnp.bfloat16), "narrow", scatter_dimension=1, tiled=True
        ).astype(jnp.float32),
        lax.psum_scatter(
            totals[5].astype(jnp.bfloat16), "narrow", scatter_dimension=1, tiled=True
        ).astype(jnp.float32),
        lax.psum_scatter(
            totals[6].astype(jnp.bfloat16), "narrow", scatter_dimension=0, tiled=True
        ).astype(jnp.float32),
    )
    final = (
        lax.psum(within[0].astype(jnp.bfloat16), "group").astype(jnp.float32),
        lax.psum(within[1].astype(jnp.bfloat16), "group").astype(jnp.float32),
        lax.psum(within[2].astype(jnp.bfloat16), "group").astype(jnp.float32),
        lax.psum(within[3].astype(jnp.bfloat16), "group").astype(jnp.float32),
        lax.psum(within[4].astype(jnp.bfloat16), "group").astype(jnp.float32),
        lax.psum(within[5].astype(jnp.bfloat16), "group").astype(jnp.float32),
        lax.psum(within[6].astype(jnp.bfloat16), "group").astype(jnp.float32),
    )
    return (
        results[None],
        final[0][None],
        final[1][None],
        final[2][None],
        final[3][None],
        final[4][None],
        final[5][None],
        final[6][None],
    )


def fused_body(
    groups, boundary, segments, qkv_weight, proj_weight, fc1_weight, fc2_weight, gains, biases, fc1_bias
):
    blk, width = boundary.shape[2:]
    rows, keys = 2 * blk, 4 * blk
    ff = fc1_weight.shape[2]
    heads = width // HDIM
    nar = lax.axis_index(NARROW)

    def bf(*shape):
        return pltpu.VMEM(shape, BF)

    def f32(*shape):
        return pltpu.VMEM(shape, F32)

    dma = pltpu.SemaphoreType.DMA
    slot = (SLOT_ROWS, SLOT_COLS)
    scratch = [
        bf(width, 3 * width), bf(width, width), bf(width, ff), bf(ff, width),
        bf(rows, width), bf(rows, width), bf(rows, width), bf(heads, rows, 128),
        bf(keys, width), bf(keys, width), bf(rows, width), bf(rows, width),
        f32(rows, width), bf(rows, width), bf(rows, ff), bf(rows, ff), bf(rows, width), bf(rows, width),
        bf(rows, width), bf(rows, width), bf(heads, rows, 128),
        bf(rows, 3 * width), bf(heads, rows, 128), bf(heads, rows, 128), bf(rows, width),
        bf(keys, 128), f32(RING, 2, *slot), bf(RING, 2, *slot), bf(RING, 2, *slot),
        bf(RING, *slot), bf(RING, *slot), f32(OWN_RING, *slot), bf(2, RING, *slot), bf(2, ZRING, *slot), bf(4, *slot),
        f32(16, width), f32(16, 256), f32(5, 16, width + 256), f32(4, 16, width + 256),
        dma((4,)), dma(()), dma((2,)), dma((2, 2)), dma((2, 2)), dma((2,)), dma((2,)), dma((2,)), dma((2,)),
        dma((heads,)), dma((heads,)), dma((3,)),
        dma((RING,)), dma((RING,)), dma((RING,)), dma((RING,)), dma((2, RING)), dma((2, ZRING)), dma((4, 2)),
        dma((4,)), dma((4,)), pltpu.SemaphoreType.REGULAR((4,)),
    ]
    hbm = pl.BlockSpec(memory_space=pl.ANY)
    vmem = pl.BlockSpec(memory_space=pltpu.VMEM)
    out = pl.pallas_call(
        functools.partial(kernel, groups),
        out_shape=(
            jax.ShapeDtypeStruct((2, blk, width), BF),
            jax.ShapeDtypeStruct((width // 4, 3 * width), BF),
            jax.ShapeDtypeStruct((width // 4, width), BF),
            jax.ShapeDtypeStruct((width // 4, ff), BF),
            jax.ShapeDtypeStruct((ff // 4, width), BF),
            jax.ShapeDtypeStruct((16, width + 256), F32),
        ),
        in_specs=[hbm, vmem, hbm, hbm, hbm, hbm, vmem, vmem, vmem],
        out_specs=(hbm, hbm, hbm, hbm, hbm, vmem),
        scratch_shapes=scratch,
        compiler_params=pltpu.CompilerParams(
            collective_id=0, has_side_effects=True, vmem_limit_bytes=63 * 2**20
        ),
        name="two_layers",
    )(boundary, segments, qkv_weight, proj_weight, fc1_weight, fc2_weight, gains, biases.reshape(1, -1), fc1_bias)
    results, qkv, proj, fc1, fc2, vecs = out
    share = lax.dynamic_slice_in_dim(vecs[:, :width], nar * (width // 4), width // 4, 1)
    fc1_share = lax.dynamic_slice_in_dim(vecs[: ff // 256, width:].reshape(-1), nar * (ff // 4), ff // 4, 0)
    return (
        results[None],
        qkv.astype(F32)[None],
        proj.astype(F32)[None],
        fc1.astype(F32)[None],
        fc2.astype(F32)[None],
        share[:4][None],
        share[4:10][None],
        fc1_share[None],
    )


def solution(mesh):
    sections, groups, narrow = (mesh.shape[name] for name in (SECTION, GROUP, NARROW))
    placed = (
        P("section", "group", "narrow", None),
        P("group", None),
        P("section", None, None),
        P("section", None, None),
        P("section", None, None),
        P("section", None, None),
        P("section", None, None),
        P("section", None, None),
        P("section", None),
    )
    fused = sections == 2 and narrow == 4 and groups > 1
    body = functools.partial(fused_body, groups) if fused else general_body
    return jax.shard_map(
        body,
        mesh=mesh,
        in_specs=placed,
        out_specs=(
            P("section", "group", "narrow", None),
            P("section", "narrow", None),
            P("section", "narrow", None),
            P("section", "narrow", None),
            P("section", "narrow", None),
            P("section", None, "narrow"),
            P("section", None, "narrow"),
            P("section", "narrow"),
        ),
        check_vma=False,
    )
```

```python
import functools

import jax
import jax.numpy as jnp
from jax import lax
from jax.experimental import pallas as pl
from jax.experimental.pallas import tpu as pltpu
from jax.sharding import PartitionSpec as P

SECTION, GROUP, NARROW = "section", "group", "narrow"
HALVES = 2
BIG = 1e30
SLOT_ROWS = 192
SLOT_COLS = 256
RING = 6
ZRING = 8
YRING = 6
OWN_RING = 12
LENT = 5
LEND_EVERY = 5
BF = jnp.bfloat16
F32 = jnp.float32
MESH = pl.DeviceIdType.MESH


def dot_nn(left, right):
    return lax.dot_general(left, right, (((1,), (0,)), ((), ())), preferred_element_type=F32)


def dot_nt(left, right):
    return lax.dot_general(left, right, (((1,), (1,)), ((), ())), preferred_element_type=F32)


def dot_tn(left, right):
    return lax.dot_general(left, right, (((0,), (0,)), ((), ())), preferred_element_type=F32)


def aligned(start, size, unit=128):
    return pl.ds(pl.multiple_of(start, unit), size)


def norm_stats(values):
    mean = jnp.mean(values, -1, keepdims=True)
    centered = values - mean
    var = jnp.mean(centered * centered, -1, keepdims=True)
    rstd = lax.rsqrt(var + 1e-06)
    return centered * rstd, rstd


def norm_back(grad, hat, rstd, gain):
    scaled = grad * gain
    mean_one = jnp.mean(scaled, -1, keepdims=True)
    mean_two = jnp.mean(scaled * hat, -1, keepdims=True)
    return rstd * (scaled - mean_one - hat * mean_two)


def three_parts(column, lane, base):
    high = column.astype(BF).astype(F32)
    rest = column - high
    mid = rest.astype(BF).astype(F32)
    low = rest - mid
    return jnp.where(
        lane == base, high, jnp.where(lane == base + 1, mid, jnp.where(lane == base + 2, low, 0.0))
    )


def kernel(groups, *refs):
    (
        boundary, segments, wqkv_h, wproj_h, wfc1_h, wfc2_h, gains, biases, fc1b,
        results, g_qkv, g_proj, g_fc1, g_fc2, vec_out,
        wqkv, wproj, wfc1, wfc2,
        hin, cot, lhs, qaug, kall, vall, zb, rb, rhs, act, mb, fout,
        dmb, doaug, dkv_send, dkv_recv,
        segf, ckeep, csend, crecv, ysend, yrecv, rown, zsend, zrecv, ostage,
        vec, dcf, vsend, vrecv, lent,
        w_sem, b_sem, bx_sem, kv_ssem, kv_rsem, x_ssem, x_rsem, xb_ssem, xb_rsem,
        dkv_ssem, dkv_rsem, res_sem,
        c_ssem, c_rsem, y_ssem, y_rsem, z_ssem, z_rsem, o_sem,
        v_ssem, v_rsem, l_ssem, l_rsem, credit,
    ) = refs
    sec = lax.axis_index(SECTION)
    grp = lax.axis_index(GROUP)
    nar = lax.axis_index(NARROW)
    yy = nar // 2
    cc = nar % 2
    sib = (sec, grp, nar + 1 - 2 * cc)
    ynb = (sec, grp, (nar + 2) % 4)
    xnb = (1 - sec, grp, nar)
    zright = (sec, grp + 1, nar)
    zleft = (sec, grp - 1, nar)
    has_right = grp < groups - 1
    has_left = grp > 0
    is_first = sec == 0
    is_second = sec == 1

    blk = boundary.shape[2]
    rows = 2 * blk
    width = boundary.shape[3]
    ff = wfc1.shape[1]
    pairs = width // 128
    chunks = rows // blk

    n2, ob, n1 = lhs.at[0], lhs.at[1], lhs.at[2]
    gp = du = rhs.at[:, 0:ff]
    dzb, dqkv = rhs.at[:, ff : ff + width], rhs.at[:, ff + width :]
    drb, dout = rb, fout

    def bias(row):
        return biases[0:1, row * width : (row + 1) * width]

    weight_copies = [
        pltpu.make_async_copy(src.at[0], dst, w_sem.at[i])
        for i, (src, dst) in enumerate(
            ((wqkv_h, wqkv), (wproj_h, wproj), (wfc1_h, wfc1), (wfc2_h, wfc2))
        )
    ]
    for copy in weight_copies:
        copy.start()

    def own_block(dst):
        return pltpu.make_async_copy(boundary.at[0, yy], dst.at[aligned(yy * blk, blk)], b_sem)

    def swap_block(dst):
        return pltpu.make_async_remote_copy(
            src_ref=boundary.at[0, 1 - yy],
            dst_ref=dst.at[aligned(yy * blk, blk)],
            send_sem=bx_sem.at[0],
            recv_sem=bx_sem.at[1],
            device_id=ynb,
            device_id_type=MESH,
        )

    @pl.when(is_first)
    def _():
        own_block(hin).start()

    @pl.when(is_second)
    def _():
        own_block(cot).start()

    barrier = pltpu.get_barrier_semaphore()
    for peer in (sib, ynb, xnb):
        pl.semaphore_signal(barrier, inc=1, device_id=peer, device_id_type=MESH)

    @pl.when(has_right)
    def _():
        pl.semaphore_signal(barrier, inc=1, device_id=zright, device_id_type=MESH)

    @pl.when(has_left)
    def _():
        pl.semaphore_signal(barrier, inc=1, device_id=zleft, device_id_type=MESH)

    pl.semaphore_wait(barrier, 3 + has_right.astype(jnp.int32) + has_left.astype(jnp.int32))

    @pl.when(is_first)
    def _():
        swap_block(hin).start()

    @pl.when(is_second)
    def _():
        swap_block(cot).start()

    keys_seg = jnp.concatenate(
        [
            segments[pl.ds(yy, 1), aligned((half * 2 + core) * blk, blk)]
            for core in (cc, 1 - cc)
            for half in range(2)
        ],
        1,
    )
    feature = lax.rem(lax.broadcasted_iota(jnp.int32, (128, 1), 0), 64)
    hot = jnp.where(keys_seg == feature, 1.0, 0.0)
    ones = jnp.where((feature >= 4) & (feature < 7), 1.0, 0.0)
    segf[...] = jnp.where(feature < 4, hot, ones).T.astype(BF)
    vec[...] = jnp.zeros_like(vec)
    dcf[...] = jnp.zeros_like(dcf)

    lane_row = lax.broadcasted_iota(jnp.int32, (1, 128), 1)
    first_row = jnp.where(lane_row < 64, 1.0, 0.0).astype(BF)
    second_row = jnp.where(lane_row < 64, 0.0, 1.0).astype(BF)
    half_lane = lax.rem(lane_row, 64)
    penalty_row = jnp.where(half_lane < 4, BIG, 0.0)

    def x_send(dst, src, j, ssem, rsem):
        part = aligned(j * blk, blk)
        return pltpu.make_async_remote_copy(
            src_ref=src.at[part],
            dst_ref=dst.at[part],
            send_sem=ssem.at[j],
            recv_sem=rsem.at[j],
            device_id=xnb,
            device_id_type=MESH,
        )

    def kv_copy(which, j):
        ref = (kall, vall)[which]
        start = pl.multiple_of(j * blk, blk)
        return pltpu.make_async_remote_copy(
            src_ref=ref.at[pl.ds(start, blk)],
            dst_ref=ref.at[pl.ds(start + rows, blk)],
            send_sem=kv_ssem.at[which, j],
            recv_sem=kv_rsem.at[which, j],
            device_id=sib,
            device_id_type=MESH,
        )

    def project(j, carry):
        @pl.when(is_first & (j == 0))
        def _():
            own_block(hin).wait()

        @pl.when(is_first & (j > 0))
        def _():
            swap_block(hin).wait()

        @pl.when(is_second)
        def _():
            x_send(hin, fout, j, x_ssem, x_rsem).wait_recv()

        block = jnp.where(is_first, (yy + j) % 2, j)
        part = aligned(block * blk, blk)
        hat, _ = norm_stats(hin[part, :].astype(F32))
        normed = (hat * gains[0, 0:1, :] + bias(0)).astype(BF)
        n1[part, :] = normed

        @pl.when(j == 0)
        def _():
            weight_copies[0].wait()

        kall[part, :] = dot_nn(normed, wqkv[:, width : 2 * width]).astype(BF)
        kv_copy(0, block).start()
        vall[part, :] = (dot_nn(normed, wqkv[:, 2 * width :]) + bias(2)).astype(BF)
        kv_copy(1, block).start()
        low = ((dot_nn(normed, wqkv[:, 0:width]) + bias(1)).astype(BF) * 0.125).astype(F32)
        penalty = (segf[part, :].astype(F32) - 1.0) * penalty_row
        for i in range(pairs):
            pair = low[:, i * 128 : (i + 1) * 128]
            qaug[2 * i, part, :] = jnp.where(lane_row < 64, pair, penalty).astype(BF)
            qaug[2 * i + 1, part, :] = jnp.where(lane_row < 64, penalty, pair).astype(BF)
        return carry

    lax.fori_loop(0, chunks, project, 0)
    for j in range(chunks):
        kv_copy(0, j).wait()
        kv_copy(1, j).wait()

    def aug_pair(pair):
        cols = aligned(pair * 128, 128)
        keys, values, feats = kall[:, cols], vall[:, cols], segf[...]
        feat_a, feat_b = feats * second_row, feats * first_row
        return (
            (keys * first_row + feat_a, values * first_row + feat_a),
            (keys * second_row + feat_b, values * second_row + feat_b),
        )

    def feed_forward(part):
        branch = dot_nn(ob[part, :], wproj[...]) + bias(3)
        zb[part, :] = branch.astype(BF)
        middle = hin[part, :].astype(F32) + gains[0, 1:2, :] * branch
        rb[part, :] = middle
        hat, _ = norm_stats(middle)
        n2[part, :] = (hat * gains[0, 2:3, :] + bias(4)).astype(BF)

        def expand(t, carry):
            cols = aligned(t * width, width)
            pre = dot_nn(n2[part, :], wfc1[:, cols]) + fc1b[0:1, cols]
            phi = 0.5 + 0.5 * lax.erf(pre * 0.7071067811865476)
            act[part, cols] = (pre * phi).astype(BF)
            slope = phi + pre * (jnp.exp(-0.5 * pre * pre) * 0.3989422804014327)
            gp[part, cols] = slope.astype(BF)
            return carry

        lax.fori_loop(0, ff // width, expand, 0)
        mlp = dot_nn(act[part, :], wfc2[...]) + bias(5)
        mb[part, :] = mlp.astype(BF)
        fout[part, :] = (rb[part, :] + gains[0, 3:4, :] * mlp).astype(BF)

    def forward_block(j, carry):
        part = aligned(j * blk, blk)

        feats = segf[...]
        own_pen = ((segf[part, :].astype(F32) - 1.0) * penalty_row).astype(BF) * first_row

        def attend(trio, carry):
            items = [trio * 3 + i for i in range(3)]
            spans = [aligned(pair * 128, 128) for pair in items]
            scores = []
            for pair, cols in zip(items, spans):
                query = jnp.concatenate(
                    [
                        jnp.concatenate([qaug[2 * pair, part, :] * first_row, own_pen], 1),
                        jnp.concatenate([qaug[2 * pair + 1, part, :] * second_row, own_pen], 1),
                    ],
                    0,
                )
                scores.append(dot_nt(query, jnp.concatenate([kall[:, cols], feats], 1)))
            for pair, cols, score in zip(items, spans, scores):
                peak = jnp.max(score, -1, keepdims=True)
                expo = jnp.exp(score - peak).astype(BF)
                mixed = dot_nn(expo, jnp.concatenate([vall[:, cols], feats], 1))
                total = mixed[:, 132:133]
                outs = mixed[:, 0:128] / total
                log_total = peak + jnp.log(total)
                for i in range(2):
                    base = 64 * (1 - i)
                    extra = three_parts(-log_total[i * blk : (i + 1) * blk], lane_row, base + 4)
                    query = qaug[2 * pair + i, part, :]
                    qaug[2 * pair + i, part, :] = (query.astype(F32) + extra).astype(BF)
                ob[part, cols] = jnp.where(lane_row < 64, outs[:blk], outs[blk:]).astype(BF)
            return carry

        lax.fori_loop(0, pairs // 3, attend, 0)

        @pl.when(j == 0)
        def _():
            for copy in weight_copies[1:]:
                copy.wait()

        feed_forward(part)

        @pl.when(is_first)
        def _():
            x_send(hin, fout, j, x_ssem, x_rsem).start()

        return carry

    lax.fori_loop(0, chunks, forward_block, 0)

    n_fc2 = 2 * (width // 128)
    n_fc1 = ff // SLOT_COLS
    n_proj = width // SLOT_COLS
    n_qkv = 3 * width // SLOT_COLS
    lo_fc1 = n_fc2
    lo_proj = lo_fc1 + n_fc1
    lo_qkv = lo_proj + n_proj
    slots = lo_qkv + n_qkv
    mine = jnp.where(is_first, slots - LENT, slots + LENT)
    vslot = slots - LENT - 4

    def slot_at(m):
        return jnp.where(is_first, m + jnp.minimum(m // (LEND_EVERY - 1), LENT), m)

    def place_of(p):
        return jnp.where(is_first, p - jnp.minimum(p // LEND_EVERY, LENT), p)

    def is_lent(p):
        return is_first & (p % LEND_EVERY == LEND_EVERY - 1) & (p < LENT * LEND_EVERY)

    def core_copy(t):
        at = t % RING
        return pltpu.make_async_remote_copy(
            src_ref=csend.at[at], dst_ref=crecv.at[at],
            send_sem=c_ssem.at[at], recv_sem=c_rsem.at[at],
            device_id=sib, device_id_type=MESH,
        )

    def y_copy(t):
        at = t % YRING
        return pltpu.make_async_remote_copy(
            src_ref=ysend.at[at], dst_ref=yrecv.at[at],
            send_sem=y_ssem.at[at], recv_sem=y_rsem.at[at],
            device_id=ynb, device_id_type=MESH,
        )

    def z_copy(way, t):
        return pltpu.make_async_remote_copy(
            src_ref=zsend.at[way, t % RING], dst_ref=zrecv.at[way, t % ZRING],
            send_sem=z_ssem.at[way, t % RING], recv_sem=z_rsem.at[way, t % ZRING],
            device_id=(zright, zleft)[way], device_id_type=MESH,
        )

    def v_copy(stage, peer):
        return pltpu.make_async_remote_copy(
            src_ref=vsend.at[stage], dst_ref=vrecv.at[stage],
            send_sem=v_ssem.at[stage], recv_sem=v_rsem.at[stage],
            device_id=peer, device_id_type=MESH,
        )

    def lend_copy(e):
        return pltpu.make_async_remote_copy(
            src_ref=lent.at[e], dst_ref=lent.at[e],
            send_sem=l_ssem.at[e], recv_sem=l_rsem.at[e],
            device_id=xnb, device_id_type=MESH,
        )

    def give(which, t, depth, peer, count=None):
        @pl.when(t + depth < (mine if count is None else count))
        def _():
            pl.semaphore_signal(credit.at[which], inc=1, device_id=peer, device_id_type=MESH)

    def take(which, t, depth):
        @pl.when(t >= depth)
        def _():
            pl.semaphore_wait(credit.at[which], 1)

    def out_parts(p, src, act):
        @pl.when(p < lo_fc1)
        def _():
            row = (p // (width // 128)) * (2 * SLOT_ROWS)
            cols = aligned((p % (width // 128)) * 128, 128)
            for i in range(2):
                rows_of = pl.ds(pl.multiple_of(row + i * SLOT_ROWS, SLOT_ROWS), SLOT_ROWS)
                act(src.at[:, i * 128 : (i + 1) * 128], g_fc2.at[rows_of, cols], i)

        for lo, count, ref in ((lo_fc1, n_fc1, g_fc1), (lo_proj, n_proj, g_proj), (lo_qkv, n_qkv, g_qkv)):
            @pl.when((p >= lo) & (p < lo + count))
            def _():
                act(src, ref.at[:, aligned((p - lo) * SLOT_COLS, SLOT_COLS)], 0)

    def own_out(m, method):
        def act(src, dst, i):
            getattr(pltpu.make_async_copy(src, dst, o_sem.at[m % 4, i]), method)()

        out_parts(slot_at(m), ostage.at[m % 4], act)

    def lent_out(e, method):
        def act(src, dst, i):
            copy = pltpu.make_async_remote_copy(
                src_ref=src, dst_ref=dst,
                send_sem=l_ssem.at[LENT + 2 * e + i], recv_sem=l_rsem.at[LENT + 2 * e + i],
                device_id=xnb, device_id_type=MESH,
            )
            getattr(copy, method)()

        out_parts(e * LEND_EVERY + LEND_EVERY - 1, ostage.at[(slots + e) % 4], act)

    def out_start(m):
        @pl.when(m < slots)
        def _():
            own_out(m, "start")

        @pl.when(m >= slots)
        def _():
            lent_out(m - slots, "start")

    def out_wait(m):
        @pl.when(m < slots)
        def _():
            own_out(m, "wait")

        @pl.when(m >= slots)
        def _():
            lent_out(m - slots, "wait_send")

    def result_stay():
        return pltpu.make_async_copy(fout.at[aligned(yy * blk, blk)], results.at[yy], res_sem.at[0])

    def result_move():
        return pltpu.make_async_remote_copy(
            src_ref=fout.at[aligned((1 - yy) * blk, blk)], dst_ref=results.at[yy],
            send_sem=res_sem.at[1], recv_sem=res_sem.at[2],
            device_id=ynb, device_id_type=MESH,
        )

    def own_terms(q):
        @pl.when(q * 3 >= RING)
        def _():
            for i in range(3):
                core_copy(q * 3 + i - RING).wait_send()

        ring = (q % 2) * 3

        @pl.when(q < lo_fc1 // 3)
        def _():
            row = (q // 2) * (2 * SLOT_ROWS)
            cols = aligned((q % 2) * 384, 384)

            def share(dest, carry):
                got = dot_tn(act[:, aligned(dest * width + row, 2 * SLOT_ROWS)], dmb[:, cols])

                def place(ref, kind):
                    for i in range(3):
                        for half in range(2):
                            ref[ring + i, dest // 2, :, half * 128 : half * 128 + 128] = got[
                                half * SLOT_ROWS : (half + 1) * SLOT_ROWS, i * 128 : (i + 1) * 128
                            ].astype(kind)

                @pl.when(cc == dest % 2)
                def _():
                    place(ckeep, F32)

                @pl.when(cc != dest % 2)
                def _():
                    place(csend, BF)

                return carry

            lax.fori_loop(0, 4, share, 0)

        @pl.when(q >= lo_fc1 // 3)
        def _():
            cols = aligned((q * 3 - lo_fc1) * SLOT_COLS, 3 * SLOT_COLS)
            left = jnp.where(q * 3 < lo_proj, 0, jnp.where(q * 3 < lo_qkv, 1, 2))

            def share(side, carry):
                got = dot_tn(lhs[left, :, aligned(side * 2 * SLOT_ROWS, 2 * SLOT_ROWS)], rhs[:, cols])
                for core in range(2):
                    @pl.when(cc == core)
                    def _():
                        for i in range(3):
                            span = slice(i * SLOT_COLS, (i + 1) * SLOT_COLS)
                            mine, theirs = slice(0, SLOT_ROWS), slice(SLOT_ROWS, 2 * SLOT_ROWS)
                            if core:
                                mine, theirs = theirs, mine
                            ckeep[ring + i, side] = got[mine, span]
                            csend[ring + i, side] = got[theirs, span].astype(BF)

                return carry

            lax.fori_loop(0, 2, share, 0)

    def stage_own(t, carry):
        @pl.when(t % 3 == 0)
        def _():
            own_terms(t // 3)

        take(0, t, RING)
        core_copy(t).start()

        @pl.when(t == slot_at(vslot))
        def _():
            vsend[0, :, 0:width] = vec[...]
            vsend[0, :, width : width + 256] = dcf[...]
            v_copy(0, sib).start()

        return carry

    def stage_chip(p, carry):
        at = p % RING
        away = 1 - yy
        t = place_of(p)
        keeps = jnp.logical_not(is_lent(p))

        @pl.when(p < slots)
        def _():
            core_copy(p).wait_recv()

        @pl.when(keeps)
        def _():
            take(1, t, YRING)

            @pl.when(t >= YRING)
            def _():
                y_copy(t - YRING).wait_send()

            @pl.when(p < slots)
            def _():
                ysend[t % YRING] = (ckeep[at, away] + crecv[at, away].astype(F32)).astype(BF)
                rown[t % OWN_RING] = (ckeep[at, yy] + crecv[at, yy].astype(F32)).astype(BF)

            @pl.when(p >= slots)
            def _():
                lend_copy(p - slots).wait_recv()
                ysend[t % YRING] = lent[p - slots, away]
                rown[t % OWN_RING] = lent[p - slots, yy]

            y_copy(t).start()

            @pl.when(t == vslot)
            def _():
                v_copy(0, sib).wait()
                vsend[1] = vsend[0] + vrecv[0]
                v_copy(1, ynb).start()

        @pl.when(is_lent(p))
        def _():
            e = p // LEND_EVERY
            for side in range(2):
                lent[e, side] = (ckeep[at, side] + crecv[at, side].astype(F32)).astype(BF)
            lend_copy(e).start()

        @pl.when(p < slots)
        def _():
            give(0, p, RING, sib, slots)

        return carry

    def stage_group(t, carry):
        y_copy(t).wait_recv()
        at = t % OWN_RING
        rown[at] = (rown[at].astype(F32) + yrecv[t % YRING].astype(F32)).astype(BF)
        give(1, t, YRING, ynb)

        @pl.when(t == vslot)
        def _():
            v_copy(1, ynb).wait()
            vsend[2] = vsend[1] + vrecv[1]

        return carry

    def stage_line(way, t, carry):
        has_before = (has_left, has_right)[way]
        has_after = (has_right, has_left)[way]
        behind = (zleft, zright)[way]
        ahead = (zright, zleft)[way]

        @pl.when(has_before)
        def _():
            z_copy(way, t).wait_recv()

        @pl.when(has_after)
        def _():
            take(2 + way, t, ZRING)

            @pl.when(t >= RING)
            def _():
                z_copy(way, t - RING).wait_send()

            @pl.when(has_before)
            def _():
                zsend[way, t % RING] = (
                    rown[t % OWN_RING].astype(F32) + zrecv[way, t % ZRING].astype(F32)
                ).astype(BF)

            @pl.when(jnp.logical_not(has_before))
            def _():
                zsend[way, t % RING] = rown[t % OWN_RING]

            z_copy(way, t).start()

        @pl.when(t == vslot)
        def _():
            @pl.when(has_before)
            def _():
                v_copy(2 + way, behind).wait_recv()

            @pl.when(has_after)
            def _():
                @pl.when(has_before)
                def _():
                    vsend[3 + way] = vsend[2] + vrecv[2 + way]

                @pl.when(jnp.logical_not(has_before))
                def _():
                    vsend[3 + way] = vsend[2]

                v_send(way, ahead).start()

        return carry

    def stage_whole(t, carry):
        at = t % ZRING
        own = rown[t % OWN_RING].astype(F32)

        @pl.when(t >= 4)
        def _():
            out_wait(t - 4)

        @pl.when(has_left & has_right)
        def _():
            ostage[t % 4] = (own + zrecv[0, at].astype(F32) + zrecv[1, at].astype(F32)).astype(BF)

        @pl.when(has_left & jnp.logical_not(has_right))
        def _():
            ostage[t % 4] = (own + zrecv[0, at].astype(F32)).astype(BF)

        @pl.when(has_right & jnp.logical_not(has_left))
        def _():
            ostage[t % 4] = (own + zrecv[1, at].astype(F32)).astype(BF)

        out_start(t)

        @pl.when(has_left)
        def _():
            give(2, t, ZRING, zleft)

        @pl.when(has_right)
        def _():
            give(3, t, ZRING, zright)

        return carry

    def v_send(way, peer):
        return pltpu.make_async_remote_copy(
            src_ref=vsend.at[3 + way], dst_ref=vrecv.at[2 + way],
            send_sem=v_ssem.at[2 + way], recv_sem=v_rsem.at[2 + way],
            device_id=peer, device_id_type=MESH,
        )

    @pl.when(is_second)
    def _():
        result_stay().start()
        result_move().start()
        own_block(cot).wait()
        swap_block(cot).wait()

    def scale_back(j):
        part = aligned(j * blk, blk)

        @pl.when(is_first)
        def _():
            x_send(cot, dout, j, xb_ssem, xb_rsem).wait_recv()

        grad = cot[part, :].astype(F32)
        vec[3:4, :] += jnp.sum(grad * mb[part, :].astype(F32), 0, keepdims=True)
        low = (gains[0, 3:4, :] * grad).astype(BF)
        dmb[part, :] = low
        vec[9:10, :] += jnp.sum(low.astype(F32), 0, keepdims=True)

    def shrink_back(j, t):
        part = aligned(j * blk, blk)
        cols = aligned(t * width, width)
        back = dot_nt(dmb[part, :], wfc2[cols, :])
        low = (gp[part, cols].astype(F32) * back).astype(BF)
        du[part, cols] = low
        sums = jnp.sum(low.astype(F32), 0, keepdims=True)
        for i in range(width // 256):
            dcf[pl.ds(t * (width // 256) + i, 1), :] += sums[:, i * 256 : (i + 1) * 256]

    def middle_back(j):
        part = aligned(j * blk, blk)
        grad_two = dot_nt(du[part, :], wfc1[...])
        hat, rstd = norm_stats(rb[part, :])
        vec[2:3, :] += jnp.sum(grad_two * hat, 0, keepdims=True)
        vec[8:9, :] += jnp.sum(grad_two, 0, keepdims=True)
        middle = cot[part, :].astype(F32) + norm_back(grad_two, hat, rstd, gains[0, 2:3, :])
        drb[part, :] = middle
        vec[1:2, :] += jnp.sum(middle * zb[part, :].astype(F32), 0, keepdims=True)
        low = (gains[0, 1:2, :] * middle).astype(BF)
        dzb[part, :] = low
        vec[7:8, :] += jnp.sum(low.astype(F32), 0, keepdims=True)

    def heads_back(j):
        part = aligned(j * blk, blk)
        grad_o = dot_nt(dzb[part, :], wproj[...]).astype(BF).astype(F32)
        for i in range(pairs):
            cols = slice(i * 128, (i + 1) * 128)
            pair = grad_o[:, cols]
            both = pair * ob[part, cols].astype(F32)
            inner_a = jnp.sum(jnp.where(lane_row < 64, both, 0.0), -1, keepdims=True)
            inner_b = jnp.sum(jnp.where(lane_row < 64, 0.0, both), -1, keepdims=True)
            extra_a = three_parts(-inner_a, lane_row, 68)
            extra_b = three_parts(-inner_b, lane_row, 4)
            doaug[2 * i, part, :] = jnp.where(lane_row < 64, pair, extra_a).astype(BF)
            doaug[2 * i + 1, part, :] = jnp.where(lane_row < 64, extra_b, pair).astype(BF)

    def dkv_copy(index, j):
        part = aligned(j * blk, blk)
        return pltpu.make_async_remote_copy(
            src_ref=dkv_send.at[index, part],
            dst_ref=dkv_recv.at[index, part],
            send_sem=dkv_ssem.at[index, j],
            recv_sem=dkv_rsem.at[index, j],
            device_id=sib,
            device_id_type=MESH,
        )

    def quadrant(keys, values, query, outer):
        prob = jnp.exp(dot_nt(keys, query))
        diff = dot_nt(values, outer)
        slope = (prob * diff).astype(BF)
        return dot_tn(slope, keys), dot_nn(slope, query), dot_nn(prob.astype(BF), outer)

    def both_heads(parts):
        return [jnp.where(lane_row < 64, first, second) for first, second in zip(*parts)]

    def key_block(array, j):
        return jnp.concatenate([array[j * blk : (j + 1) * blk], array[rows + j * blk : rows + (j + 1) * blk]], 0)

    def pair_spans(pair):
        return [aligned(third * width + pair * 128, 128) for third in range(3)]

    def attend_back_first(pair):
        wide, narrow = [], []
        for i, (keys, values) in enumerate(aug_pair(pair)):
            query, outer = qaug[2 * pair + i], doaug[2 * pair + i]
            wide.append(quadrant(key_block(keys, 0), key_block(values, 0), query, outer))
            narrow.append(quadrant(key_block(keys, 1), key_block(values, 1), query[0:blk], outer[0:blk]))
        (dq_w, dk_w, dv_w), (dq_n, dk_n, dv_n) = both_heads(wide), both_heads(narrow)
        q_cols, k_cols, v_cols = pair_spans(pair)
        dkv_send[pair, 0:blk] = dk_w[blk:].astype(BF)
        dkv_send[pairs + pair, 0:blk] = dv_w[blk:].astype(BF)
        dkv_copy(pair, 0).start()
        dkv_copy(pairs + pair, 0).start()
        dkv_send[pair, blk:] = dk_n[blk:].astype(BF)
        dkv_send[pairs + pair, blk:] = dv_n[blk:].astype(BF)
        dqkv[0:blk, q_cols] = ((dq_w[0:blk] + dq_n) * 0.125).astype(BF)
        dqkv[blk:, q_cols] = (dq_w[blk:] * 0.125).astype(BF)
        dqkv[0:blk, k_cols] = dk_w[0:blk].astype(BF)
        dqkv[blk:, k_cols] = dk_n[0:blk].astype(BF)
        dqkv[0:blk, v_cols] = dv_w[0:blk].astype(BF)
        dqkv[blk:, v_cols] = dv_n[0:blk].astype(BF)

    def attend_back_second(duo):
        found = [second_terms(2 * duo + i) for i in range(2)]
        for i in range(2):
            second_sums(2 * duo + i, *found[i])

    def second_terms(pair):
        parts = []
        for i, (keys, values) in enumerate(aug_pair(pair)):
            query, outer = qaug[2 * pair + i, blk:], doaug[2 * pair + i, blk:]
            parts.append(quadrant(key_block(keys, 1), key_block(values, 1), query, outer))
        return both_heads(parts)

    def second_sums(pair, dq, dk, dv):
        q_cols, k_cols, v_cols = pair_spans(pair)
        for index, term in ((pair, dk), (pairs + pair, dv)):
            dkv_send[index, blk:] = (dkv_send[index, blk:].astype(F32) + term[blk:]).astype(BF)
            dkv_copy(index, 1).start()
        for cols, term in ((q_cols, dq * 0.125), (k_cols, dk[0:blk]), (v_cols, dv[0:blk])):
            dqkv[blk:, cols] = (dqkv[blk:, cols].astype(F32) + term).astype(BF)

    def finish_back(j):
        part = aligned(j * blk, blk)

        def collect(index, carry):
            dkv_copy(index, j).wait()
            cols = aligned(width + index * 128, 128)
            dqkv[part, cols] = (dqkv[part, cols].astype(F32) + dkv_recv[index, part].astype(F32)).astype(BF)
            return carry

        lax.fori_loop(0, 2 * pairs, collect, 0)

        @pl.when(is_first & (j == 0))
        def _():
            for i in range(chunks):
                x_send(hin, fout, i, x_ssem, x_rsem).wait_send()

        @pl.when(is_second & (j == 0))
        def _():
            result_stay().wait()
            result_move().wait_send()

        vec[5:6, :] += jnp.sum(dqkv[part, 0:width].astype(F32), 0, keepdims=True)
        vec[6:7, :] += jnp.sum(dqkv[part, 2 * width : 3 * width].astype(F32), 0, keepdims=True)
        grad_one = dot_nt(dqkv[part, :], wqkv[...])
        hat, rstd = norm_stats(hin[part, :].astype(F32))
        vec[0:1, :] += jnp.sum(grad_one * hat, 0, keepdims=True)
        vec[4:5, :] += jnp.sum(grad_one, 0, keepdims=True)
        total = drb[part, :] + norm_back(grad_one, hat, rstd, gains[0, 0:1, :])
        dout[part, :] = total.astype(BF)

        @pl.when(is_second)
        def _():
            x_send(cot, dout, j, xb_ssem, xb_rsem).start()

    tiles = ff // width
    per_block = tiles + 3
    dense = chunks * per_block
    first_end = dense + pairs
    second_end = first_end + 1 + pairs // 2

    beside = 22

    def pieces_done(v):
        total = second_end + 1
        first = per_block + 1
        spread = jnp.minimum(first + (v * (total - first) + beside - 1) // beside, total)
        return jnp.where(v < 0, 0, jnp.where(is_first, spread, total))

    def advance(stage, lag, count, v, at=lambda m: m):
        def done(v):
            return jnp.minimum(jnp.maximum(v + 1 - lag, 0), count)

        lax.fori_loop(at(done(v - 1)), at(done(v)), stage, 0)

    late = jnp.maximum(grp, groups - 1 - grp)
    chip_lag, group_lag, hop_lag = 2, 4, 2
    visits = mine + group_lag + hop_lag * (groups - 1)

    def piece(w, carry):
        @pl.when(w < dense)
        def _():
            j, r = w // per_block, w % per_block

            @pl.when(r == 0)
            def _():
                scale_back(j)

            @pl.when((r > 0) & (r <= tiles))
            def _():
                shrink_back(j, r - 1)

            @pl.when(r == tiles + 1)
            def _():
                middle_back(j)

            @pl.when(r == tiles + 2)
            def _():
                heads_back(j)

        @pl.when((w >= dense) & (w < first_end))
        def _():
            attend_back_first(w - dense)

        @pl.when((w > first_end) & (w < second_end))
        def _():
            attend_back_second(w - first_end - 1)

        @pl.when((w == first_end) | (w == second_end))
        def _():
            finish_back((w - first_end) // (pairs // 2 + 1))

        return carry

    def visit(v, carry):
        lax.fori_loop(pieces_done(v - 1), pieces_done(v), piece, 0)
        advance(stage_own, 0, jnp.minimum(mine, slots), v, slot_at)
        advance(stage_chip, chip_lag, mine, v, slot_at)
        advance(stage_group, group_lag, mine, v)
        for way in range(2):
            place = grp if way == 0 else groups - 1 - grp
            advance(functools.partial(stage_line, way), group_lag + hop_lag * place, mine, v)
        advance(stage_whole, group_lag + hop_lag * late, mine, v)

        @pl.when(is_first & (v == slots))
        def _():
            result_stay().start()
            result_move().start()

        return carry

    lax.fori_loop(0, visits, visit, 0)

    def drain(i, carry):
        y_copy(mine - YRING + i).wait_send()

        @pl.when(i < 4)
        def _():
            out_wait(mine - 4 + i)

        @pl.when(i < RING)
        def _():
            core_copy(slots - RING + i).wait_send()

            @pl.when(has_right)
            def _():
                z_copy(0, mine - RING + i).wait_send()

            @pl.when(has_left)
            def _():
                z_copy(1, mine - RING + i).wait_send()

        return carry

    lax.fori_loop(0, YRING, drain, 0)

    @pl.when(is_first)
    def _():
        for e in range(LENT):
            lend_copy(e).wait_send()
            lent_out(e, "wait_recv")

    @pl.when(has_right)
    def _():
        v_send(0, zright).wait_send()

    @pl.when(has_left)
    def _():
        v_send(1, zleft).wait_send()

    total = vsend[2]
    vec_out[...] = total

    @pl.when(has_left)
    def _():
        vec_out[...] = vec_out[...] + vrecv[2]

    @pl.when(has_right)
    def _():
        vec_out[...] = vec_out[...] + vrecv[3]

    @pl.when(is_first)
    def _():
        result_stay().wait()
        result_move().wait_send()

    @pl.when(is_second)
    def _():
        for j in range(chunks):
            x_send(cot, dout, j, xb_ssem, xb_rsem).wait_send()

    result_move().wait_recv()

HEADS = 12
HDIM = 64


def from_behind(block, axis, distance):
    devices = range(lax.axis_size(axis))
    route = [(i - distance, i) for i in devices if i - distance in devices]
    return lax.ppermute(block, axis, route)


def normalize(values, scale_vec, shift_vec):
    row_mean = jnp.mean(values, -1, keepdims=True)
    centered = values - row_mean
    variance = jnp.mean(centered * centered, -1, keepdims=True)
    return centered * lax.rsqrt(variance + 1e-06) * scale_vec + shift_vec


def gelu_exact(values):
    return jax.nn.gelu(values, approximate=False)


def back_dot(left, weight):
    return lax.dot_general(
        left, weight, (((1,), (1,)), ((), ())), preferred_element_type=jnp.float32
    )


def row_contract(left, right):
    return lax.dot_general(
        left, right, (((0,), (0,)), ((), ())), preferred_element_type=jnp.float32
    )


def masked_scores(query, keys_all, seg_row):
    row_count = query.shape[0]
    length = keys_all.shape[0]
    start = lax.axis_index("narrow") * row_count
    own_seg = lax.dynamic_slice_in_dim(seg_row, start, row_count)
    same = own_seg[:, None] == seg_row[None, :]
    raw = (
        jnp.einsum(
            "qhd,khd->hqk",
            query.reshape(row_count, HEADS, HDIM),
            keys_all.reshape(length, HEADS, HDIM),
            preferred_element_type=jnp.float32,
        )
        * 0.125
    )
    return jnp.where(same[None], raw, -1e30)


def forward_layer(inputs, seg_row, weights):
    qkv_w, proj_w, fc1_w, fc2_w, gain_rows, bias_rows, fc1_b = weights
    row_count, model_width = inputs.shape
    normed = normalize(inputs, gain_rows[0], bias_rows[0]).astype(jnp.bfloat16)
    qkv = jnp.dot(normed, qkv_w, preferred_element_type=jnp.float32)
    query = (qkv[:, :model_width] + bias_rows[1]).astype(jnp.bfloat16)
    key_rows = qkv[:, model_width : 2 * model_width].astype(jnp.bfloat16)
    value_rows = (qkv[:, 2 * model_width :] + bias_rows[2]).astype(jnp.bfloat16)
    keys_all, values_all = (
        lax.all_gather(key_rows, "narrow", axis=0, tiled=True),
        lax.all_gather(value_rows, "narrow", axis=0, tiled=True),
    )
    length = keys_all.shape[0]
    scores = masked_scores(query, keys_all, seg_row)
    peak = jnp.max(scores, -1, keepdims=True)
    log_total = peak + jnp.log(jnp.sum(jnp.exp(scores - peak), -1, keepdims=True))
    probs = jnp.exp(scores - log_total).astype(jnp.bfloat16)
    mixed = jnp.einsum(
        "hqk,khd->qhd",
        probs,
        values_all.reshape(length, HEADS, HDIM),
        preferred_element_type=jnp.float32,
    )
    attended = mixed.reshape(row_count, model_width).astype(jnp.bfloat16)
    branch = jnp.dot(attended, proj_w, preferred_element_type=jnp.float32) + bias_rows[3]
    middle = inputs + gain_rows[1] * branch
    normed_two = normalize(middle, gain_rows[2], bias_rows[4]).astype(jnp.bfloat16)
    hidden_pre = jnp.dot(normed_two, fc1_w, preferred_element_type=jnp.float32) + fc1_b
    activated = gelu_exact(hidden_pre).astype(jnp.bfloat16)
    mlp_out = jnp.dot(activated, fc2_w, preferred_element_type=jnp.float32) + bias_rows[5]
    output = middle + gain_rows[3] * mlp_out
    saved = (
        inputs,
        query,
        keys_all,
        values_all,
        log_total,
        attended,
        branch,
        middle,
        hidden_pre,
        mlp_out,
    )
    return (output, saved)


def backward_layer(grad_out, saved, seg_row, weights):
    qkv_w, proj_w, fc1_w, fc2_w, gain_rows, bias_rows, fc1_b = weights
    (
        inputs,
        query,
        keys_all,
        values_all,
        log_total,
        attended,
        branch,
        middle,
        hidden_pre,
        mlp_out,
    ) = saved
    row_count, model_width = inputs.shape
    length = keys_all.shape[0]
    scale_two = jnp.sum(grad_out * mlp_out, 0)
    mlp_grad = (gain_rows[3] * grad_out).astype(jnp.bfloat16)
    activated, gelu_pull = jax.vjp(gelu_exact, hidden_pre)
    grad_fc2 = row_contract(activated.astype(jnp.bfloat16), mlp_grad)
    shift_five = jnp.sum(mlp_grad.astype(jnp.float32), 0)
    pre_grad = gelu_pull(back_dot(mlp_grad, fc2_w))[0].astype(jnp.bfloat16)
    normed_two, norm_pull_two = jax.vjp(normalize, middle, gain_rows[2], bias_rows[4])
    grad_fc1 = row_contract(normed_two.astype(jnp.bfloat16), pre_grad)
    grad_fc1b = jnp.sum(pre_grad.astype(jnp.float32), 0)
    middle_part, gain_two, shift_four = norm_pull_two(back_dot(pre_grad, fc1_w))
    middle_grad = grad_out + middle_part
    scale_one = jnp.sum(middle_grad * branch, 0)
    branch_grad = (gain_rows[1] * middle_grad).astype(jnp.bfloat16)
    grad_proj = row_contract(attended, branch_grad)
    shift_three = jnp.sum(branch_grad.astype(jnp.float32), 0)
    heads_grad = back_dot(branch_grad, proj_w).astype(jnp.bfloat16).reshape(row_count, HEADS, HDIM)
    scores = masked_scores(query, keys_all, seg_row)
    probs = jnp.exp(scores - log_total)
    keys_heads = keys_all.reshape(length, HEADS, HDIM)
    prob_grad = jnp.einsum(
        "qhd,khd->hqk",
        heads_grad,
        values_all.reshape(length, HEADS, HDIM),
        preferred_element_type=jnp.float32,
    )
    inner = jnp.sum(probs * prob_grad, -1, keepdims=True)
    score_grad = (probs * (prob_grad - inner)).astype(jnp.bfloat16)
    query_grad = (
        (
            jnp.einsum("hqk,khd->qhd", score_grad, keys_heads, preferred_element_type=jnp.float32)
            * 0.125
        )
        .reshape(row_count, model_width)
        .astype(jnp.bfloat16)
    )
    key_part = (
        jnp.einsum(
            "hqk,qhd->khd",
            score_grad,
            query.reshape(row_count, HEADS, HDIM),
            preferred_element_type=jnp.float32,
        )
        * 0.125
    ).reshape(length, model_width)
    value_part = jnp.einsum(
        "hqk,qhd->khd", probs.astype(jnp.bfloat16), heads_grad, preferred_element_type=jnp.float32
    ).reshape(length, model_width)
    key_sum, value_sum = (
        lax.psum_scatter(
            key_part.astype(jnp.bfloat16), "narrow", scatter_dimension=0, tiled=True
        ).astype(jnp.float32),
        lax.psum_scatter(
            value_part.astype(jnp.bfloat16), "narrow", scatter_dimension=0, tiled=True
        ).astype(jnp.float32),
    )
    key_grad = key_sum.astype(jnp.bfloat16)
    value_grad = value_sum.astype(jnp.bfloat16)
    qkv_grad = jnp.concatenate([query_grad, key_grad, value_grad], 1)
    normed, norm_pull_one = jax.vjp(normalize, inputs, gain_rows[0], bias_rows[0])
    grad_qkv = row_contract(normed.astype(jnp.bfloat16), qkv_grad)
    input_part, gain_one, shift_zero = norm_pull_one(back_dot(qkv_grad, qkv_w))
    input_grad = middle_grad + input_part
    gain_grads = jnp.stack([gain_one, scale_one, gain_two, scale_two])
    shift_grads = jnp.stack(
        [
            shift_zero,
            jnp.sum(query_grad.astype(jnp.float32), 0),
            jnp.sum(value_grad.astype(jnp.float32), 0),
            shift_three,
            shift_four,
            shift_five,
        ]
    )
    return (
        input_grad,
        (grad_qkv, grad_proj, grad_fc1, grad_fc2, gain_grads, shift_grads, grad_fc1b),
    )


def general_body(
    boundary, segments, qkv_weight, proj_weight, fc1_weight, fc2_weight, gains, biases, fc1_bias
):
    weights = (
        qkv_weight[0],
        proj_weight[0],
        fc1_weight[0],
        fc2_weight[0],
        gains[0],
        biases[0],
        fc1_bias[0],
    )
    local_ends = boundary[0]
    micro_count = local_ends.shape[0]
    first_section = lax.axis_index("section") == 0
    arrived = jnp.zeros(local_ends.shape[1:], jnp.bfloat16)
    stored = []
    outputs = []
    for step_index in range(micro_count + 1):
        lower = min(step_index, micro_count - 1)
        upper = max(step_index - 1, 0)
        inputs = jnp.where(
            first_section, local_ends[lower].astype(jnp.float32), arrived.astype(jnp.float32)
        )
        seg_row = jnp.where(first_section, segments[lower], segments[upper])
        output, saved = forward_layer(inputs, seg_row, weights)
        stored.append((saved, seg_row))
        outputs.append(output)
        if step_index < micro_count:
            arrived = from_behind(output.astype(jnp.bfloat16), "section", 1)
    totals = tuple((jnp.zeros(w.shape, jnp.float32) for w in weights))
    returned = jnp.zeros(local_ends.shape[1:], jnp.bfloat16)
    input_grads = []
    for step_index in range(micro_count + 1):
        lower = min(step_index, micro_count - 1)
        upper = max(step_index - 1, 0)
        picked = jax.tree.map(
            lambda early, later: jnp.where(first_section, early, later),
            stored[upper],
            stored[lower + 1],
        )
        cotangent = jnp.where(
            first_section, returned.astype(jnp.float32), local_ends[lower].astype(jnp.float32)
        )
        is_valid = jnp.where(first_section, step_index >= 1, step_index < micro_count)
        cotangent = jnp.where(is_valid, cotangent, 0.0)
        grad_in, pieces = backward_layer(cotangent, picked[0], picked[1], weights)
        totals = tuple((acc + part for acc, part in zip(totals, pieces)))
        input_grads.append(grad_in)
        if step_index < micro_count:
            returned = from_behind(grad_in.astype(jnp.bfloat16), "section", -1)
    results = jnp.stack(
        [jnp.where(first_section, input_grads[j + 1], outputs[j + 1]) for j in range(micro_count)]
    )
    results = results.astype(jnp.bfloat16)
    within = (
        lax.psum_scatter(
            totals[0].astype(jnp.bfloat16), "narrow", scatter_dimension=0, tiled=True
        ).astype(jnp.float32),
        lax.psum_scatter(
            totals[1].astype(jnp.bfloat16), "narrow", scatter_dimension=0, tiled=True
        ).astype(jnp.float32),
        lax.psum_scatter(
            totals[2].astype(jnp.bfloat16), "narrow", scatter_dimension=0, tiled=True
        ).astype(jnp.float32),
        lax.psum_scatter(
            totals[3].astype(jnp.bfloat16), "narrow", scatter_dimension=0, tiled=True
        ).astype(jnp.float32),
        lax.psum_scatter(
            totals[4].astype(jnp.bfloat16), "narrow", scatter_dimension=1, tiled=True
        ).astype(jnp.float32),
        lax.psum_scatter(
            totals[5].astype(jnp.bfloat16), "narrow", scatter_dimension=1, tiled=True
        ).astype(jnp.float32),
        lax.psum_scatter(
            totals[6].astype(jnp.bfloat16), "narrow", scatter_dimension=0, tiled=True
        ).astype(jnp.float32),
    )
    final = (
        lax.psum(within[0].astype(jnp.bfloat16), "group").astype(jnp.float32),
        lax.psum(within[1].astype(jnp.bfloat16), "group").astype(jnp.float32),
        lax.psum(within[2].astype(jnp.bfloat16), "group").astype(jnp.float32),
        lax.psum(within[3].astype(jnp.bfloat16), "group").astype(jnp.float32),
        lax.psum(within[4].astype(jnp.bfloat16), "group").astype(jnp.float32),
        lax.psum(within[5].astype(jnp.bfloat16), "group").astype(jnp.float32),
        lax.psum(within[6].astype(jnp.bfloat16), "group").astype(jnp.float32),
    )
    return (
        results[None],
        final[0][None],
        final[1][None],
        final[2][None],
        final[3][None],
        final[4][None],
        final[5][None],
        final[6][None],
    )


def fused_body(
    groups, boundary, segments, qkv_weight, proj_weight, fc1_weight, fc2_weight, gains, biases, fc1_bias
):
    blk, width = boundary.shape[2:]
    rows, keys = 2 * blk, 4 * blk
    ff = fc1_weight.shape[2]
    heads = width // HDIM
    nar = lax.axis_index(NARROW)

    def bf(*shape):
        return pltpu.VMEM(shape, BF)

    def f32(*shape):
        return pltpu.VMEM(shape, F32)

    dma = pltpu.SemaphoreType.DMA
    slot = (SLOT_ROWS, SLOT_COLS)
    scratch = [
        bf(width, 3 * width), bf(width, width), bf(width, ff), bf(ff, width),
        bf(rows, width), bf(rows, width), bf(3, rows, width), bf(heads, rows, 128),
        bf(keys, width), bf(keys, width), bf(rows, width), f32(rows, width),
        bf(rows, ff + 4 * width), bf(rows, ff), bf(rows, width), bf(rows, width),
        bf(rows, width), bf(heads, rows, 128), bf(heads, rows, 128), bf(heads, rows, 128),
        bf(keys, 128), f32(RING, 2, *slot), bf(RING, 2, *slot), bf(RING, 2, *slot),
        bf(YRING, *slot), bf(YRING, *slot), bf(OWN_RING, *slot), bf(2, RING, *slot), bf(2, ZRING, *slot), bf(4, *slot),
        f32(16, width), f32(16, 256), f32(5, 16, width + 256), f32(4, 16, width + 256), bf(LENT, 2, *slot),
        dma((4,)), dma(()), dma((2,)), dma((2, 2)), dma((2, 2)), dma((2,)), dma((2,)), dma((2,)), dma((2,)),
        dma((heads, 2)), dma((heads, 2)), dma((3,)),
        dma((RING,)), dma((RING,)), dma((YRING,)), dma((YRING,)), dma((2, RING)), dma((2, ZRING)), dma((4, 2)),
        dma((4,)), dma((4,)), dma((3 * LENT,)), dma((3 * LENT,)), pltpu.SemaphoreType.REGULAR((4,)),
    ]
    hbm = pl.BlockSpec(memory_space=pl.ANY)
    vmem = pl.BlockSpec(memory_space=pltpu.VMEM)
    out = pl.pallas_call(
        functools.partial(kernel, groups),
        out_shape=(
            jax.ShapeDtypeStruct((2, blk, width), BF),
            jax.ShapeDtypeStruct((width // 4, 3 * width), BF),
            jax.ShapeDtypeStruct((width // 4, width), BF),
            jax.ShapeDtypeStruct((width // 4, ff), BF),
            jax.ShapeDtypeStruct((ff // 4, width), BF),
            jax.ShapeDtypeStruct((16, width + 256), F32),
        ),
        in_specs=[hbm, vmem, hbm, hbm, hbm, hbm, vmem, vmem, vmem],
        out_specs=(hbm, hbm, hbm, hbm, hbm, vmem),
        scratch_shapes=scratch,
        compiler_params=pltpu.CompilerParams(
            collective_id=0, has_side_effects=True, vmem_limit_bytes=63 * 2**20
        ),
        name="two_layers",
    )(boundary, segments, qkv_weight, proj_weight, fc1_weight, fc2_weight, gains, biases.reshape(1, -1), fc1_bias)
    results, qkv, proj, fc1, fc2, vecs = out
    return widen(results, qkv, proj, fc1, fc2, vecs)


def widen_kernel(results, qkv, proj, fc1, fc2, vecs, *outs):
    o_results, o_qkv, o_proj, o_fc1, o_fc2, o_gains, o_biases, o_fc1b = outs
    o_results[0] = results[...]
    for src, dst in ((qkv, o_qkv), (proj, o_proj), (fc1, o_fc1), (fc2, o_fc2)):
        dst[0] = src[...].astype(F32)

    @pl.when(pl.program_id(0) == 0)
    def _():
        nar = lax.axis_index(NARROW)
        share = o_gains.shape[2]
        parts = o_fc1b.shape[1] // 256
        for i in range(4):
            @pl.when(nar == i)
            def _():
                cols = slice(i * share, (i + 1) * share)
                o_gains[0] = vecs[0:4, cols]
                for row in range(6):
                    o_biases[row] = vecs[4 + row : 5 + row, cols]
                for part in range(parts):
                    o_fc1b[:, part * 256 : (part + 1) * 256] = vecs[
                        i * parts + part : i * parts + part + 1, 4 * share :
                    ]


def widen(results, qkv, proj, fc1, fc2, vecs):
    steps = 4

    def block(shape, lead):
        size = (shape[0] // steps,) + shape[1:]
        rest = (0,) * (len(shape) - 1)
        if lead:
            return pl.BlockSpec((1,) + size, lambda i: (0, i) + rest)
        return pl.BlockSpec(size, lambda i: (i,) + rest)

    def whole(shape):
        return pl.BlockSpec(shape, lambda i: (0,) * len(shape))

    halves, rows, width = results.shape
    flat = results.reshape(halves * rows, width)
    flats = (flat, qkv, proj, fc1, fc2)
    share = width // 4
    small = ((1, 4, share), (6, 1, share), (1, fc2.shape[0]))
    out = pl.pallas_call(
        widen_kernel,
        grid=(steps,),
        in_specs=[block(a.shape, False) for a in flats] + [whole(vecs.shape)],
        out_specs=[block(a.shape, True) for a in flats] + [whole(s) for s in small],
        out_shape=[jax.ShapeDtypeStruct((1,) + a.shape, BF if i == 0 else F32) for i, a in enumerate(flats)]
        + [jax.ShapeDtypeStruct(s, F32) for s in small],
        name="widen",
    )(*flats, vecs)
    return (
        out[0].reshape(1, halves, rows, width),
        *out[1:6],
        out[6].transpose(1, 0, 2),
        out[7],
    )


def solution(mesh):
    sections, groups, narrow = (mesh.shape[name] for name in (SECTION, GROUP, NARROW))
    placed = (
        P("section", "group", "narrow", None),
        P("group", None),
        P("section", None, None),
        P("section", None, None),
        P("section", None, None),
        P("section", None, None),
        P("section", None, None),
        P("section", None, None),
        P("section", None),
    )
    fused = sections == 2 and narrow == 4 and groups > 1
    body = functools.partial(fused_body, groups) if fused else general_body
    return jax.shard_map(
        body,
        mesh=mesh,
        in_specs=placed,
        out_specs=(
            P("section", "group", "narrow", None),
            P("section", "narrow", None),
            P("section", "narrow", None),
            P("section", "narrow", None),
            P("section", "narrow", None),
            P("section", None, "narrow"),
            P("section", None, "narrow"),
            P("section", "narrow"),
        ),
        check_vma=False,
    )
```

```python
import functools

import jax
import jax.numpy as jnp
from jax import lax
from jax.experimental import pallas as pl
from jax.experimental.pallas import tpu as pltpu
from jax.sharding import PartitionSpec as P

SECTION, GROUP, NARROW = "section", "group", "narrow"
HALVES = 2
BIG = 1e30
SLOT_ROWS = 192
SLOT_COLS = 256
RING = 6
ZRING = 8
YRING = 6
OWN_RING = 12
LENT = 5
LEND_EVERY = 5
BF = jnp.bfloat16
F32 = jnp.float32
MESH = pl.DeviceIdType.MESH


def dot_nn(left, right):
    return lax.dot_general(left, right, (((1,), (0,)), ((), ())), preferred_element_type=F32)


def dot_nt(left, right):
    return lax.dot_general(left, right, (((1,), (1,)), ((), ())), preferred_element_type=F32)


def dot_tn(left, right):
    return lax.dot_general(left, right, (((0,), (0,)), ((), ())), preferred_element_type=F32)


def aligned(start, size, unit=128):
    return pl.ds(pl.multiple_of(start, unit), size)


def norm_stats(values):
    mean = jnp.mean(values, -1, keepdims=True)
    centered = values - mean
    var = jnp.mean(centered * centered, -1, keepdims=True)
    rstd = lax.rsqrt(var + 1e-06)
    return centered * rstd, rstd


def norm_back(grad, hat, rstd, gain):
    scaled = grad * gain
    mean_one = jnp.mean(scaled, -1, keepdims=True)
    mean_two = jnp.mean(scaled * hat, -1, keepdims=True)
    return rstd * (scaled - mean_one - hat * mean_two)


def three_parts(column, lane, base):
    high = column.astype(BF).astype(F32)
    rest = column - high
    mid = rest.astype(BF).astype(F32)
    low = rest - mid
    return jnp.where(
        lane == base, high, jnp.where(lane == base + 1, mid, jnp.where(lane == base + 2, low, 0.0))
    )


def kernel(groups, *refs):
    (
        boundary, segments, wqkv_h, wproj_h, wfc1_h, wfc2_h, gains, biases, fc1b,
        results, g_qkv, g_proj, g_fc1, g_fc2, vec_out,
        wqkv, wproj, wfc1, wfc2,
        hin, cot, lhs, qaug, kall, vall, zb, rb, rhs, act, mb, fout,
        dmb, doaug, dkv_send, dkv_recv,
        segf, ckeep, csend, crecv, ysend, yrecv, rown, zsend, zrecv, ostage,
        vec, dcf, vsend, vrecv, lent,
        w_sem, b_sem, bx_sem, kv_ssem, kv_rsem, x_ssem, x_rsem, xb_ssem, xb_rsem,
        dkv_ssem, dkv_rsem, res_sem,
        c_ssem, c_rsem, y_ssem, y_rsem, z_ssem, z_rsem, o_sem,
        v_ssem, v_rsem, l_ssem, l_rsem, credit,
    ) = refs
    sec = lax.axis_index(SECTION)
    grp = lax.axis_index(GROUP)
    nar = lax.axis_index(NARROW)
    yy = nar // 2
    cc = nar % 2
    sib = (sec, grp, nar + 1 - 2 * cc)
    ynb = (sec, grp, (nar + 2) % 4)
    xnb = (1 - sec, grp, nar)
    zright = (sec, grp + 1, nar)
    zleft = (sec, grp - 1, nar)
    has_right = grp < groups - 1
    has_left = grp > 0
    is_first = sec == 0
    is_second = sec == 1

    blk = boundary.shape[2]
    rows = 2 * blk
    width = boundary.shape[3]
    ff = wfc1.shape[1]
    pairs = width // 128
    chunks = rows // blk

    n2, ob, n1 = lhs.at[0], lhs.at[1], lhs.at[2]
    gp = du = rhs.at[:, 0:ff]
    dzb, dqkv = rhs.at[:, ff : ff + width], rhs.at[:, ff + width :]
    drb, dout = rb, fout

    def bias(row):
        return biases[0:1, row * width : (row + 1) * width]

    weight_copies = [
        pltpu.make_async_copy(src.at[0], dst, w_sem.at[i])
        for i, (src, dst) in enumerate(
            ((wqkv_h, wqkv), (wproj_h, wproj), (wfc1_h, wfc1), (wfc2_h, wfc2))
        )
    ]
    for copy in weight_copies:
        copy.start()

    def own_block(dst):
        return pltpu.make_async_copy(boundary.at[0, yy], dst.at[aligned(yy * blk, blk)], b_sem)

    half_blk = blk // 2

    def swap_half(dst, half):
        return pltpu.make_async_remote_copy(
            src_ref=boundary.at[0, 1 - yy, pl.ds(half * half_blk, half_blk)],
            dst_ref=dst.at[aligned(yy * blk + half * half_blk, half_blk)],
            send_sem=bx_sem.at[0, half],
            recv_sem=bx_sem.at[1, half],
            device_id=ynb,
            device_id_type=MESH,
        )

    @pl.when(is_first)
    def _():
        own_block(hin).start()

    @pl.when(is_second)
    def _():
        own_block(cot).start()

    barrier = pltpu.get_barrier_semaphore()
    for peer in (sib, ynb, xnb):
        pl.semaphore_signal(barrier, inc=1, device_id=peer, device_id_type=MESH)

    @pl.when(has_right)
    def _():
        pl.semaphore_signal(barrier, inc=1, device_id=zright, device_id_type=MESH)

    @pl.when(has_left)
    def _():
        pl.semaphore_signal(barrier, inc=1, device_id=zleft, device_id_type=MESH)

    pl.semaphore_wait(barrier, 3 + has_right.astype(jnp.int32) + has_left.astype(jnp.int32))

    @pl.when(is_first)
    def _():
        swap_half(hin, 0).start()
        swap_half(hin, 1).start()

    @pl.when(is_second)
    def _():
        swap_half(cot, 0).start()
        swap_half(cot, 1).start()

    keys_seg = jnp.concatenate(
        [
            segments[pl.ds(yy, 1), aligned((half * 2 + core) * blk, blk)]
            for core in (cc, 1 - cc)
            for half in range(2)
        ],
        1,
    )
    feature = lax.rem(lax.broadcasted_iota(jnp.int32, (128, 1), 0), 64)
    hot = jnp.where(keys_seg == feature, 1.0, 0.0)
    ones = jnp.where((feature >= 4) & (feature < 7), 1.0, 0.0)
    segf[...] = jnp.where(feature < 4, hot, ones).T.astype(BF)
    vec[...] = jnp.zeros_like(vec)
    dcf[...] = jnp.zeros_like(dcf)

    lane_row = lax.broadcasted_iota(jnp.int32, (1, 128), 1)
    first_row = jnp.where(lane_row < 64, 1.0, 0.0).astype(BF)
    second_row = jnp.where(lane_row < 64, 0.0, 1.0).astype(BF)
    half_lane = lax.rem(lane_row, 64)
    penalty_row = jnp.where(half_lane < 4, BIG, 0.0)

    def x_send(dst, src, j, ssem, rsem):
        part = aligned(j * blk, blk)
        return pltpu.make_async_remote_copy(
            src_ref=src.at[part],
            dst_ref=dst.at[part],
            send_sem=ssem.at[j],
            recv_sem=rsem.at[j],
            device_id=xnb,
            device_id_type=MESH,
        )

    def x_half(half):
        part = aligned((chunks - 1) * blk + half * half_blk, half_blk)
        return pltpu.make_async_remote_copy(
            src_ref=fout.at[part],
            dst_ref=hin.at[part],
            send_sem=x_ssem.at[chunks - 1 + half],
            recv_sem=x_rsem.at[chunks - 1 + half],
            device_id=xnb,
            device_id_type=MESH,
        )

    def kv_copy(which, part):
        ref = (kall, vall)[which]
        index = part.start // half_blk
        return pltpu.make_async_remote_copy(
            src_ref=ref.at[part],
            dst_ref=ref.at[aligned(part.start + rows, part.size)],
            send_sem=kv_ssem.at[which, index],
            recv_sem=kv_rsem.at[which, index],
            device_id=sib,
            device_id_type=MESH,
        )

    def project(part):
        size = part.size
        hat, _ = norm_stats(hin[part, :].astype(F32))
        normed = (hat * gains[0, 0:1, :] + bias(0)).astype(BF)
        n1[part, :] = normed
        kall[part, :] = dot_nn(normed, wqkv[:, width : 2 * width]).astype(BF)
        kv_copy(0, part).start()
        vall[part, :] = (dot_nn(normed, wqkv[:, 2 * width :]) + bias(2)).astype(BF)
        kv_copy(1, part).start()
        low = ((dot_nn(normed, wqkv[:, 0:width]) + bias(1)).astype(BF) * 0.125).astype(F32)
        penalty = (segf[part, :].astype(F32) - 1.0) * penalty_row
        for i in range(pairs):
            pair = low[:, i * 128 : (i + 1) * 128]
            qaug[2 * i, part, :] = jnp.where(lane_row < 64, pair, penalty).astype(BF)
            qaug[2 * i + 1, part, :] = jnp.where(lane_row < 64, penalty, pair).astype(BF)

    @pl.when(is_first)
    def _():
        own_block(hin).wait()

    @pl.when(is_second)
    def _():
        x_send(hin, fout, 0, x_ssem, x_rsem).wait_recv()

    weight_copies[0].wait()
    first_at = jnp.where(is_first, yy, 0) * blk
    project(aligned(first_at, blk))

    def project_half(half, carry):
        @pl.when(is_first)
        def _():
            swap_half(hin, half).wait()

        @pl.when(is_second)
        def _():
            x_half(half).wait_recv()

        project(aligned(blk - first_at + half * half_blk, half_blk))
        return carry

    lax.fori_loop(0, 2, project_half, 0)
    for which in range(2):
        kv_copy(which, aligned(first_at, blk)).wait()
        for half in range(2):
            kv_copy(which, aligned(blk - first_at + half * half_blk, half_blk)).wait()

    def feed_forward(part):
        branch = dot_nn(ob[part, :], wproj[...]) + bias(3)
        zb[part, :] = branch.astype(BF)
        middle = hin[part, :].astype(F32) + gains[0, 1:2, :] * branch
        rb[part, :] = middle
        hat, _ = norm_stats(middle)
        n2[part, :] = (hat * gains[0, 2:3, :] + bias(4)).astype(BF)

        def expand(t, carry):
            cols = aligned(t * width, width)
            pre = dot_nn(n2[part, :], wfc1[:, cols]) + fc1b[0:1, cols]
            phi = 0.5 + 0.5 * lax.erf(pre * 0.7071067811865476)
            act[part, cols] = (pre * phi).astype(BF)
            slope = phi + pre * (jnp.exp(-0.5 * pre * pre) * 0.3989422804014327)
            gp[part, cols] = slope.astype(BF)
            return carry

        lax.fori_loop(0, ff // width, expand, 0, unroll=True)
        mlp = dot_nn(act[part, :], wfc2[...]) + bias(5)
        mb[part, :] = mlp.astype(BF)
        fout[part, :] = (rb[part, :] + gains[0, 3:4, :] * mlp).astype(BF)

    def forward_block(j, carry):
        part = aligned(j * blk, blk)

        feats = segf[...]
        own_pen = ((segf[part, :].astype(F32) - 1.0) * penalty_row).astype(BF) * first_row

        def attend(trio, carry):
            items = [trio * 3 + i for i in range(3)]
            spans = [aligned(pair * 128, 128) for pair in items]
            scores = []
            for pair, cols in zip(items, spans):
                query = jnp.concatenate(
                    [
                        jnp.concatenate([qaug[2 * pair, part, :] * first_row, own_pen], 1),
                        jnp.concatenate([qaug[2 * pair + 1, part, :] * second_row, own_pen], 1),
                    ],
                    0,
                )
                scores.append(dot_nt(query, jnp.concatenate([kall[:, cols], feats], 1)))
            for pair, cols, score in zip(items, spans, scores):
                peak = jnp.max(score, -1, keepdims=True)
                expo = jnp.exp(score - peak).astype(BF)
                mixed = dot_nn(expo, jnp.concatenate([vall[:, cols], feats], 1))
                total = mixed[:, 132:133]
                outs = mixed[:, 0:128] / total
                log_total = peak + jnp.log(total)
                for i in range(2):
                    base = 64 * (1 - i)
                    extra = three_parts(-log_total[i * blk : (i + 1) * blk], lane_row, base + 4)
                    query = qaug[2 * pair + i, part, :]
                    qaug[2 * pair + i, part, :] = (query.astype(F32) + extra).astype(BF)
                ob[part, cols] = jnp.where(lane_row < 64, outs[:blk], outs[blk:]).astype(BF)
            return carry

        lax.fori_loop(0, pairs // 3, attend, 0, unroll=True)

        @pl.when(j == 0)
        def _():
            for copy in weight_copies[1:]:
                copy.wait()

        @pl.when(is_first & (j == chunks - 1))
        def _():
            def feed_half(half, carry):
                feed_forward(aligned((chunks - 1) * blk + half * half_blk, half_blk))
                x_half(half).start()
                return carry

            lax.fori_loop(0, 2, feed_half, 0)

        @pl.when(is_second | (j < chunks - 1))
        def _():
            feed_forward(part)

        @pl.when(is_first & (j < chunks - 1))
        def _():
            x_send(hin, fout, j, x_ssem, x_rsem).start()

        return carry

    lax.fori_loop(0, chunks, forward_block, 0)

    n_fc2 = 2 * (width // 128)
    n_fc1 = ff // SLOT_COLS
    n_proj = width // SLOT_COLS
    n_qkv = 3 * width // SLOT_COLS
    lo_fc1 = n_fc2
    lo_proj = lo_fc1 + n_fc1
    lo_qkv = lo_proj + n_proj
    slots = lo_qkv + n_qkv
    mine = jnp.where(is_first, slots - LENT, slots + LENT)
    vslot = slots - LENT - 4
    lent_from = slots - LENT - 1

    def slot_at(m):
        return jnp.where(is_first, m + jnp.minimum(m // (LEND_EVERY - 1), LENT), m)

    def place_of(p):
        return jnp.where(is_first, p - jnp.minimum(p // LEND_EVERY, LENT), p)

    def lent_before(m):
        return jnp.minimum(jnp.maximum(m - lent_from, 0), LENT)

    def own_slot(m):
        return jnp.where(is_first, slot_at(m), m - lent_before(m))

    def is_borrowed(m):
        return is_second & (m >= lent_from) & (m < lent_from + LENT)

    def is_lent(p):
        return is_first & (p % LEND_EVERY == LEND_EVERY - 1) & (p < LENT * LEND_EVERY)

    def core_copy(t):
        at = t % RING
        return pltpu.make_async_remote_copy(
            src_ref=csend.at[at], dst_ref=crecv.at[at],
            send_sem=c_ssem.at[at], recv_sem=c_rsem.at[at],
            device_id=sib, device_id_type=MESH,
        )

    def y_copy(t):
        at = t % YRING
        return pltpu.make_async_remote_copy(
            src_ref=ysend.at[at], dst_ref=yrecv.at[at],
            send_sem=y_ssem.at[at], recv_sem=y_rsem.at[at],
            device_id=ynb, device_id_type=MESH,
        )

    def z_copy(way, t):
        return pltpu.make_async_remote_copy(
            src_ref=zsend.at[way, t % RING], dst_ref=zrecv.at[way, t % ZRING],
            send_sem=z_ssem.at[way, t % RING], recv_sem=z_rsem.at[way, t % ZRING],
            device_id=(zright, zleft)[way], device_id_type=MESH,
        )

    def v_copy(stage, peer):
        return pltpu.make_async_remote_copy(
            src_ref=vsend.at[stage], dst_ref=vrecv.at[stage],
            send_sem=v_ssem.at[stage], recv_sem=v_rsem.at[stage],
            device_id=peer, device_id_type=MESH,
        )

    def lend_copy(e):
        return pltpu.make_async_remote_copy(
            src_ref=lent.at[e], dst_ref=lent.at[e],
            send_sem=l_ssem.at[e], recv_sem=l_rsem.at[e],
            device_id=xnb, device_id_type=MESH,
        )

    def give(which, t, depth, peer, count=None):
        @pl.when(t + depth < (mine if count is None else count))
        def _():
            pl.semaphore_signal(credit.at[which], inc=1, device_id=peer, device_id_type=MESH)

    def take(which, t, depth):
        @pl.when(t >= depth)
        def _():
            pl.semaphore_wait(credit.at[which], 1)

    def out_parts(p, src, act):
        @pl.when(p < lo_fc1)
        def _():
            row = (p // (width // 128)) * (2 * SLOT_ROWS)
            cols = aligned((p % (width // 128)) * 128, 128)
            for i in range(2):
                rows_of = pl.ds(pl.multiple_of(row + i * SLOT_ROWS, SLOT_ROWS), SLOT_ROWS)
                act(src.at[:, i * 128 : (i + 1) * 128], g_fc2.at[rows_of, cols], i)

        for lo, count, ref in ((lo_fc1, n_fc1, g_fc1), (lo_proj, n_proj, g_proj), (lo_qkv, n_qkv, g_qkv)):
            @pl.when((p >= lo) & (p < lo + count))
            def _():
                act(src, ref.at[:, aligned((p - lo) * SLOT_COLS, SLOT_COLS)], 0)

    def own_out(m, method):
        def act(src, dst, i):
            getattr(pltpu.make_async_copy(src, dst, o_sem.at[m % 4, i]), method)()

        out_parts(own_slot(m), ostage.at[m % 4], act)

    def lent_out(e, method):
        def act(src, dst, i):
            copy = pltpu.make_async_remote_copy(
                src_ref=src, dst_ref=dst,
                send_sem=l_ssem.at[LENT + 2 * e + i], recv_sem=l_rsem.at[LENT + 2 * e + i],
                device_id=xnb, device_id_type=MESH,
            )
            getattr(copy, method)()

        out_parts(e * LEND_EVERY + LEND_EVERY - 1, ostage.at[(lent_from + e) % 4], act)

    def out_start(m):
        @pl.when(jnp.logical_not(is_borrowed(m)))
        def _():
            own_out(m, "start")

        @pl.when(is_borrowed(m))
        def _():
            lent_out(m - lent_from, "start")

    def out_wait(m):
        @pl.when(jnp.logical_not(is_borrowed(m)))
        def _():
            own_out(m, "wait")

        @pl.when(is_borrowed(m))
        def _():
            lent_out(m - lent_from, "wait_send")

    def result_stay():
        return pltpu.make_async_copy(fout.at[aligned(yy * blk, blk)], results.at[yy], res_sem.at[0])

    def result_move():
        return pltpu.make_async_remote_copy(
            src_ref=fout.at[aligned((1 - yy) * blk, blk)], dst_ref=results.at[yy],
            send_sem=res_sem.at[1], recv_sem=res_sem.at[2],
            device_id=ynb, device_id_type=MESH,
        )

    def own_terms(q):
        @pl.when(q * 3 >= RING)
        def _():
            for i in range(3):
                core_copy(q * 3 + i - RING).wait_send()

        ring = (q % 2) * 3

        @pl.when(q < lo_fc1 // 3)
        def _():
            row = (q // 2) * (2 * SLOT_ROWS)
            cols = aligned((q % 2) * 384, 384)

            def share(dest, carry):
                got = dot_tn(act[:, aligned(dest * width + row, 2 * SLOT_ROWS)], dmb[:, cols])

                def place(ref, kind):
                    for i in range(3):
                        for half in range(2):
                            ref[ring + i, dest // 2, :, half * 128 : half * 128 + 128] = got[
                                half * SLOT_ROWS : (half + 1) * SLOT_ROWS, i * 128 : (i + 1) * 128
                            ].astype(kind)

                @pl.when(cc == dest % 2)
                def _():
                    place(ckeep, F32)

                @pl.when(cc != dest % 2)
                def _():
                    place(csend, BF)

                return carry

            lax.fori_loop(0, 4, share, 0)

        @pl.when(q >= lo_fc1 // 3)
        def _():
            cols = aligned((q * 3 - lo_fc1) * SLOT_COLS, 3 * SLOT_COLS)
            left = jnp.where(q * 3 < lo_proj, 0, jnp.where(q * 3 < lo_qkv, 1, 2))

            def share(side, carry):
                got = dot_tn(lhs[left, :, aligned(side * 2 * SLOT_ROWS, 2 * SLOT_ROWS)], rhs[:, cols])
                for core in range(2):
                    @pl.when(cc == core)
                    def _():
                        for i in range(3):
                            span = slice(i * SLOT_COLS, (i + 1) * SLOT_COLS)
                            mine, theirs = slice(0, SLOT_ROWS), slice(SLOT_ROWS, 2 * SLOT_ROWS)
                            if core:
                                mine, theirs = theirs, mine
                            ckeep[ring + i, side] = got[mine, span]
                            csend[ring + i, side] = got[theirs, span].astype(BF)

                return carry

            lax.fori_loop(0, 2, share, 0)

    def stage_own(t, carry):
        @pl.when(t % 3 == 0)
        def _():
            own_terms(t // 3)

        take(0, t, RING)
        core_copy(t).start()

        @pl.when(t == own_slot(vslot))
        def _():
            vsend[0, :, 0:width] = vec[...]
            vsend[0, :, width : width + 256] = dcf[...]
            v_copy(0, sib).start()

        return carry

    def stage_chip(p, carry):
        own = jnp.where(is_first, p, p - lent_before(p))
        borrowed = is_borrowed(p)
        at = own % RING
        away = 1 - yy
        t = place_of(p)
        keeps = jnp.logical_not(is_lent(p))

        @pl.when(jnp.logical_not(borrowed))
        def _():
            core_copy(own).wait_recv()

        @pl.when(keeps)
        def _():
            take(1, t, YRING)

            @pl.when(t >= YRING)
            def _():
                y_copy(t - YRING).wait_send()

            @pl.when(jnp.logical_not(borrowed))
            def _():
                ysend[t % YRING] = (ckeep[at, away] + crecv[at, away].astype(F32)).astype(BF)
                rown[t % OWN_RING] = (ckeep[at, yy] + crecv[at, yy].astype(F32)).astype(BF)

            @pl.when(borrowed)
            def _():
                lend_copy(p - lent_from).wait_recv()
                ysend[t % YRING] = lent[p - lent_from, away]
                rown[t % OWN_RING] = lent[p - lent_from, yy]

            y_copy(t).start()

            @pl.when(t == vslot)
            def _():
                v_copy(0, sib).wait()
                vsend[1] = vsend[0] + vrecv[0]
                v_copy(1, ynb).start()

        @pl.when(is_lent(p))
        def _():
            e = p // LEND_EVERY
            for side in range(2):
                lent[e, side] = (ckeep[at, side] + crecv[at, side].astype(F32)).astype(BF)
            lend_copy(e).start()

        @pl.when(jnp.logical_not(borrowed))
        def _():
            give(0, own, RING, sib, slots)

        return carry

    def stage_group(t, carry):
        y_copy(t).wait_recv()
        at = t % OWN_RING
        rown[at] = (rown[at].astype(F32) + yrecv[t % YRING].astype(F32)).astype(BF)
        give(1, t, YRING, ynb)

        @pl.when(t == vslot)
        def _():
            v_copy(1, ynb).wait()
            vsend[2] = vsend[1] + vrecv[1]

        return carry

    def stage_line(way, t, carry):
        has_before = (has_left, has_right)[way]
        has_after = (has_right, has_left)[way]
        behind = (zleft, zright)[way]
        ahead = (zright, zleft)[way]

        @pl.when(has_before)
        def _():
            z_copy(way, t).wait_recv()

        @pl.when(has_after)
        def _():
            take(2 + way, t, ZRING)

            @pl.when(t >= RING)
            def _():
                z_copy(way, t - RING).wait_send()

            @pl.when(has_before)
            def _():
                zsend[way, t % RING] = (
                    rown[t % OWN_RING].astype(F32) + zrecv[way, t % ZRING].astype(F32)
                ).astype(BF)

            @pl.when(jnp.logical_not(has_before))
            def _():
                zsend[way, t % RING] = rown[t % OWN_RING]

            z_copy(way, t).start()

        @pl.when(t == vslot)
        def _():
            @pl.when(has_before)
            def _():
                v_copy(2 + way, behind).wait_recv()

            @pl.when(has_after)
            def _():
                @pl.when(has_before)
                def _():
                    vsend[3 + way] = vsend[2] + vrecv[2 + way]

                @pl.when(jnp.logical_not(has_before))
                def _():
                    vsend[3 + way] = vsend[2]

                v_send(way, ahead).start()

        return carry

    def stage_whole(t, carry):
        at = t % ZRING
        own = rown[t % OWN_RING].astype(F32)

        @pl.when(t >= 4)
        def _():
            out_wait(t - 4)

        @pl.when(has_left & has_right)
        def _():
            ostage[t % 4] = (own + zrecv[0, at].astype(F32) + zrecv[1, at].astype(F32)).astype(BF)

        @pl.when(has_left & jnp.logical_not(has_right))
        def _():
            ostage[t % 4] = (own + zrecv[0, at].astype(F32)).astype(BF)

        @pl.when(has_right & jnp.logical_not(has_left))
        def _():
            ostage[t % 4] = (own + zrecv[1, at].astype(F32)).astype(BF)

        out_start(t)

        @pl.when(has_left)
        def _():
            give(2, t, ZRING, zleft)

        @pl.when(has_right)
        def _():
            give(3, t, ZRING, zright)

        return carry

    def v_send(way, peer):
        return pltpu.make_async_remote_copy(
            src_ref=vsend.at[3 + way], dst_ref=vrecv.at[2 + way],
            send_sem=v_ssem.at[2 + way], recv_sem=v_rsem.at[2 + way],
            device_id=peer, device_id_type=MESH,
        )

    @pl.when(is_second)
    def _():
        result_stay().start()
        result_move().start()
        own_block(cot).wait()
        swap_half(cot, 0).wait()
        swap_half(cot, 1).wait()

    def scale_back(j):
        part = aligned(j * blk, blk)

        @pl.when(is_first)
        def _():
            x_send(cot, dout, j, xb_ssem, xb_rsem).wait_recv()

        grad = cot[part, :].astype(F32)
        vec[3:4, :] += jnp.sum(grad * mb[part, :].astype(F32), 0, keepdims=True)
        low = (gains[0, 3:4, :] * grad).astype(BF)
        dmb[part, :] = low
        vec[9:10, :] += jnp.sum(low.astype(F32), 0, keepdims=True)

    def shrink_back(j):
        part = aligned(j * blk, blk)
        for t in range(ff // width):
            cols = slice(t * width, (t + 1) * width)
            back = dot_nt(dmb[part, :], wfc2[cols, :])
            low = (gp[part, cols].astype(F32) * back).astype(BF)
            du[part, cols] = low
            sums = jnp.sum(low.astype(F32), 0, keepdims=True)
            for i in range(width // 256):
                row = t * (width // 256) + i
                dcf[row : row + 1, :] += sums[:, i * 256 : (i + 1) * 256]

    def middle_back(j):
        part = aligned(j * blk, blk)
        grad_two = dot_nt(du[part, :], wfc1[...])
        hat, rstd = norm_stats(rb[part, :])
        vec[2:3, :] += jnp.sum(grad_two * hat, 0, keepdims=True)
        vec[8:9, :] += jnp.sum(grad_two, 0, keepdims=True)
        middle = cot[part, :].astype(F32) + norm_back(grad_two, hat, rstd, gains[0, 2:3, :])
        drb[part, :] = middle
        vec[1:2, :] += jnp.sum(middle * zb[part, :].astype(F32), 0, keepdims=True)
        low = (gains[0, 1:2, :] * middle).astype(BF)
        dzb[part, :] = low
        vec[7:8, :] += jnp.sum(low.astype(F32), 0, keepdims=True)

    def heads_back(j):
        part = aligned(j * blk, blk)
        grad_o = dot_nt(dzb[part, :], wproj[...]).astype(BF).astype(F32)
        for i in range(pairs):
            cols = slice(i * 128, (i + 1) * 128)
            pair = grad_o[:, cols]
            both = pair * ob[part, cols].astype(F32)
            inner_a = jnp.sum(jnp.where(lane_row < 64, both, 0.0), -1, keepdims=True)
            inner_b = jnp.sum(jnp.where(lane_row < 64, 0.0, both), -1, keepdims=True)
            extra_a = three_parts(-inner_a, lane_row, 68)
            extra_b = three_parts(-inner_b, lane_row, 4)
            doaug[2 * i, part, :] = jnp.where(lane_row < 64, pair, extra_a).astype(BF)
            doaug[2 * i + 1, part, :] = jnp.where(lane_row < 64, extra_b, pair).astype(BF)

    def dkv_copy(index, j):
        part = aligned(j * blk, blk)
        return pltpu.make_async_remote_copy(
            src_ref=dkv_send.at[index, part],
            dst_ref=dkv_recv.at[index, part],
            send_sem=dkv_ssem.at[index, j],
            recv_sem=dkv_rsem.at[index, j],
            device_id=sib,
            device_id_type=MESH,
        )

    def stacked(ref, pair, part):
        first, second = ref[2 * pair, part], ref[2 * pair + 1, part]
        return jnp.concatenate(
            [
                jnp.concatenate([first * first_row, first * second_row], 1),
                jnp.concatenate([second * second_row, second * first_row], 1),
            ],
            0,
        )

    def quadrant(pair, j, part):
        cols = aligned(pair * 128, 128)

        def key_block(ref):
            return jnp.concatenate(
                [ref[j * blk : (j + 1) * blk, cols], ref[rows + j * blk : rows + (j + 1) * blk, cols]], 0
            )

        feats = jnp.concatenate([segf[j * blk : (j + 1) * blk], segf[rows + j * blk : rows + (j + 1) * blk]], 0)
        keys, values = key_block(kall), key_block(vall)
        query, outer = stacked(qaug, pair, part), stacked(doaug, pair, part)
        prob = jnp.exp(dot_nt(jnp.concatenate([keys, feats], 1), query))
        diff = dot_nt(jnp.concatenate([values, feats], 1), outer)
        slope = (prob * diff).astype(BF)
        dq = dot_tn(slope, keys)
        count = dq.shape[0] // 2
        return (
            jnp.where(lane_row < 64, dq[:count], dq[count:]),
            dot_nn(slope, query[:, 0:128]),
            dot_nn(prob.astype(BF), outer[:, 0:128]),
        )

    def pair_spans(pair):
        return [aligned(third * width + pair * 128, 128) for third in range(3)]

    def attend_back_first(pair):
        dq_w, dk_w, dv_w = quadrant(pair, 0, slice(0, rows))
        dq_n, dk_n, dv_n = quadrant(pair, 1, slice(0, blk))
        q_cols, k_cols, v_cols = pair_spans(pair)
        dkv_send[pair, 0:blk] = dk_w[blk:].astype(BF)
        dkv_send[pairs + pair, 0:blk] = dv_w[blk:].astype(BF)
        dkv_copy(pair, 0).start()
        dkv_copy(pairs + pair, 0).start()
        dkv_send[pair, blk:] = dk_n[blk:].astype(BF)
        dkv_send[pairs + pair, blk:] = dv_n[blk:].astype(BF)
        dqkv[0:blk, q_cols] = ((dq_w[0:blk] + dq_n) * 0.125).astype(BF)
        dqkv[blk:, q_cols] = (dq_w[blk:] * 0.125).astype(BF)
        dqkv[0:blk, k_cols] = dk_w[0:blk].astype(BF)
        dqkv[blk:, k_cols] = dk_n[0:blk].astype(BF)
        dqkv[0:blk, v_cols] = dv_w[0:blk].astype(BF)
        dqkv[blk:, v_cols] = dv_n[0:blk].astype(BF)

    def attend_back_second(duo):
        found = [quadrant(2 * duo + i, 1, slice(blk, rows)) for i in range(2)]
        for i in range(2):
            second_sums(2 * duo + i, *found[i])

    def second_sums(pair, dq, dk, dv):
        q_cols, k_cols, v_cols = pair_spans(pair)
        for index, term in ((pair, dk), (pairs + pair, dv)):
            dkv_send[index, blk:] = (dkv_send[index, blk:].astype(F32) + term[blk:]).astype(BF)
            dkv_copy(index, 1).start()
        for cols, term in ((q_cols, dq * 0.125), (k_cols, dk[0:blk]), (v_cols, dv[0:blk])):
            dqkv[blk:, cols] = (dqkv[blk:, cols].astype(F32) + term).astype(BF)

    def finish_back(j):
        part = aligned(j * blk, blk)

        for index in range(2 * pairs):
            dkv_copy(index, j).wait()
        for index in range(2 * pairs):
            cols = slice(width + index * 128, width + (index + 1) * 128)
            dqkv[part, cols] = (dqkv[part, cols].astype(F32) + dkv_recv[index, part].astype(F32)).astype(BF)

        @pl.when(is_first & (j == 0))
        def _():
            x_send(hin, fout, 0, x_ssem, x_rsem).wait_send()
            x_half(0).wait_send()
            x_half(1).wait_send()

        @pl.when(is_second & (j == 0))
        def _():
            result_stay().wait()
            result_move().wait_send()

        vec[5:6, :] += jnp.sum(dqkv[part, 0:width].astype(F32), 0, keepdims=True)
        vec[6:7, :] += jnp.sum(dqkv[part, 2 * width : 3 * width].astype(F32), 0, keepdims=True)
        grad_one = dot_nt(dqkv[part, :], wqkv[...])
        hat, rstd = norm_stats(hin[part, :].astype(F32))
        vec[0:1, :] += jnp.sum(grad_one * hat, 0, keepdims=True)
        vec[4:5, :] += jnp.sum(grad_one, 0, keepdims=True)
        total = drb[part, :] + norm_back(grad_one, hat, rstd, gains[0, 0:1, :])
        dout[part, :] = total.astype(BF)

        @pl.when(is_second)
        def _():
            x_send(cot, dout, j, xb_ssem, xb_rsem).start()

    per_block = 4
    dense = chunks * per_block
    first_end = dense + pairs
    second_end = first_end + 1 + pairs // 2

    beside = 22

    def pieces_done(v):
        total = second_end + 1
        first = per_block + 1
        spread = jnp.minimum(first + (v * (total - first) + beside - 1) // beside, total)
        return jnp.where(v < 0, 0, jnp.where(is_first, spread, total))

    def advance(stage, lag, count, v, at=lambda m: m):
        def done(v):
            return jnp.minimum(jnp.maximum(v + 1 - lag, 0), count)

        lax.fori_loop(at(done(v - 1)), at(done(v)), stage, 0)

    late = jnp.maximum(grp, groups - 1 - grp)
    chip_lag, group_lag, hop_lag = 2, 4, 2
    visits = mine + group_lag + hop_lag * (groups - 1)

    def piece(w, carry):
        @pl.when(w < dense)
        def _():
            j, r = w // per_block, w % per_block

            @pl.when(r == 0)
            def _():
                scale_back(j)

            @pl.when(r == 1)
            def _():
                shrink_back(j)

            @pl.when(r == 2)
            def _():
                middle_back(j)

            @pl.when(r == 3)
            def _():
                heads_back(j)

        @pl.when((w >= dense) & (w < first_end))
        def _():
            attend_back_first(w - dense)

        @pl.when((w > first_end) & (w < second_end))
        def _():
            attend_back_second(w - first_end - 1)

        @pl.when((w == first_end) | (w == second_end))
        def _():
            finish_back((w - first_end) // (pairs // 2 + 1))

        return carry

    def visit(v, carry):
        lax.fori_loop(pieces_done(v - 1), pieces_done(v), piece, 0)
        advance(stage_own, 0, mine, v, own_slot)
        advance(stage_chip, chip_lag, mine, v, slot_at)
        advance(stage_group, group_lag, mine, v)
        for way in range(2):
            place = grp if way == 0 else groups - 1 - grp
            advance(functools.partial(stage_line, way), group_lag + hop_lag * place, mine, v)
        advance(stage_whole, group_lag + hop_lag * late, mine, v)

        @pl.when(is_first & (v == slots))
        def _():
            result_stay().start()
            result_move().start()

        return carry

    lax.fori_loop(0, visits, visit, 0)

    def drain(i, carry):
        y_copy(mine - YRING + i).wait_send()

        @pl.when(i < 4)
        def _():
            out_wait(mine - 4 + i)

        @pl.when(i < RING)
        def _():
            core_copy(slots - RING + i).wait_send()

            @pl.when(has_right)
            def _():
                z_copy(0, mine - RING + i).wait_send()

            @pl.when(has_left)
            def _():
                z_copy(1, mine - RING + i).wait_send()

        return carry

    lax.fori_loop(0, YRING, drain, 0)

    @pl.when(is_first)
    def _():
        for e in range(LENT):
            lend_copy(e).wait_send()
            lent_out(e, "wait_recv")

    @pl.when(has_right)
    def _():
        v_send(0, zright).wait_send()

    @pl.when(has_left)
    def _():
        v_send(1, zleft).wait_send()

    total = vsend[2]
    vec_out[...] = total

    @pl.when(has_left)
    def _():
        vec_out[...] = vec_out[...] + vrecv[2]

    @pl.when(has_right)
    def _():
        vec_out[...] = vec_out[...] + vrecv[3]

    @pl.when(is_first)
    def _():
        result_stay().wait()
        result_move().wait_send()

    @pl.when(is_second)
    def _():
        for j in range(chunks):
            x_send(cot, dout, j, xb_ssem, xb_rsem).wait_send()

    result_move().wait_recv()

HEADS = 12
HDIM = 64


def from_behind(block, axis, distance):
    devices = range(lax.axis_size(axis))
    route = [(i - distance, i) for i in devices if i - distance in devices]
    return lax.ppermute(block, axis, route)


def normalize(values, scale_vec, shift_vec):
    row_mean = jnp.mean(values, -1, keepdims=True)
    centered = values - row_mean
    variance = jnp.mean(centered * centered, -1, keepdims=True)
    return centered * lax.rsqrt(variance + 1e-06) * scale_vec + shift_vec


def gelu_exact(values):
    return jax.nn.gelu(values, approximate=False)


def back_dot(left, weight):
    return lax.dot_general(
        left, weight, (((1,), (1,)), ((), ())), preferred_element_type=jnp.float32
    )


def row_contract(left, right):
    return lax.dot_general(
        left, right, (((0,), (0,)), ((), ())), preferred_element_type=jnp.float32
    )


def masked_scores(query, keys_all, seg_row):
    row_count = query.shape[0]
    length = keys_all.shape[0]
    start = lax.axis_index("narrow") * row_count
    own_seg = lax.dynamic_slice_in_dim(seg_row, start, row_count)
    same = own_seg[:, None] == seg_row[None, :]
    raw = (
        jnp.einsum(
            "qhd,khd->hqk",
            query.reshape(row_count, HEADS, HDIM),
            keys_all.reshape(length, HEADS, HDIM),
            preferred_element_type=jnp.float32,
        )
        * 0.125
    )
    return jnp.where(same[None], raw, -1e30)


def forward_layer(inputs, seg_row, weights):
    qkv_w, proj_w, fc1_w, fc2_w, gain_rows, bias_rows, fc1_b = weights
    row_count, model_width = inputs.shape
    normed = normalize(inputs, gain_rows[0], bias_rows[0]).astype(jnp.bfloat16)
    qkv = jnp.dot(normed, qkv_w, preferred_element_type=jnp.float32)
    query = (qkv[:, :model_width] + bias_rows[1]).astype(jnp.bfloat16)
    key_rows = qkv[:, model_width : 2 * model_width].astype(jnp.bfloat16)
    value_rows = (qkv[:, 2 * model_width :] + bias_rows[2]).astype(jnp.bfloat16)
    keys_all, values_all = (
        lax.all_gather(key_rows, "narrow", axis=0, tiled=True),
        lax.all_gather(value_rows, "narrow", axis=0, tiled=True),
    )
    length = keys_all.shape[0]
    scores = masked_scores(query, keys_all, seg_row)
    peak = jnp.max(scores, -1, keepdims=True)
    log_total = peak + jnp.log(jnp.sum(jnp.exp(scores - peak), -1, keepdims=True))
    probs = jnp.exp(scores - log_total).astype(jnp.bfloat16)
    mixed = jnp.einsum(
        "hqk,khd->qhd",
        probs,
        values_all.reshape(length, HEADS, HDIM),
        preferred_element_type=jnp.float32,
    )
    attended = mixed.reshape(row_count, model_width).astype(jnp.bfloat16)
    branch = jnp.dot(attended, proj_w, preferred_element_type=jnp.float32) + bias_rows[3]
    middle = inputs + gain_rows[1] * branch
    normed_two = normalize(middle, gain_rows[2], bias_rows[4]).astype(jnp.bfloat16)
    hidden_pre = jnp.dot(normed_two, fc1_w, preferred_element_type=jnp.float32) + fc1_b
    activated = gelu_exact(hidden_pre).astype(jnp.bfloat16)
    mlp_out = jnp.dot(activated, fc2_w, preferred_element_type=jnp.float32) + bias_rows[5]
    output = middle + gain_rows[3] * mlp_out
    saved = (
        inputs,
        query,
        keys_all,
        values_all,
        log_total,
        attended,
        branch,
        middle,
        hidden_pre,
        mlp_out,
    )
    return (output, saved)


def backward_layer(grad_out, saved, seg_row, weights):
    qkv_w, proj_w, fc1_w, fc2_w, gain_rows, bias_rows, fc1_b = weights
    (
        inputs,
        query,
        keys_all,
        values_all,
        log_total,
        attended,
        branch,
        middle,
        hidden_pre,
        mlp_out,
    ) = saved
    row_count, model_width = inputs.shape
    length = keys_all.shape[0]
    scale_two = jnp.sum(grad_out * mlp_out, 0)
    mlp_grad = (gain_rows[3] * grad_out).astype(jnp.bfloat16)
    activated, gelu_pull = jax.vjp(gelu_exact, hidden_pre)
    grad_fc2 = row_contract(activated.astype(jnp.bfloat16), mlp_grad)
    shift_five = jnp.sum(mlp_grad.astype(jnp.float32), 0)
    pre_grad = gelu_pull(back_dot(mlp_grad, fc2_w))[0].astype(jnp.bfloat16)
    normed_two, norm_pull_two = jax.vjp(normalize, middle, gain_rows[2], bias_rows[4])
    grad_fc1 = row_contract(normed_two.astype(jnp.bfloat16), pre_grad)
    grad_fc1b = jnp.sum(pre_grad.astype(jnp.float32), 0)
    middle_part, gain_two, shift_four = norm_pull_two(back_dot(pre_grad, fc1_w))
    middle_grad = grad_out + middle_part
    scale_one = jnp.sum(middle_grad * branch, 0)
    branch_grad = (gain_rows[1] * middle_grad).astype(jnp.bfloat16)
    grad_proj = row_contract(attended, branch_grad)
    shift_three = jnp.sum(branch_grad.astype(jnp.float32), 0)
    heads_grad = back_dot(branch_grad, proj_w).astype(jnp.bfloat16).reshape(row_count, HEADS, HDIM)
    scores = masked_scores(query, keys_all, seg_row)
    probs = jnp.exp(scores - log_total)
    keys_heads = keys_all.reshape(length, HEADS, HDIM)
    prob_grad = jnp.einsum(
        "qhd,khd->hqk",
        heads_grad,
        values_all.reshape(length, HEADS, HDIM),
        preferred_element_type=jnp.float32,
    )
    inner = jnp.sum(probs * prob_grad, -1, keepdims=True)
    score_grad = (probs * (prob_grad - inner)).astype(jnp.bfloat16)
    query_grad = (
        (
            jnp.einsum("hqk,khd->qhd", score_grad, keys_heads, preferred_element_type=jnp.float32)
            * 0.125
        )
        .reshape(row_count, model_width)
        .astype(jnp.bfloat16)
    )
    key_part = (
        jnp.einsum(
            "hqk,qhd->khd",
            score_grad,
            query.reshape(row_count, HEADS, HDIM),
            preferred_element_type=jnp.float32,
        )
        * 0.125
    ).reshape(length, model_width)
    value_part = jnp.einsum(
        "hqk,qhd->khd", probs.astype(jnp.bfloat16), heads_grad, preferred_element_type=jnp.float32
    ).reshape(length, model_width)
    key_sum, value_sum = (
        lax.psum_scatter(
            key_part.astype(jnp.bfloat16), "narrow", scatter_dimension=0, tiled=True
        ).astype(jnp.float32),
        lax.psum_scatter(
            value_part.astype(jnp.bfloat16), "narrow", scatter_dimension=0, tiled=True
        ).astype(jnp.float32),
    )
    key_grad = key_sum.astype(jnp.bfloat16)
    value_grad = value_sum.astype(jnp.bfloat16)
    qkv_grad = jnp.concatenate([query_grad, key_grad, value_grad], 1)
    normed, norm_pull_one = jax.vjp(normalize, inputs, gain_rows[0], bias_rows[0])
    grad_qkv = row_contract(normed.astype(jnp.bfloat16), qkv_grad)
    input_part, gain_one, shift_zero = norm_pull_one(back_dot(qkv_grad, qkv_w))
    input_grad = middle_grad + input_part
    gain_grads = jnp.stack([gain_one, scale_one, gain_two, scale_two])
    shift_grads = jnp.stack(
        [
            shift_zero,
            jnp.sum(query_grad.astype(jnp.float32), 0),
            jnp.sum(value_grad.astype(jnp.float32), 0),
            shift_three,
            shift_four,
            shift_five,
        ]
    )
    return (
        input_grad,
        (grad_qkv, grad_proj, grad_fc1, grad_fc2, gain_grads, shift_grads, grad_fc1b),
    )


def general_body(
    boundary, segments, qkv_weight, proj_weight, fc1_weight, fc2_weight, gains, biases, fc1_bias
):
    weights = (
        qkv_weight[0],
        proj_weight[0],
        fc1_weight[0],
        fc2_weight[0],
        gains[0],
        biases[0],
        fc1_bias[0],
    )
    local_ends = boundary[0]
    micro_count = local_ends.shape[0]
    first_section = lax.axis_index("section") == 0
    arrived = jnp.zeros(local_ends.shape[1:], jnp.bfloat16)
    stored = []
    outputs = []
    for step_index in range(micro_count + 1):
        lower = min(step_index, micro_count - 1)
        upper = max(step_index - 1, 0)
        inputs = jnp.where(
            first_section, local_ends[lower].astype(jnp.float32), arrived.astype(jnp.float32)
        )
        seg_row = jnp.where(first_section, segments[lower], segments[upper])
        output, saved = forward_layer(inputs, seg_row, weights)
        stored.append((saved, seg_row))
        outputs.append(output)
        if step_index < micro_count:
            arrived = from_behind(output.astype(jnp.bfloat16), "section", 1)
    totals = tuple((jnp.zeros(w.shape, jnp.float32) for w in weights))
    returned = jnp.zeros(local_ends.shape[1:], jnp.bfloat16)
    input_grads = []
    for step_index in range(micro_count + 1):
        lower = min(step_index, micro_count - 1)
        upper = max(step_index - 1, 0)
        picked = jax.tree.map(
            lambda early, later: jnp.where(first_section, early, later),
            stored[upper],
            stored[lower + 1],
        )
        cotangent = jnp.where(
            first_section, returned.astype(jnp.float32), local_ends[lower].astype(jnp.float32)
        )
        is_valid = jnp.where(first_section, step_index >= 1, step_index < micro_count)
        cotangent = jnp.where(is_valid, cotangent, 0.0)
        grad_in, pieces = backward_layer(cotangent, picked[0], picked[1], weights)
        totals = tuple((acc + part for acc, part in zip(totals, pieces)))
        input_grads.append(grad_in)
        if step_index < micro_count:
            returned = from_behind(grad_in.astype(jnp.bfloat16), "section", -1)
    results = jnp.stack(
        [jnp.where(first_section, input_grads[j + 1], outputs[j + 1]) for j in range(micro_count)]
    )
    results = results.astype(jnp.bfloat16)
    within = (
        lax.psum_scatter(
            totals[0].astype(jnp.bfloat16), "narrow", scatter_dimension=0, tiled=True
        ).astype(jnp.float32),
        lax.psum_scatter(
            totals[1].astype(jnp.bfloat16), "narrow", scatter_dimension=0, tiled=True
        ).astype(jnp.float32),
        lax.psum_scatter(
            totals[2].astype(jnp.bfloat16), "narrow", scatter_dimension=0, tiled=True
        ).astype(jnp.float32),
        lax.psum_scatter(
            totals[3].astype(jnp.bfloat16), "narrow", scatter_dimension=0, tiled=True
        ).astype(jnp.float32),
        lax.psum_scatter(
            totals[4].astype(jnp.bfloat16), "narrow", scatter_dimension=1, tiled=True
        ).astype(jnp.float32),
        lax.psum_scatter(
            totals[5].astype(jnp.bfloat16), "narrow", scatter_dimension=1, tiled=True
        ).astype(jnp.float32),
        lax.psum_scatter(
            totals[6].astype(jnp.bfloat16), "narrow", scatter_dimension=0, tiled=True
        ).astype(jnp.float32),
    )
    final = (
        lax.psum(within[0].astype(jnp.bfloat16), "group").astype(jnp.float32),
        lax.psum(within[1].astype(jnp.bfloat16), "group").astype(jnp.float32),
        lax.psum(within[2].astype(jnp.bfloat16), "group").astype(jnp.float32),
        lax.psum(within[3].astype(jnp.bfloat16), "group").astype(jnp.float32),
        lax.psum(within[4].astype(jnp.bfloat16), "group").astype(jnp.float32),
        lax.psum(within[5].astype(jnp.bfloat16), "group").astype(jnp.float32),
        lax.psum(within[6].astype(jnp.bfloat16), "group").astype(jnp.float32),
    )
    return (
        results[None],
        final[0][None],
        final[1][None],
        final[2][None],
        final[3][None],
        final[4][None],
        final[5][None],
        final[6][None],
    )


def fused_body(
    groups, boundary, segments, qkv_weight, proj_weight, fc1_weight, fc2_weight, gains, biases, fc1_bias
):
    blk, width = boundary.shape[2:]
    rows, keys = 2 * blk, 4 * blk
    ff = fc1_weight.shape[2]
    heads = width // HDIM
    nar = lax.axis_index(NARROW)

    def bf(*shape):
        return pltpu.VMEM(shape, BF)

    def f32(*shape):
        return pltpu.VMEM(shape, F32)

    dma = pltpu.SemaphoreType.DMA
    slot = (SLOT_ROWS, SLOT_COLS)
    scratch = [
        bf(width, 3 * width), bf(width, width), bf(width, ff), bf(ff, width),
        bf(rows, width), bf(rows, width), bf(3, rows, width), bf(heads, rows, 128),
        bf(keys, width), bf(keys, width), bf(rows, width), f32(rows, width),
        bf(rows, ff + 4 * width), bf(rows, ff), bf(rows, width), bf(rows, width),
        bf(rows, width), bf(heads, rows, 128), bf(heads, rows, 128), bf(heads, rows, 128),
        bf(keys, 128), f32(RING, 2, *slot), bf(RING, 2, *slot), bf(RING, 2, *slot),
        bf(YRING, *slot), bf(YRING, *slot), bf(OWN_RING, *slot), bf(2, RING, *slot), bf(2, ZRING, *slot), bf(4, *slot),
        f32(16, width), f32(16, 256), f32(5, 16, width + 256), f32(4, 16, width + 256), bf(LENT, 2, *slot),
        dma((4,)), dma(()), dma((2, 2)), dma((2, 4)), dma((2, 4)), dma((3,)), dma((3,)), dma((2,)), dma((2,)),
        dma((heads, 2)), dma((heads, 2)), dma((3,)),
        dma((RING,)), dma((RING,)), dma((YRING,)), dma((YRING,)), dma((2, RING)), dma((2, ZRING)), dma((4, 2)),
        dma((4,)), dma((4,)), dma((3 * LENT,)), dma((3 * LENT,)), pltpu.SemaphoreType.REGULAR((4,)),
    ]
    hbm = pl.BlockSpec(memory_space=pl.ANY)
    vmem = pl.BlockSpec(memory_space=pltpu.VMEM)
    out = pl.pallas_call(
        functools.partial(kernel, groups),
        out_shape=(
            jax.ShapeDtypeStruct((2, blk, width), BF),
            jax.ShapeDtypeStruct((width // 4, 3 * width), BF),
            jax.ShapeDtypeStruct((width // 4, width), BF),
            jax.ShapeDtypeStruct((width // 4, ff), BF),
            jax.ShapeDtypeStruct((ff // 4, width), BF),
            jax.ShapeDtypeStruct((16, width + 256), F32),
        ),
        in_specs=[hbm, vmem, hbm, hbm, hbm, hbm, vmem, vmem, vmem],
        out_specs=(hbm, hbm, hbm, hbm, hbm, vmem),
        scratch_shapes=scratch,
        compiler_params=pltpu.CompilerParams(
            collective_id=0, has_side_effects=True, vmem_limit_bytes=63 * 2**20
        ),
        name="two_layers",
    )(boundary, segments, qkv_weight, proj_weight, fc1_weight, fc2_weight, gains, biases.reshape(1, -1), fc1_bias)
    results, qkv, proj, fc1, fc2, vecs = out
    return widen(results, qkv, proj, fc1, fc2, vecs)


def widen_kernel(results, qkv, proj, fc1, fc2, vecs, *outs):
    o_results, o_qkv, o_proj, o_fc1, o_fc2, o_gains, o_biases, o_fc1b = outs
    o_results[0] = results[...]
    for src, dst in ((qkv, o_qkv), (proj, o_proj), (fc1, o_fc1), (fc2, o_fc2)):
        dst[0] = src[...].astype(F32)

    @pl.when(pl.program_id(0) == 0)
    def _():
        nar = lax.axis_index(NARROW)
        share = o_gains.shape[2]
        parts = o_fc1b.shape[1] // 256
        for i in range(4):
            @pl.when(nar == i)
            def _():
                cols = slice(i * share, (i + 1) * share)
                o_gains[0] = vecs[0:4, cols]
                for row in range(6):
                    o_biases[row] = vecs[4 + row : 5 + row, cols]
                for part in range(parts):
                    o_fc1b[:, part * 256 : (part + 1) * 256] = vecs[
                        i * parts + part : i * parts + part + 1, 4 * share :
                    ]


def widen(results, qkv, proj, fc1, fc2, vecs):
    steps = 2

    def block(shape, lead):
        size = (shape[0] // steps,) + shape[1:]
        rest = (0,) * (len(shape) - 1)
        if lead:
            return pl.BlockSpec((1,) + size, lambda i: (0, i) + rest)
        return pl.BlockSpec(size, lambda i: (i,) + rest)

    def whole(shape):
        return pl.BlockSpec(shape, lambda i: (0,) * len(shape))

    halves, rows, width = results.shape
    flat = results.reshape(halves * rows, width)
    flats = (flat, qkv, proj, fc1, fc2)
    share = width // 4
    small = ((1, 4, share), (6, 1, share), (1, fc2.shape[0]))
    out = pl.pallas_call(
        widen_kernel,
        grid=(steps,),
        in_specs=[block(a.shape, False) for a in flats] + [whole(vecs.shape)],
        out_specs=[block(a.shape, True) for a in flats] + [whole(s) for s in small],
        out_shape=[jax.ShapeDtypeStruct((1,) + a.shape, BF if i == 0 else F32) for i, a in enumerate(flats)]
        + [jax.ShapeDtypeStruct(s, F32) for s in small],
        name="widen",
    )(*flats, vecs)
    return (
        out[0].reshape(1, halves, rows, width),
        *out[1:6],
        out[6].transpose(1, 0, 2),
        out[7],
    )


def solution(mesh):
    sections, groups, narrow = (mesh.shape[name] for name in (SECTION, GROUP, NARROW))
    placed = (
        P("section", "group", "narrow", None),
        P("group", None),
        P("section", None, None),
        P("section", None, None),
        P("section", None, None),
        P("section", None, None),
        P("section", None, None),
        P("section", None, None),
        P("section", None),
    )
    fused = sections == 2 and narrow == 4 and groups > 1
    body = functools.partial(fused_body, groups) if fused else general_body
    return jax.shard_map(
        body,
        mesh=mesh,
        in_specs=placed,
        out_specs=(
            P("section", "group", "narrow", None),
            P("section", "narrow", None),
            P("section", "narrow", None),
            P("section", "narrow", None),
            P("section", "narrow", None),
            P("section", None, "narrow"),
            P("section", None, "narrow"),
            P("section", "narrow"),
        ),
        check_vma=False,
    )
```

```python
import functools

import jax
import jax.numpy as jnp
from jax import lax
from jax.experimental import pallas as pl
from jax.experimental.pallas import tpu as pltpu
from jax.sharding import PartitionSpec as P

SECTION, GROUP, NARROW = "section", "group", "narrow"
HALVES = 2
BIG = 1e30
SLOT_ROWS = 192
SLOT_COLS = 256
RING = 6
ZRING = 8
YRING = 6
OWN_RING = 12
LENT = 6
LEND_EVERY = 5
BF = jnp.bfloat16
F32 = jnp.float32
MESH = pl.DeviceIdType.MESH


def dot_nn(left, right):
    return lax.dot_general(left, right, (((1,), (0,)), ((), ())), preferred_element_type=F32)


def dot_nt(left, right):
    return lax.dot_general(left, right, (((1,), (1,)), ((), ())), preferred_element_type=F32)


def dot_tn(left, right):
    return lax.dot_general(left, right, (((0,), (0,)), ((), ())), preferred_element_type=F32)


def aligned(start, size, unit=128):
    return pl.ds(pl.multiple_of(start, unit), size)


def norm_stats(values):
    mean = jnp.mean(values, -1, keepdims=True)
    centered = values - mean
    var = jnp.mean(centered * centered, -1, keepdims=True)
    rstd = lax.rsqrt(var + 1e-06)
    return centered * rstd, rstd


def norm_back(grad, hat, rstd, gain):
    scaled = grad * gain
    mean_one = jnp.mean(scaled, -1, keepdims=True)
    mean_two = jnp.mean(scaled * hat, -1, keepdims=True)
    return rstd * (scaled - mean_one - hat * mean_two)


def three_parts(column, lane, base):
    high = column.astype(BF).astype(F32)
    rest = column - high
    mid = rest.astype(BF).astype(F32)
    low = rest - mid
    return jnp.where(
        lane == base, high, jnp.where(lane == base + 1, mid, jnp.where(lane == base + 2, low, 0.0))
    )


def kernel(groups, *refs):
    (
        boundary, segments, wqkv_h, wproj_h, wfc1_h, wfc2_h, gains, biases, fc1b,
        results, g_qkv, g_proj, g_fc1, g_fc2, vec_out,
        wqkv, wproj, wfc1, wfc2,
        hin, cot, lhs, qaug, kall, vall, zb, rb, rhs, act, mb, fout,
        dmb, doaug, dkv_send, dkv_recv,
        segf, ckeep, csend, crecv, ysend, yrecv, rown, zsend, zrecv, ostage,
        vec, dcf, vsend, vrecv, lent,
        w_sem, b_sem, bx_sem, kv_ssem, kv_rsem, x_ssem, x_rsem, xb_ssem, xb_rsem,
        dkv_ssem, dkv_rsem, res_sem,
        c_ssem, c_rsem, y_ssem, y_rsem, z_ssem, z_rsem, o_sem,
        v_ssem, v_rsem, l_ssem, l_rsem, credit,
    ) = refs
    sec = lax.axis_index(SECTION)
    grp = lax.axis_index(GROUP)
    nar = lax.axis_index(NARROW)
    yy = nar // 2
    cc = nar % 2
    sib = (sec, grp, nar + 1 - 2 * cc)
    ynb = (sec, grp, (nar + 2) % 4)
    xnb = (1 - sec, grp, nar)
    zright = (sec, grp + 1, nar)
    zleft = (sec, grp - 1, nar)
    has_right = grp < groups - 1
    has_left = grp > 0
    is_first = sec == 0
    is_second = sec == 1

    blk = boundary.shape[2]
    rows = 2 * blk
    width = boundary.shape[3]
    ff = wfc1.shape[1]
    pairs = width // 128
    chunks = rows // blk

    n2, ob, n1 = lhs.at[0], lhs.at[1], lhs.at[2]
    gp = du = rhs.at[:, 0:ff]
    dzb, dqkv = rhs.at[:, ff : ff + width], rhs.at[:, ff + width :]
    drb, dout = rb, fout

    def bias(row):
        return biases[0:1, row * width : (row + 1) * width]

    weight_copies = [
        pltpu.make_async_copy(src.at[0], dst, w_sem.at[i])
        for i, (src, dst) in enumerate(
            ((wqkv_h, wqkv), (wproj_h, wproj), (wfc1_h, wfc1), (wfc2_h, wfc2))
        )
    ]
    for copy in weight_copies:
        copy.start()

    def own_block(dst):
        return pltpu.make_async_copy(boundary.at[0, yy], dst.at[aligned(yy * blk, blk)], b_sem)

    half_blk = blk // 2

    def swap_half(dst, half):
        return pltpu.make_async_remote_copy(
            src_ref=boundary.at[0, 1 - yy, pl.ds(half * half_blk, half_blk)],
            dst_ref=dst.at[aligned(yy * blk + half * half_blk, half_blk)],
            send_sem=bx_sem.at[0, half],
            recv_sem=bx_sem.at[1, half],
            device_id=ynb,
            device_id_type=MESH,
        )

    @pl.when(is_first)
    def _():
        own_block(hin).start()

    @pl.when(is_second)
    def _():
        own_block(cot).start()

    barrier = pltpu.get_barrier_semaphore()
    for peer in (sib, ynb, xnb):
        pl.semaphore_signal(barrier, inc=1, device_id=peer, device_id_type=MESH)

    @pl.when(has_right)
    def _():
        pl.semaphore_signal(barrier, inc=1, device_id=zright, device_id_type=MESH)

    @pl.when(has_left)
    def _():
        pl.semaphore_signal(barrier, inc=1, device_id=zleft, device_id_type=MESH)

    pl.semaphore_wait(barrier, 3 + has_right.astype(jnp.int32) + has_left.astype(jnp.int32))

    @pl.when(is_first)
    def _():
        swap_half(hin, 0).start()
        swap_half(hin, 1).start()

    @pl.when(is_second)
    def _():
        swap_half(cot, 0).start()
        swap_half(cot, 1).start()

    keys_seg = jnp.concatenate(
        [
            segments[pl.ds(yy, 1), aligned((half * 2 + core) * blk, blk)]
            for core in (cc, 1 - cc)
            for half in range(2)
        ],
        1,
    )
    feature = lax.rem(lax.broadcasted_iota(jnp.int32, (128, 1), 0), 64)
    hot = jnp.where(keys_seg == feature, 1.0, 0.0)
    ones = jnp.where((feature >= 4) & (feature < 7), 1.0, 0.0)
    segf[...] = jnp.where(feature < 4, hot, ones).T.astype(BF)
    vec[...] = jnp.zeros_like(vec)
    dcf[...] = jnp.zeros_like(dcf)

    lane_row = lax.broadcasted_iota(jnp.int32, (1, 128), 1)
    first_row = jnp.where(lane_row < 64, 1.0, 0.0).astype(BF)
    second_row = jnp.where(lane_row < 64, 0.0, 1.0).astype(BF)
    half_lane = lax.rem(lane_row, 64)
    penalty_row = jnp.where(half_lane < 4, BIG, 0.0)

    def x_send(dst, src, j, ssem, rsem):
        part = aligned(j * blk, blk)
        return pltpu.make_async_remote_copy(
            src_ref=src.at[part],
            dst_ref=dst.at[part],
            send_sem=ssem.at[j],
            recv_sem=rsem.at[j],
            device_id=xnb,
            device_id_type=MESH,
        )

    def x_half(half):
        part = aligned(half * half_blk, half_blk)
        return pltpu.make_async_remote_copy(
            src_ref=fout.at[part],
            dst_ref=hin.at[part],
            send_sem=x_ssem.at[half],
            recv_sem=x_rsem.at[half],
            device_id=xnb,
            device_id_type=MESH,
        )

    def kv_copy(which, part):
        ref = (kall, vall)[which]
        index = part.start // half_blk
        return pltpu.make_async_remote_copy(
            src_ref=ref.at[part],
            dst_ref=ref.at[aligned(part.start + rows, part.size)],
            send_sem=kv_ssem.at[which, index],
            recv_sem=kv_rsem.at[which, index],
            device_id=sib,
            device_id_type=MESH,
        )

    def project(part):
        size = part.size
        hat, _ = norm_stats(hin[part, :].astype(F32))
        normed = (hat * gains[0, 0:1, :] + bias(0)).astype(BF)
        n1[part, :] = normed
        kall[part, :] = dot_nn(normed, wqkv[:, width : 2 * width]).astype(BF)
        kv_copy(0, part).start()
        vall[part, :] = (dot_nn(normed, wqkv[:, 2 * width :]) + bias(2)).astype(BF)
        kv_copy(1, part).start()
        low = ((dot_nn(normed, wqkv[:, 0:width]) + bias(1)).astype(BF) * 0.125).astype(F32)
        penalty = (segf[part, :].astype(F32) - 1.0) * penalty_row
        for i in range(pairs):
            pair = low[:, i * 128 : (i + 1) * 128]
            qaug[2 * i, part, :] = jnp.where(lane_row < 64, pair, penalty).astype(BF)
            qaug[2 * i + 1, part, :] = jnp.where(lane_row < 64, penalty, pair).astype(BF)

    first_at = jnp.where(is_first, yy, 0) * blk

    @pl.when(is_first)
    def _():
        own_block(hin).wait()

    weight_copies[0].wait()

    def project_half(half, carry):
        @pl.when(is_first & (half >= 2))
        def _():
            swap_half(hin, half % 2).wait()

        @pl.when(is_second)
        def _():
            x_half(half).wait_recv()

        start = jnp.where(half < 2, first_at, blk - first_at) + (half % 2) * half_blk
        project(aligned(start, half_blk))
        return carry

    lax.fori_loop(0, 4, project_half, 0)
    for which in range(2):
        for half in range(4):
            kv_copy(which, aligned(half * half_blk, half_blk)).wait()

    def feed_forward(part):
        branch = dot_nn(ob[part, :], wproj[...]) + bias(3)
        zb[part, :] = branch.astype(BF)
        middle = hin[part, :].astype(F32) + gains[0, 1:2, :] * branch
        rb[part, :] = middle
        hat, _ = norm_stats(middle)
        n2[part, :] = (hat * gains[0, 2:3, :] + bias(4)).astype(BF)

        def expand(t, carry):
            cols = aligned(t * width, width)
            pre = dot_nn(n2[part, :], wfc1[:, cols]) + fc1b[0:1, cols]
            phi = 0.5 + 0.5 * lax.erf(pre * 0.7071067811865476)
            act[part, cols] = (pre * phi).astype(BF)
            slope = phi + pre * (jnp.exp(-0.5 * pre * pre) * 0.3989422804014327)
            gp[part, cols] = slope.astype(BF)
            return carry

        lax.fori_loop(0, ff // width, expand, 0, unroll=True)
        mlp = dot_nn(act[part, :], wfc2[...]) + bias(5)
        mb[part, :] = mlp.astype(BF)
        fout[part, :] = (rb[part, :] + gains[0, 3:4, :] * mlp).astype(BF)

    def forward_block(j, carry):
        part = aligned(j * blk, blk)

        feats = segf[...]
        own_pen = ((segf[part, :].astype(F32) - 1.0) * penalty_row).astype(BF) * first_row

        def attend(trio, carry):
            items = [trio * 3 + i for i in range(3)]
            spans = [aligned(pair * 128, 128) for pair in items]
            scores = []
            for pair, cols in zip(items, spans):
                query = jnp.concatenate(
                    [
                        jnp.concatenate([qaug[2 * pair, part, :] * first_row, own_pen], 1),
                        jnp.concatenate([qaug[2 * pair + 1, part, :] * second_row, own_pen], 1),
                    ],
                    0,
                )
                scores.append(dot_nt(query, jnp.concatenate([kall[:, cols], feats], 1)))
            for pair, cols, score in zip(items, spans, scores):
                peak = jnp.max(score, -1, keepdims=True)
                expo = jnp.exp(score - peak).astype(BF)
                mixed = dot_nn(expo, jnp.concatenate([vall[:, cols], feats], 1))
                total = mixed[:, 132:133]
                outs = mixed[:, 0:128] / total
                log_total = peak + jnp.log(total)
                for i in range(2):
                    base = 64 * (1 - i)
                    extra = three_parts(-log_total[i * blk : (i + 1) * blk], lane_row, base + 4)
                    query = qaug[2 * pair + i, part, :]
                    qaug[2 * pair + i, part, :] = (query.astype(F32) + extra).astype(BF)
                ob[part, cols] = jnp.where(lane_row < 64, outs[:blk], outs[blk:]).astype(BF)
            return carry

        lax.fori_loop(0, pairs // 3, attend, 0, unroll=True)

        @pl.when(j == 0)
        def _():
            for copy in weight_copies[1:]:
                copy.wait()

        @pl.when(is_first)
        def _():
            def feed_half(half, carry):
                feed_forward(aligned(half * half_blk, half_blk))
                x_half(half).start()
                return carry

            lax.fori_loop(2 * j, 2 * j + 2, feed_half, 0)

        @pl.when(is_second)
        def _():
            feed_forward(part)

        return carry

    lax.fori_loop(0, chunks, forward_block, 0)

    n_fc2 = 2 * (width // 128)
    n_fc1 = ff // SLOT_COLS
    n_proj = width // SLOT_COLS
    n_qkv = 3 * width // SLOT_COLS
    lo_fc1 = n_fc2
    lo_proj = lo_fc1 + n_fc1
    lo_qkv = lo_proj + n_proj
    slots = lo_qkv + n_qkv
    mine = jnp.where(is_first, slots - LENT, slots + LENT)
    vslot = slots - LENT - 6
    lent_from = slots - LENT - 1

    def slot_at(m):
        return jnp.where(is_first, m + jnp.minimum(m // (LEND_EVERY - 1), LENT), m)

    def place_of(p):
        return jnp.where(is_first, p - jnp.minimum(p // LEND_EVERY, LENT), p)

    def lent_before(m):
        return jnp.minimum(jnp.maximum(m - lent_from, 0), LENT)

    def own_slot(m):
        return jnp.where(is_first, slot_at(m), m - lent_before(m))

    def is_borrowed(m):
        return is_second & (m >= lent_from) & (m < lent_from + LENT)

    def is_lent(p):
        return is_first & (p % LEND_EVERY == LEND_EVERY - 1) & (p < LENT * LEND_EVERY)

    def core_copy(t):
        at = t % RING
        return pltpu.make_async_remote_copy(
            src_ref=csend.at[at], dst_ref=crecv.at[at],
            send_sem=c_ssem.at[at], recv_sem=c_rsem.at[at],
            device_id=sib, device_id_type=MESH,
        )

    def y_copy(t):
        at = t % YRING
        return pltpu.make_async_remote_copy(
            src_ref=ysend.at[at], dst_ref=yrecv.at[at],
            send_sem=y_ssem.at[at], recv_sem=y_rsem.at[at],
            device_id=ynb, device_id_type=MESH,
        )

    def z_copy(way, t):
        return pltpu.make_async_remote_copy(
            src_ref=zsend.at[way, t % RING], dst_ref=zrecv.at[way, t % ZRING],
            send_sem=z_ssem.at[way, t % RING], recv_sem=z_rsem.at[way, t % ZRING],
            device_id=(zright, zleft)[way], device_id_type=MESH,
        )

    def v_copy(stage, peer):
        return pltpu.make_async_remote_copy(
            src_ref=vsend.at[stage], dst_ref=vrecv.at[stage],
            send_sem=v_ssem.at[stage], recv_sem=v_rsem.at[stage],
            device_id=peer, device_id_type=MESH,
        )

    def lend_copy(e):
        return pltpu.make_async_remote_copy(
            src_ref=lent.at[e], dst_ref=lent.at[e],
            send_sem=l_ssem.at[e], recv_sem=l_rsem.at[e],
            device_id=xnb, device_id_type=MESH,
        )

    def give(which, t, depth, peer, count=None):
        @pl.when(t + depth < (mine if count is None else count))
        def _():
            pl.semaphore_signal(credit.at[which], inc=1, device_id=peer, device_id_type=MESH)

    def take(which, t, depth):
        @pl.when(t >= depth)
        def _():
            pl.semaphore_wait(credit.at[which], 1)

    def out_parts(p, src, act):
        @pl.when(p < lo_fc1)
        def _():
            row = (p // (width // 128)) * (2 * SLOT_ROWS)
            cols = aligned((p % (width // 128)) * 128, 128)
            for i in range(2):
                rows_of = pl.ds(pl.multiple_of(row + i * SLOT_ROWS, SLOT_ROWS), SLOT_ROWS)
                act(src.at[:, i * 128 : (i + 1) * 128], g_fc2.at[rows_of, cols], i)

        for lo, count, ref in ((lo_fc1, n_fc1, g_fc1), (lo_proj, n_proj, g_proj), (lo_qkv, n_qkv, g_qkv)):
            @pl.when((p >= lo) & (p < lo + count))
            def _():
                act(src, ref.at[:, aligned((p - lo) * SLOT_COLS, SLOT_COLS)], 0)

    def own_out(m, method):
        def act(src, dst, i):
            getattr(pltpu.make_async_copy(src, dst, o_sem.at[m % 4, i]), method)()

        out_parts(own_slot(m), ostage.at[m % 4], act)

    def lent_out(e, method):
        def act(src, dst, i):
            copy = pltpu.make_async_remote_copy(
                src_ref=src, dst_ref=dst,
                send_sem=l_ssem.at[LENT + 2 * e + i], recv_sem=l_rsem.at[LENT + 2 * e + i],
                device_id=xnb, device_id_type=MESH,
            )
            getattr(copy, method)()

        out_parts(e * LEND_EVERY + LEND_EVERY - 1, ostage.at[(lent_from + e) % 4], act)

    def out_start(m):
        @pl.when(jnp.logical_not(is_borrowed(m)))
        def _():
            own_out(m, "start")

        @pl.when(is_borrowed(m))
        def _():
            lent_out(m - lent_from, "start")

    def out_wait(m):
        @pl.when(jnp.logical_not(is_borrowed(m)))
        def _():
            own_out(m, "wait")

        @pl.when(is_borrowed(m))
        def _():
            lent_out(m - lent_from, "wait_send")

    def result_stay():
        return pltpu.make_async_copy(fout.at[aligned(yy * blk, blk)], results.at[yy], res_sem.at[0])

    def result_move():
        return pltpu.make_async_remote_copy(
            src_ref=fout.at[aligned((1 - yy) * blk, blk)], dst_ref=results.at[yy],
            send_sem=res_sem.at[1], recv_sem=res_sem.at[2],
            device_id=ynb, device_id_type=MESH,
        )

    def own_terms(q):
        @pl.when(q * 3 >= RING)
        def _():
            for i in range(3):
                core_copy(q * 3 + i - RING).wait_send()

        ring = (q % 2) * 3

        @pl.when(q < lo_fc1 // 3)
        def _():
            row = (q // 2) * (2 * SLOT_ROWS)
            cols = aligned((q % 2) * 384, 384)

            def share(dest, carry):
                got = dot_tn(act[:, aligned(dest * width + row, 2 * SLOT_ROWS)], dmb[:, cols])

                def place(ref, kind):
                    for i in range(3):
                        for half in range(2):
                            ref[ring + i, dest // 2, :, half * 128 : half * 128 + 128] = got[
                                half * SLOT_ROWS : (half + 1) * SLOT_ROWS, i * 128 : (i + 1) * 128
                            ].astype(kind)

                @pl.when(cc == dest % 2)
                def _():
                    place(ckeep, F32)

                @pl.when(cc != dest % 2)
                def _():
                    place(csend, BF)

                return carry

            lax.fori_loop(0, 4, share, 0)

        @pl.when(q >= lo_fc1 // 3)
        def _():
            cols = aligned((q * 3 - lo_fc1) * SLOT_COLS, 3 * SLOT_COLS)
            left = jnp.where(q * 3 < lo_proj, 0, jnp.where(q * 3 < lo_qkv, 1, 2))

            def share(side, carry):
                got = dot_tn(lhs[left, :, aligned(side * 2 * SLOT_ROWS, 2 * SLOT_ROWS)], rhs[:, cols])
                for core in range(2):
                    @pl.when(cc == core)
                    def _():
                        for i in range(3):
                            span = slice(i * SLOT_COLS, (i + 1) * SLOT_COLS)
                            mine, theirs = slice(0, SLOT_ROWS), slice(SLOT_ROWS, 2 * SLOT_ROWS)
                            if core:
                                mine, theirs = theirs, mine
                            ckeep[ring + i, side] = got[mine, span]
                            csend[ring + i, side] = got[theirs, span].astype(BF)

                return carry

            lax.fori_loop(0, 2, share, 0)

    def stage_own(t, carry):
        @pl.when(t % 3 == 0)
        def _():
            own_terms(t // 3)

        take(0, t, RING)
        core_copy(t).start()

        @pl.when(t == own_slot(vslot))
        def _():
            vsend[0, :, 0:width] = vec[...]
            vsend[0, :, width : width + 256] = dcf[...]
            v_copy(0, sib).start()

        return carry

    def stage_chip(p, carry):
        own = jnp.where(is_first, p, p - lent_before(p))
        borrowed = is_borrowed(p)
        at = own % RING
        away = 1 - yy
        t = place_of(p)
        keeps = jnp.logical_not(is_lent(p))

        @pl.when(jnp.logical_not(borrowed))
        def _():
            core_copy(own).wait_recv()

        @pl.when(keeps)
        def _():
            take(1, t, YRING)

            @pl.when(t >= YRING)
            def _():
                y_copy(t - YRING).wait_send()

            @pl.when(jnp.logical_not(borrowed))
            def _():
                ysend[t % YRING] = (ckeep[at, away] + crecv[at, away].astype(F32)).astype(BF)
                rown[t % OWN_RING] = (ckeep[at, yy] + crecv[at, yy].astype(F32)).astype(BF)

            @pl.when(borrowed)
            def _():
                lend_copy(p - lent_from).wait_recv()
                ysend[t % YRING] = lent[p - lent_from, away]
                rown[t % OWN_RING] = lent[p - lent_from, yy]

            y_copy(t).start()

            @pl.when(t == vslot)
            def _():
                v_copy(0, sib).wait()
                vsend[1] = vsend[0] + vrecv[0]
                v_copy(1, ynb).start()

        @pl.when(is_lent(p))
        def _():
            e = p // LEND_EVERY
            for side in range(2):
                lent[e, side] = (ckeep[at, side] + crecv[at, side].astype(F32)).astype(BF)
            lend_copy(e).start()

        @pl.when(jnp.logical_not(borrowed))
        def _():
            give(0, own, RING, sib, slots)

        return carry

    def stage_group(t, carry):
        y_copy(t).wait_recv()
        at = t % OWN_RING
        rown[at] = (rown[at].astype(F32) + yrecv[t % YRING].astype(F32)).astype(BF)
        give(1, t, YRING, ynb)

        @pl.when(t == vslot + 1)
        def _():
            v_copy(1, ynb).wait()
            vsend[2] = vsend[1] + vrecv[1]

        return carry

    def stage_line(way, t, carry):
        has_before = (has_left, has_right)[way]
        has_after = (has_right, has_left)[way]
        behind = (zleft, zright)[way]
        ahead = (zright, zleft)[way]

        @pl.when(has_before)
        def _():
            z_copy(way, t).wait_recv()

        @pl.when(has_after)
        def _():
            take(2 + way, t, ZRING)

            @pl.when(t >= RING)
            def _():
                z_copy(way, t - RING).wait_send()

            @pl.when(has_before)
            def _():
                zsend[way, t % RING] = (
                    rown[t % OWN_RING].astype(F32) + zrecv[way, t % ZRING].astype(F32)
                ).astype(BF)

            @pl.when(jnp.logical_not(has_before))
            def _():
                zsend[way, t % RING] = rown[t % OWN_RING]

            z_copy(way, t).start()

        @pl.when(t == vslot + 1 + (grp if way == 0 else groups - 1 - grp))
        def _():
            @pl.when(has_before)
            def _():
                v_copy(2 + way, behind).wait_recv()

            @pl.when(has_after)
            def _():
                @pl.when(has_before)
                def _():
                    vsend[3 + way] = vsend[2] + vrecv[2 + way]

                @pl.when(jnp.logical_not(has_before))
                def _():
                    vsend[3 + way] = vsend[2]

                v_send(way, ahead).start()

        return carry

    def stage_whole(t, carry):
        at = t % ZRING
        own = rown[t % OWN_RING].astype(F32)

        @pl.when(t >= 4)
        def _():
            out_wait(t - 4)

        @pl.when(has_left & has_right)
        def _():
            ostage[t % 4] = (own + zrecv[0, at].astype(F32) + zrecv[1, at].astype(F32)).astype(BF)

        @pl.when(has_left & jnp.logical_not(has_right))
        def _():
            ostage[t % 4] = (own + zrecv[0, at].astype(F32)).astype(BF)

        @pl.when(has_right & jnp.logical_not(has_left))
        def _():
            ostage[t % 4] = (own + zrecv[1, at].astype(F32)).astype(BF)

        out_start(t)

        @pl.when(has_left)
        def _():
            give(2, t, ZRING, zleft)

        @pl.when(has_right)
        def _():
            give(3, t, ZRING, zright)

        return carry

    def v_send(way, peer):
        return pltpu.make_async_remote_copy(
            src_ref=vsend.at[3 + way], dst_ref=vrecv.at[2 + way],
            send_sem=v_ssem.at[2 + way], recv_sem=v_rsem.at[2 + way],
            device_id=peer, device_id_type=MESH,
        )

    @pl.when(is_second)
    def _():
        result_stay().start()
        result_move().start()
        own_block(cot).wait()
        swap_half(cot, 0).wait()
        swap_half(cot, 1).wait()

    def scale_back(j):
        part = aligned(j * blk, blk)

        @pl.when(is_first)
        def _():
            x_send(cot, dout, j, xb_ssem, xb_rsem).wait_recv()

        grad = cot[part, :].astype(F32)
        vec[3:4, :] += jnp.sum(grad * mb[part, :].astype(F32), 0, keepdims=True)
        low = (gains[0, 3:4, :] * grad).astype(BF)
        dmb[part, :] = low
        vec[9:10, :] += jnp.sum(low.astype(F32), 0, keepdims=True)

    def shrink_back(j):
        part = aligned(j * blk, blk)
        for t in range(ff // width):
            cols = slice(t * width, (t + 1) * width)
            back = dot_nt(dmb[part, :], wfc2[cols, :])
            low = (gp[part, cols].astype(F32) * back).astype(BF)
            du[part, cols] = low
            sums = jnp.sum(low.astype(F32), 0, keepdims=True)
            for i in range(width // 256):
                row = t * (width // 256) + i
                dcf[row : row + 1, :] += sums[:, i * 256 : (i + 1) * 256]

    def middle_back(j):
        part = aligned(j * blk, blk)
        grad_two = dot_nt(du[part, :], wfc1[...])
        hat, rstd = norm_stats(rb[part, :])
        vec[2:3, :] += jnp.sum(grad_two * hat, 0, keepdims=True)
        vec[8:9, :] += jnp.sum(grad_two, 0, keepdims=True)
        middle = cot[part, :].astype(F32) + norm_back(grad_two, hat, rstd, gains[0, 2:3, :])
        drb[part, :] = middle
        vec[1:2, :] += jnp.sum(middle * zb[part, :].astype(F32), 0, keepdims=True)
        low = (gains[0, 1:2, :] * middle).astype(BF)
        dzb[part, :] = low
        vec[7:8, :] += jnp.sum(low.astype(F32), 0, keepdims=True)

    def heads_back(j):
        part = aligned(j * blk, blk)
        grad_o = dot_nt(dzb[part, :], wproj[...]).astype(BF).astype(F32)
        for i in range(pairs):
            cols = slice(i * 128, (i + 1) * 128)
            pair = grad_o[:, cols]
            both = pair * ob[part, cols].astype(F32)
            inner_a = jnp.sum(jnp.where(lane_row < 64, both, 0.0), -1, keepdims=True)
            inner_b = jnp.sum(jnp.where(lane_row < 64, 0.0, both), -1, keepdims=True)
            extra_a = three_parts(-inner_a, lane_row, 68)
            extra_b = three_parts(-inner_b, lane_row, 4)
            doaug[2 * i, part, :] = jnp.where(lane_row < 64, pair, extra_a).astype(BF)
            doaug[2 * i + 1, part, :] = jnp.where(lane_row < 64, extra_b, pair).astype(BF)

    def dkv_copy(index, j):
        part = aligned(j * blk, blk)
        return pltpu.make_async_remote_copy(
            src_ref=dkv_send.at[index, part],
            dst_ref=dkv_recv.at[index, part],
            send_sem=dkv_ssem.at[index, j],
            recv_sem=dkv_rsem.at[index, j],
            device_id=sib,
            device_id_type=MESH,
        )

    def stacked(ref, pair, part):
        first, second = ref[2 * pair, part], ref[2 * pair + 1, part]
        return jnp.concatenate(
            [
                jnp.concatenate([first * first_row, first * second_row], 1),
                jnp.concatenate([second * second_row, second * first_row], 1),
            ],
            0,
        )

    def quadrant(pair, j, part):
        cols = aligned(pair * 128, 128)

        def key_block(ref):
            return jnp.concatenate(
                [ref[j * blk : (j + 1) * blk, cols], ref[rows + j * blk : rows + (j + 1) * blk, cols]], 0
            )

        feats = jnp.concatenate([segf[j * blk : (j + 1) * blk], segf[rows + j * blk : rows + (j + 1) * blk]], 0)
        keys, values = key_block(kall), key_block(vall)
        query, outer = stacked(qaug, pair, part), stacked(doaug, pair, part)
        prob = jnp.exp(dot_nt(jnp.concatenate([keys, feats], 1), query))
        diff = dot_nt(jnp.concatenate([values, feats], 1), outer)
        slope = (prob * diff).astype(BF)
        dq = dot_tn(slope, keys)
        count = dq.shape[0] // 2
        return (
            jnp.where(lane_row < 64, dq[:count], dq[count:]),
            dot_nn(slope, query[:, 0:128]),
            dot_nn(prob.astype(BF), outer[:, 0:128]),
        )

    def pair_spans(pair):
        return [aligned(third * width + pair * 128, 128) for third in range(3)]

    def attend_back_first(pair):
        dq_w, dk_w, dv_w = quadrant(pair, 0, slice(0, rows))
        dq_n, dk_n, dv_n = quadrant(pair, 1, slice(0, blk))
        q_cols, k_cols, v_cols = pair_spans(pair)
        dkv_send[pair, 0:blk] = dk_w[blk:].astype(BF)
        dkv_send[pairs + pair, 0:blk] = dv_w[blk:].astype(BF)
        dkv_copy(pair, 0).start()
        dkv_copy(pairs + pair, 0).start()
        dkv_send[pair, blk:] = dk_n[blk:].astype(BF)
        dkv_send[pairs + pair, blk:] = dv_n[blk:].astype(BF)
        dqkv[0:blk, q_cols] = ((dq_w[0:blk] + dq_n) * 0.125).astype(BF)
        dqkv[blk:, q_cols] = (dq_w[blk:] * 0.125).astype(BF)
        dqkv[0:blk, k_cols] = dk_w[0:blk].astype(BF)
        dqkv[blk:, k_cols] = dk_n[0:blk].astype(BF)
        dqkv[0:blk, v_cols] = dv_w[0:blk].astype(BF)
        dqkv[blk:, v_cols] = dv_n[0:blk].astype(BF)

    def attend_back_second(duo):
        found = [quadrant(2 * duo + i, 1, slice(blk, rows)) for i in range(2)]
        for i in range(2):
            second_sums(2 * duo + i, *found[i])

    def second_sums(pair, dq, dk, dv):
        q_cols, k_cols, v_cols = pair_spans(pair)
        for index, term in ((pair, dk), (pairs + pair, dv)):
            dkv_send[index, blk:] = (dkv_send[index, blk:].astype(F32) + term[blk:]).astype(BF)
            dkv_copy(index, 1).start()
        for cols, term in ((q_cols, dq * 0.125), (k_cols, dk[0:blk]), (v_cols, dv[0:blk])):
            dqkv[blk:, cols] = (dqkv[blk:, cols].astype(F32) + term).astype(BF)

    def finish_back(j):
        part = aligned(j * blk, blk)

        for index in range(2 * pairs):
            dkv_copy(index, j).wait()
        for index in range(2 * pairs):
            cols = slice(width + index * 128, width + (index + 1) * 128)
            dqkv[part, cols] = (dqkv[part, cols].astype(F32) + dkv_recv[index, part].astype(F32)).astype(BF)

        @pl.when(is_first & (j == 0))
        def _():
            for half in range(4):
                x_half(half).wait_send()

        @pl.when(is_second & (j == 0))
        def _():
            result_stay().wait()
            result_move().wait_send()

        grad_one = dot_nt(dqkv[part, :], wqkv[...])
        hat, rstd = norm_stats(hin[part, :].astype(F32))
        total = drb[part, :] + norm_back(grad_one, hat, rstd, gains[0, 0:1, :])
        dout[part, :] = total.astype(BF)

        @pl.when(is_second)
        def _():
            x_send(cot, dout, j, xb_ssem, xb_rsem).start()

        vec[0:1, :] += jnp.sum(grad_one * hat, 0, keepdims=True)
        vec[4:5, :] += jnp.sum(grad_one, 0, keepdims=True)
        vec[5:6, :] += jnp.sum(dqkv[part, 0:width].astype(F32), 0, keepdims=True)
        vec[6:7, :] += jnp.sum(dqkv[part, 2 * width : 3 * width].astype(F32), 0, keepdims=True)

    per_block = 4
    dense = chunks * per_block
    first_end = dense + pairs
    second_end = first_end + 1 + pairs // 2

    beside = 22

    def pieces_done(v):
        total = second_end + 1
        first = per_block + 1
        spread = jnp.minimum(first + (v * (total - first) + beside - 1) // beside, total)
        return jnp.where(v < 0, 0, jnp.where(is_first, spread, total))

    def advance(stage, lag, count, v, at=lambda m: m):
        def done(v):
            return jnp.minimum(jnp.maximum(v + 1 - lag, 0), count)

        lax.fori_loop(at(done(v - 1)), at(done(v)), stage, 0)

    late = jnp.maximum(grp, groups - 1 - grp)
    chip_lag, group_lag, hop_lag = 2, 4, 2
    visits = mine + group_lag + hop_lag * (groups - 1)

    def piece(w, carry):
        @pl.when(w < dense)
        def _():
            j, r = w // per_block, w % per_block

            @pl.when(r == 0)
            def _():
                scale_back(j)

            @pl.when(r == 1)
            def _():
                shrink_back(j)

            @pl.when(r == 2)
            def _():
                middle_back(j)

            @pl.when(r == 3)
            def _():
                heads_back(j)

        @pl.when((w >= dense) & (w < first_end))
        def _():
            attend_back_first(w - dense)

        @pl.when((w > first_end) & (w < second_end))
        def _():
            attend_back_second(w - first_end - 1)

        @pl.when((w == first_end) | (w == second_end))
        def _():
            finish_back((w - first_end) // (pairs // 2 + 1))

        return carry

    def visit(v, carry):
        lax.fori_loop(pieces_done(v - 1), pieces_done(v), piece, 0)
        advance(stage_own, 0, mine, v, own_slot)
        advance(stage_chip, chip_lag, mine, v, slot_at)
        advance(stage_group, group_lag, mine, v)
        for way in range(2):
            place = grp if way == 0 else groups - 1 - grp
            advance(functools.partial(stage_line, way), group_lag + hop_lag * place, mine, v)
        advance(stage_whole, group_lag + hop_lag * late, mine, v)

        @pl.when(is_first & (v == mine + 1))
        def _():
            result_stay().start()
            result_move().start()

        return carry

    lax.fori_loop(0, visits, visit, 0)

    def drain(i, carry):
        y_copy(mine - YRING + i).wait_send()

        @pl.when(i < 4)
        def _():
            out_wait(mine - 4 + i)

        @pl.when(i < RING)
        def _():
            core_copy(slots - RING + i).wait_send()

            @pl.when(has_right)
            def _():
                z_copy(0, mine - RING + i).wait_send()

            @pl.when(has_left)
            def _():
                z_copy(1, mine - RING + i).wait_send()

        return carry

    lax.fori_loop(0, YRING, drain, 0)

    @pl.when(is_first)
    def _():
        for e in range(LENT):
            lend_copy(e).wait_send()
            lent_out(e, "wait_recv")

    @pl.when(has_right)
    def _():
        v_send(0, zright).wait_send()

    @pl.when(has_left)
    def _():
        v_send(1, zleft).wait_send()

    total = vsend[2]
    vec_out[...] = total

    @pl.when(has_left)
    def _():
        vec_out[...] = vec_out[...] + vrecv[2]

    @pl.when(has_right)
    def _():
        vec_out[...] = vec_out[...] + vrecv[3]

    @pl.when(is_first)
    def _():
        result_stay().wait()
        result_move().wait_send()

    @pl.when(is_second)
    def _():
        for j in range(chunks):
            x_send(cot, dout, j, xb_ssem, xb_rsem).wait_send()

    result_move().wait_recv()

HEADS = 12
HDIM = 64


def from_behind(block, axis, distance):
    devices = range(lax.axis_size(axis))
    route = [(i - distance, i) for i in devices if i - distance in devices]
    return lax.ppermute(block, axis, route)


def normalize(values, scale_vec, shift_vec):
    row_mean = jnp.mean(values, -1, keepdims=True)
    centered = values - row_mean
    variance = jnp.mean(centered * centered, -1, keepdims=True)
    return centered * lax.rsqrt(variance + 1e-06) * scale_vec + shift_vec


def gelu_exact(values):
    return jax.nn.gelu(values, approximate=False)


def back_dot(left, weight):
    return lax.dot_general(
        left, weight, (((1,), (1,)), ((), ())), preferred_element_type=jnp.float32
    )


def row_contract(left, right):
    return lax.dot_general(
        left, right, (((0,), (0,)), ((), ())), preferred_element_type=jnp.float32
    )


def masked_scores(query, keys_all, seg_row):
    row_count = query.shape[0]
    length = keys_all.shape[0]
    start = lax.axis_index("narrow") * row_count
    own_seg = lax.dynamic_slice_in_dim(seg_row, start, row_count)
    same = own_seg[:, None] == seg_row[None, :]
    raw = (
        jnp.einsum(
            "qhd,khd->hqk",
            query.reshape(row_count, HEADS, HDIM),
            keys_all.reshape(length, HEADS, HDIM),
            preferred_element_type=jnp.float32,
        )
        * 0.125
    )
    return jnp.where(same[None], raw, -1e30)


def forward_layer(inputs, seg_row, weights):
    qkv_w, proj_w, fc1_w, fc2_w, gain_rows, bias_rows, fc1_b = weights
    row_count, model_width = inputs.shape
    normed = normalize(inputs, gain_rows[0], bias_rows[0]).astype(jnp.bfloat16)
    qkv = jnp.dot(normed, qkv_w, preferred_element_type=jnp.float32)
    query = (qkv[:, :model_width] + bias_rows[1]).astype(jnp.bfloat16)
    key_rows = qkv[:, model_width : 2 * model_width].astype(jnp.bfloat16)
    value_rows = (qkv[:, 2 * model_width :] + bias_rows[2]).astype(jnp.bfloat16)
    keys_all, values_all = (
        lax.all_gather(key_rows, "narrow", axis=0, tiled=True),
        lax.all_gather(value_rows, "narrow", axis=0, tiled=True),
    )
    length = keys_all.shape[0]
    scores = masked_scores(query, keys_all, seg_row)
    peak = jnp.max(scores, -1, keepdims=True)
    log_total = peak + jnp.log(jnp.sum(jnp.exp(scores - peak), -1, keepdims=True))
    probs = jnp.exp(scores - log_total).astype(jnp.bfloat16)
    mixed = jnp.einsum(
        "hqk,khd->qhd",
        probs,
        values_all.reshape(length, HEADS, HDIM),
        preferred_element_type=jnp.float32,
    )
    attended = mixed.reshape(row_count, model_width).astype(jnp.bfloat16)
    branch = jnp.dot(attended, proj_w, preferred_element_type=jnp.float32) + bias_rows[3]
    middle = inputs + gain_rows[1] * branch
    normed_two = normalize(middle, gain_rows[2], bias_rows[4]).astype(jnp.bfloat16)
    hidden_pre = jnp.dot(normed_two, fc1_w, preferred_element_type=jnp.float32) + fc1_b
    activated = gelu_exact(hidden_pre).astype(jnp.bfloat16)
    mlp_out = jnp.dot(activated, fc2_w, preferred_element_type=jnp.float32) + bias_rows[5]
    output = middle + gain_rows[3] * mlp_out
    saved = (
        inputs,
        query,
        keys_all,
        values_all,
        log_total,
        attended,
        branch,
        middle,
        hidden_pre,
        mlp_out,
    )
    return (output, saved)


def backward_layer(grad_out, saved, seg_row, weights):
    qkv_w, proj_w, fc1_w, fc2_w, gain_rows, bias_rows, fc1_b = weights
    (
        inputs,
        query,
        keys_all,
        values_all,
        log_total,
        attended,
        branch,
        middle,
        hidden_pre,
        mlp_out,
    ) = saved
    row_count, model_width = inputs.shape
    length = keys_all.shape[0]
    scale_two = jnp.sum(grad_out * mlp_out, 0)
    mlp_grad = (gain_rows[3] * grad_out).astype(jnp.bfloat16)
    activated, gelu_pull = jax.vjp(gelu_exact, hidden_pre)
    grad_fc2 = row_contract(activated.astype(jnp.bfloat16), mlp_grad)
    shift_five = jnp.sum(mlp_grad.astype(jnp.float32), 0)
    pre_grad = gelu_pull(back_dot(mlp_grad, fc2_w))[0].astype(jnp.bfloat16)
    normed_two, norm_pull_two = jax.vjp(normalize, middle, gain_rows[2], bias_rows[4])
    grad_fc1 = row_contract(normed_two.astype(jnp.bfloat16), pre_grad)
    grad_fc1b = jnp.sum(pre_grad.astype(jnp.float32), 0)
    middle_part, gain_two, shift_four = norm_pull_two(back_dot(pre_grad, fc1_w))
    middle_grad = grad_out + middle_part
    scale_one = jnp.sum(middle_grad * branch, 0)
    branch_grad = (gain_rows[1] * middle_grad).astype(jnp.bfloat16)
    grad_proj = row_contract(attended, branch_grad)
    shift_three = jnp.sum(branch_grad.astype(jnp.float32), 0)
    heads_grad = back_dot(branch_grad, proj_w).astype(jnp.bfloat16).reshape(row_count, HEADS, HDIM)
    scores = masked_scores(query, keys_all, seg_row)
    probs = jnp.exp(scores - log_total)
    keys_heads = keys_all.reshape(length, HEADS, HDIM)
    prob_grad = jnp.einsum(
        "qhd,khd->hqk",
        heads_grad,
        values_all.reshape(length, HEADS, HDIM),
        preferred_element_type=jnp.float32,
    )
    inner = jnp.sum(probs * prob_grad, -1, keepdims=True)
    score_grad = (probs * (prob_grad - inner)).astype(jnp.bfloat16)
    query_grad = (
        (
            jnp.einsum("hqk,khd->qhd", score_grad, keys_heads, preferred_element_type=jnp.float32)
            * 0.125
        )
        .reshape(row_count, model_width)
        .astype(jnp.bfloat16)
    )
    key_part = (
        jnp.einsum(
            "hqk,qhd->khd",
            score_grad,
            query.reshape(row_count, HEADS, HDIM),
            preferred_element_type=jnp.float32,
        )
        * 0.125
    ).reshape(length, model_width)
    value_part = jnp.einsum(
        "hqk,qhd->khd", probs.astype(jnp.bfloat16), heads_grad, preferred_element_type=jnp.float32
    ).reshape(length, model_width)
    key_sum, value_sum = (
        lax.psum_scatter(
            key_part.astype(jnp.bfloat16), "narrow", scatter_dimension=0, tiled=True
        ).astype(jnp.float32),
        lax.psum_scatter(
            value_part.astype(jnp.bfloat16), "narrow", scatter_dimension=0, tiled=True
        ).astype(jnp.float32),
    )
    key_grad = key_sum.astype(jnp.bfloat16)
    value_grad = value_sum.astype(jnp.bfloat16)
    qkv_grad = jnp.concatenate([query_grad, key_grad, value_grad], 1)
    normed, norm_pull_one = jax.vjp(normalize, inputs, gain_rows[0], bias_rows[0])
    grad_qkv = row_contract(normed.astype(jnp.bfloat16), qkv_grad)
    input_part, gain_one, shift_zero = norm_pull_one(back_dot(qkv_grad, qkv_w))
    input_grad = middle_grad + input_part
    gain_grads = jnp.stack([gain_one, scale_one, gain_two, scale_two])
    shift_grads = jnp.stack(
        [
            shift_zero,
            jnp.sum(query_grad.astype(jnp.float32), 0),
            jnp.sum(value_grad.astype(jnp.float32), 0),
            shift_three,
            shift_four,
            shift_five,
        ]
    )
    return (
        input_grad,
        (grad_qkv, grad_proj, grad_fc1, grad_fc2, gain_grads, shift_grads, grad_fc1b),
    )


def general_body(
    boundary, segments, qkv_weight, proj_weight, fc1_weight, fc2_weight, gains, biases, fc1_bias
):
    weights = (
        qkv_weight[0],
        proj_weight[0],
        fc1_weight[0],
        fc2_weight[0],
        gains[0],
        biases[0],
        fc1_bias[0],
    )
    local_ends = boundary[0]
    micro_count = local_ends.shape[0]
    first_section = lax.axis_index("section") == 0
    arrived = jnp.zeros(local_ends.shape[1:], jnp.bfloat16)
    stored = []
    outputs = []
    for step_index in range(micro_count + 1):
        lower = min(step_index, micro_count - 1)
        upper = max(step_index - 1, 0)
        inputs = jnp.where(
            first_section, local_ends[lower].astype(jnp.float32), arrived.astype(jnp.float32)
        )
        seg_row = jnp.where(first_section, segments[lower], segments[upper])
        output, saved = forward_layer(inputs, seg_row, weights)
        stored.append((saved, seg_row))
        outputs.append(output)
        if step_index < micro_count:
            arrived = from_behind(output.astype(jnp.bfloat16), "section", 1)
    totals = tuple((jnp.zeros(w.shape, jnp.float32) for w in weights))
    returned = jnp.zeros(local_ends.shape[1:], jnp.bfloat16)
    input_grads = []
    for step_index in range(micro_count + 1):
        lower = min(step_index, micro_count - 1)
        upper = max(step_index - 1, 0)
        picked = jax.tree.map(
            lambda early, later: jnp.where(first_section, early, later),
            stored[upper],
            stored[lower + 1],
        )
        cotangent = jnp.where(
            first_section, returned.astype(jnp.float32), local_ends[lower].astype(jnp.float32)
        )
        is_valid = jnp.where(first_section, step_index >= 1, step_index < micro_count)
        cotangent = jnp.where(is_valid, cotangent, 0.0)
        grad_in, pieces = backward_layer(cotangent, picked[0], picked[1], weights)
        totals = tuple((acc + part for acc, part in zip(totals, pieces)))
        input_grads.append(grad_in)
        if step_index < micro_count:
            returned = from_behind(grad_in.astype(jnp.bfloat16), "section", -1)
    results = jnp.stack(
        [jnp.where(first_section, input_grads[j + 1], outputs[j + 1]) for j in range(micro_count)]
    )
    results = results.astype(jnp.bfloat16)
    within = (
        lax.psum_scatter(
            totals[0].astype(jnp.bfloat16), "narrow", scatter_dimension=0, tiled=True
        ).astype(jnp.float32),
        lax.psum_scatter(
            totals[1].astype(jnp.bfloat16), "narrow", scatter_dimension=0, tiled=True
        ).astype(jnp.float32),
        lax.psum_scatter(
            totals[2].astype(jnp.bfloat16), "narrow", scatter_dimension=0, tiled=True
        ).astype(jnp.float32),
        lax.psum_scatter(
            totals[3].astype(jnp.bfloat16), "narrow", scatter_dimension=0, tiled=True
        ).astype(jnp.float32),
        lax.psum_scatter(
            totals[4].astype(jnp.bfloat16), "narrow", scatter_dimension=1, tiled=True
        ).astype(jnp.float32),
        lax.psum_scatter(
            totals[5].astype(jnp.bfloat16), "narrow", scatter_dimension=1, tiled=True
        ).astype(jnp.float32),
        lax.psum_scatter(
            totals[6].astype(jnp.bfloat16), "narrow", scatter_dimension=0, tiled=True
        ).astype(jnp.float32),
    )
    final = (
        lax.psum(within[0].astype(jnp.bfloat16), "group").astype(jnp.float32),
        lax.psum(within[1].astype(jnp.bfloat16), "group").astype(jnp.float32),
        lax.psum(within[2].astype(jnp.bfloat16), "group").astype(jnp.float32),
        lax.psum(within[3].astype(jnp.bfloat16), "group").astype(jnp.float32),
        lax.psum(within[4].astype(jnp.bfloat16), "group").astype(jnp.float32),
        lax.psum(within[5].astype(jnp.bfloat16), "group").astype(jnp.float32),
        lax.psum(within[6].astype(jnp.bfloat16), "group").astype(jnp.float32),
    )
    return (
        results[None],
        final[0][None],
        final[1][None],
        final[2][None],
        final[3][None],
        final[4][None],
        final[5][None],
        final[6][None],
    )


def fused_body(
    groups, boundary, segments, qkv_weight, proj_weight, fc1_weight, fc2_weight, gains, biases, fc1_bias
):
    blk, width = boundary.shape[2:]
    rows, keys = 2 * blk, 4 * blk
    ff = fc1_weight.shape[2]
    heads = width // HDIM
    nar = lax.axis_index(NARROW)

    def bf(*shape):
        return pltpu.VMEM(shape, BF)

    def f32(*shape):
        return pltpu.VMEM(shape, F32)

    dma = pltpu.SemaphoreType.DMA
    slot = (SLOT_ROWS, SLOT_COLS)
    scratch = [
        bf(width, 3 * width), bf(width, width), bf(width, ff), bf(ff, width),
        bf(rows, width), bf(rows, width), bf(3, rows, width), bf(heads, rows, 128),
        bf(keys, width), bf(keys, width), bf(rows, width), f32(rows, width),
        bf(rows, ff + 4 * width), bf(rows, ff), bf(rows, width), bf(rows, width),
        bf(rows, width), bf(heads, rows, 128), bf(heads, rows, 128), bf(heads, rows, 128),
        bf(keys, 128), f32(RING, 2, *slot), bf(RING, 2, *slot), bf(RING, 2, *slot),
        bf(YRING, *slot), bf(YRING, *slot), bf(OWN_RING, *slot), bf(2, RING, *slot), bf(2, ZRING, *slot), bf(4, *slot),
        f32(16, width), f32(16, 256), f32(5, 16, width + 256), f32(4, 16, width + 256), bf(LENT, 2, *slot),
        dma((4,)), dma(()), dma((2, 2)), dma((2, 4)), dma((2, 4)), dma((4,)), dma((4,)), dma((2,)), dma((2,)),
        dma((heads, 2)), dma((heads, 2)), dma((3,)),
        dma((RING,)), dma((RING,)), dma((YRING,)), dma((YRING,)), dma((2, RING)), dma((2, ZRING)), dma((4, 2)),
        dma((4,)), dma((4,)), dma((3 * LENT,)), dma((3 * LENT,)), pltpu.SemaphoreType.REGULAR((4,)),
    ]
    hbm = pl.BlockSpec(memory_space=pl.ANY)
    vmem = pl.BlockSpec(memory_space=pltpu.VMEM)
    out = pl.pallas_call(
        functools.partial(kernel, groups),
        out_shape=(
            jax.ShapeDtypeStruct((2, blk, width), BF),
            jax.ShapeDtypeStruct((width // 4, 3 * width), BF),
            jax.ShapeDtypeStruct((width // 4, width), BF),
            jax.ShapeDtypeStruct((width // 4, ff), BF),
            jax.ShapeDtypeStruct((ff // 4, width), BF),
            jax.ShapeDtypeStruct((16, width + 256), F32),
        ),
        in_specs=[hbm, vmem, hbm, hbm, hbm, hbm, vmem, vmem, vmem],
        out_specs=(hbm, hbm, hbm, hbm, hbm, vmem),
        scratch_shapes=scratch,
        compiler_params=pltpu.CompilerParams(
            collective_id=0, has_side_effects=True, vmem_limit_bytes=63 * 2**20
        ),
        name="two_layers",
    )(boundary, segments, qkv_weight, proj_weight, fc1_weight, fc2_weight, gains, biases.reshape(1, -1), fc1_bias)
    results, qkv, proj, fc1, fc2, vecs = out
    return widen(results, qkv, proj, fc1, fc2, vecs)


def widen_kernel(results, qkv, proj, fc1, fc2, vecs, *outs):
    o_results, o_qkv, o_proj, o_fc1, o_fc2, o_gains, o_biases, o_fc1b = outs
    o_results[0] = results[...]
    for src, dst in ((qkv, o_qkv), (proj, o_proj), (fc1, o_fc1), (fc2, o_fc2)):
        dst[0] = src[...].astype(F32)

    @pl.when(pl.program_id(0) == 0)
    def _():
        nar = lax.axis_index(NARROW)
        share = o_gains.shape[2]
        parts = o_fc1b.shape[1] // 256
        for i in range(4):
            @pl.when(nar == i)
            def _():
                cols = slice(i * share, (i + 1) * share)
                o_gains[0] = vecs[0:4, cols]
                for row in range(6):
                    o_biases[row] = vecs[4 + row : 5 + row, cols]
                for part in range(parts):
                    o_fc1b[:, part * 256 : (part + 1) * 256] = vecs[
                        i * parts + part : i * parts + part + 1, 4 * share :
                    ]


def widen(results, qkv, proj, fc1, fc2, vecs):
    steps = 2

    def block(shape, lead):
        size = (shape[0] // steps,) + shape[1:]
        rest = (0,) * (len(shape) - 1)
        if lead:
            return pl.BlockSpec((1,) + size, lambda i: (0, i) + rest)
        return pl.BlockSpec(size, lambda i: (i,) + rest)

    def whole(shape):
        return pl.BlockSpec(shape, lambda i: (0,) * len(shape))

    halves, rows, width = results.shape
    flat = results.reshape(halves * rows, width)
    flats = (flat, qkv, proj, fc1, fc2)
    share = width // 4
    small = ((1, 4, share), (6, 1, share), (1, fc2.shape[0]))
    out = pl.pallas_call(
        widen_kernel,
        grid=(steps,),
        in_specs=[block(a.shape, False) for a in flats] + [whole(vecs.shape)],
        out_specs=[block(a.shape, True) for a in flats] + [whole(s) for s in small],
        out_shape=[jax.ShapeDtypeStruct((1,) + a.shape, BF if i == 0 else F32) for i, a in enumerate(flats)]
        + [jax.ShapeDtypeStruct(s, F32) for s in small],
        name="widen",
    )(*flats, vecs)
    return (
        out[0].reshape(1, halves, rows, width),
        *out[1:6],
        out[6].transpose(1, 0, 2),
        out[7],
    )


def solution(mesh):
    sections, groups, narrow = (mesh.shape[name] for name in (SECTION, GROUP, NARROW))
    placed = (
        P("section", "group", "narrow", None),
        P("group", None),
        P("section", None, None),
        P("section", None, None),
        P("section", None, None),
        P("section", None, None),
        P("section", None, None),
        P("section", None, None),
        P("section", None),
    )
    fused = sections == 2 and narrow == 4 and groups > 1
    body = functools.partial(fused_body, groups) if fused else general_body
    return jax.shard_map(
        body,
        mesh=mesh,
        in_specs=placed,
        out_specs=(
            P("section", "group", "narrow", None),
            P("section", "narrow", None),
            P("section", "narrow", None),
            P("section", "narrow", None),
            P("section", "narrow", None),
            P("section", None, "narrow"),
            P("section", None, "narrow"),
            P("section", "narrow"),
        ),
        check_vma=False,
    )
```

```python
import functools

import jax
import jax.numpy as jnp
from jax import lax
from jax.experimental import pallas as pl
from jax.experimental.pallas import tpu as pltpu
from jax.sharding import PartitionSpec as P

SECTION, GROUP, NARROW = "section", "group", "narrow"
HALVES = 2
BIG = 1e30
SLOT_ROWS = 192
SLOT_COLS = 256
RING = 6
ZRING = 8
YRING = 6
OWN_RING = 12
LENT = 6
LEND_EVERY = 5
BF = jnp.bfloat16
F32 = jnp.float32
MESH = pl.DeviceIdType.MESH


def dot_nn(left, right):
    return lax.dot_general(left, right, (((1,), (0,)), ((), ())), preferred_element_type=F32)


def dot_nt(left, right):
    return lax.dot_general(left, right, (((1,), (1,)), ((), ())), preferred_element_type=F32)


def dot_tn(left, right):
    return lax.dot_general(left, right, (((0,), (0,)), ((), ())), preferred_element_type=F32)


def aligned(start, size, unit=128):
    return pl.ds(pl.multiple_of(start, unit), size)


def norm_stats(values):
    mean = jnp.mean(values, -1, keepdims=True)
    centered = values - mean
    var = jnp.mean(centered * centered, -1, keepdims=True)
    rstd = lax.rsqrt(var + 1e-06)
    return centered * rstd, rstd


def norm_back(grad, hat, rstd, gain):
    scaled = grad * gain
    mean_one = jnp.mean(scaled, -1, keepdims=True)
    mean_two = jnp.mean(scaled * hat, -1, keepdims=True)
    return rstd * (scaled - mean_one - hat * mean_two)


def three_parts(column, lane, base):
    high = column.astype(BF).astype(F32)
    rest = column - high
    mid = rest.astype(BF).astype(F32)
    low = rest - mid
    return jnp.where(
        lane == base, high, jnp.where(lane == base + 1, mid, jnp.where(lane == base + 2, low, 0.0))
    )


def kernel(groups, *refs):
    (
        boundary, segments, wqkv_h, wproj_h, wfc1_h, wfc2_h, gains, biases, fc1b,
        results, g_qkv, g_proj, g_fc1, g_fc2, vec_out,
        wqkv, wproj, wfc1, wfc2,
        hin, cot, lhs, qaug, kall, vall, zb, rb, rhs, act, mb, fout,
        dmb, doaug, dkv_send, dkv_recv,
        segf, ckeep, csend, crecv, ysend, yrecv, rown, zsend, zrecv, ostage,
        vec, dcf, vsend, vrecv, lent,
        w_sem, b_sem, bx_sem, kv_ssem, kv_rsem, x_ssem, x_rsem, xb_ssem, xb_rsem,
        dkv_ssem, dkv_rsem, res_sem,
        c_ssem, c_rsem, y_ssem, y_rsem, z_ssem, z_rsem, o_sem,
        v_ssem, v_rsem, l_ssem, l_rsem, credit,
    ) = refs
    sec = lax.axis_index(SECTION)
    grp = lax.axis_index(GROUP)
    nar = lax.axis_index(NARROW)
    yy = nar // 2
    cc = nar % 2
    sib = (sec, grp, nar + 1 - 2 * cc)
    ynb = (sec, grp, (nar + 2) % 4)
    xnb = (1 - sec, grp, nar)
    zright = (sec, grp + 1, nar)
    zleft = (sec, grp - 1, nar)
    has_right = grp < groups - 1
    has_left = grp > 0
    is_first = sec == 0
    is_second = sec == 1

    blk = boundary.shape[2]
    rows = 2 * blk
    width = boundary.shape[3]
    ff = wfc1.shape[1]
    pairs = width // 128
    chunks = rows // blk

    n2, ob, n1 = lhs.at[0], lhs.at[1], lhs.at[2]
    gp = du = rhs.at[:, 0:ff]
    dzb, dqkv = rhs.at[:, ff : ff + width], rhs.at[:, ff + width :]
    drb, dout = rb, fout

    def bias(row):
        return biases[0:1, row * width : (row + 1) * width]

    weight_copies = [
        pltpu.make_async_copy(src.at[0], dst, w_sem.at[i])
        for i, (src, dst) in enumerate(
            ((wqkv_h, wqkv), (wproj_h, wproj), (wfc1_h, wfc1), (wfc2_h, wfc2))
        )
    ]
    for copy in weight_copies:
        copy.start()

    def own_block(dst):
        return pltpu.make_async_copy(boundary.at[0, yy], dst.at[aligned(yy * blk, blk)], b_sem)

    half_blk = blk // 2

    def swap_half(dst, half):
        return pltpu.make_async_remote_copy(
            src_ref=boundary.at[0, 1 - yy, pl.ds(half * half_blk, half_blk)],
            dst_ref=dst.at[aligned(yy * blk + half * half_blk, half_blk)],
            send_sem=bx_sem.at[0, half],
            recv_sem=bx_sem.at[1, half],
            device_id=ynb,
            device_id_type=MESH,
        )

    @pl.when(is_first)
    def _():
        own_block(hin).start()

    @pl.when(is_second)
    def _():
        own_block(cot).start()

    barrier = pltpu.get_barrier_semaphore()
    for peer in (sib, ynb, xnb):
        pl.semaphore_signal(barrier, inc=1, device_id=peer, device_id_type=MESH)

    @pl.when(has_right)
    def _():
        pl.semaphore_signal(barrier, inc=1, device_id=zright, device_id_type=MESH)

    @pl.when(has_left)
    def _():
        pl.semaphore_signal(barrier, inc=1, device_id=zleft, device_id_type=MESH)

    pl.semaphore_wait(barrier, 3 + has_right.astype(jnp.int32) + has_left.astype(jnp.int32))

    @pl.when(is_first)
    def _():
        swap_half(hin, 0).start()
        swap_half(hin, 1).start()

    @pl.when(is_second)
    def _():
        swap_half(cot, 0).start()
        swap_half(cot, 1).start()

    keys_seg = jnp.concatenate(
        [
            segments[pl.ds(yy, 1), aligned((half * 2 + core) * blk, blk)]
            for core in (cc, 1 - cc)
            for half in range(2)
        ],
        1,
    )
    feature = lax.rem(lax.broadcasted_iota(jnp.int32, (128, 1), 0), 64)
    hot = jnp.where(keys_seg == feature, 1.0, 0.0)
    ones = jnp.where((feature >= 4) & (feature < 7), 1.0, 0.0)
    segf[...] = jnp.where(feature < 4, hot, ones).T.astype(BF)
    vec[...] = jnp.zeros_like(vec)
    dcf[...] = jnp.zeros_like(dcf)

    lane_row = lax.broadcasted_iota(jnp.int32, (1, 128), 1)
    first_row = jnp.where(lane_row < 64, 1.0, 0.0).astype(BF)
    second_row = jnp.where(lane_row < 64, 0.0, 1.0).astype(BF)
    half_lane = lax.rem(lane_row, 64)
    penalty_row = jnp.where(half_lane < 4, BIG, 0.0)

    def x_send(dst, src, j, ssem, rsem):
        part = aligned(j * blk, blk)
        return pltpu.make_async_remote_copy(
            src_ref=src.at[part],
            dst_ref=dst.at[part],
            send_sem=ssem.at[j],
            recv_sem=rsem.at[j],
            device_id=xnb,
            device_id_type=MESH,
        )

    def x_half(half):
        part = aligned(half * half_blk, half_blk)
        return pltpu.make_async_remote_copy(
            src_ref=fout.at[part],
            dst_ref=hin.at[part],
            send_sem=x_ssem.at[half],
            recv_sem=x_rsem.at[half],
            device_id=xnb,
            device_id_type=MESH,
        )

    def kv_copy(which, part):
        ref = (kall, vall)[which]
        index = part.start // half_blk
        return pltpu.make_async_remote_copy(
            src_ref=ref.at[part],
            dst_ref=ref.at[aligned(part.start + rows, part.size)],
            send_sem=kv_ssem.at[which, index],
            recv_sem=kv_rsem.at[which, index],
            device_id=sib,
            device_id_type=MESH,
        )

    def project(part):
        size = part.size
        hat, _ = norm_stats(hin[part, :].astype(F32))
        normed = (hat * gains[0, 0:1, :] + bias(0)).astype(BF)
        n1[part, :] = normed
        kall[part, :] = dot_nn(normed, wqkv[:, width : 2 * width]).astype(BF)
        kv_copy(0, part).start()
        vall[part, :] = (dot_nn(normed, wqkv[:, 2 * width :]) + bias(2)).astype(BF)
        kv_copy(1, part).start()
        low = ((dot_nn(normed, wqkv[:, 0:width]) + bias(1)).astype(BF) * 0.125).astype(F32)
        penalty = (segf[part, :].astype(F32) - 1.0) * penalty_row
        for i in range(pairs):
            pair = low[:, i * 128 : (i + 1) * 128]
            qaug[2 * i, part, :] = jnp.where(lane_row < 64, pair, penalty).astype(BF)
            qaug[2 * i + 1, part, :] = jnp.where(lane_row < 64, penalty, pair).astype(BF)

    first_at = jnp.where(is_first, yy, 0) * blk

    @pl.when(is_first)
    def _():
        own_block(hin).wait()

    weight_copies[0].wait()

    def project_half(half, carry):
        @pl.when(is_first & (half >= 2))
        def _():
            swap_half(hin, half % 2).wait()

        @pl.when(is_second)
        def _():
            x_half(half).wait_recv()

        start = jnp.where(half < 2, first_at, blk - first_at) + (half % 2) * half_blk
        project(aligned(start, half_blk))
        return carry

    lax.fori_loop(0, 4, project_half, 0)
    for which in range(2):
        for half in range(4):
            kv_copy(which, aligned(half * half_blk, half_blk)).wait()

    def feed_forward(part):
        branch = dot_nn(ob[part, :], wproj[...]) + bias(3)
        zb[part, :] = branch.astype(BF)
        middle = hin[part, :].astype(F32) + gains[0, 1:2, :] * branch
        rb[part, :] = middle
        hat, _ = norm_stats(middle)
        n2[part, :] = (hat * gains[0, 2:3, :] + bias(4)).astype(BF)

        def expand(t, carry):
            cols = aligned(t * width, width)
            pre = dot_nn(n2[part, :], wfc1[:, cols]) + fc1b[0:1, cols]
            phi = 0.5 + 0.5 * lax.erf(pre * 0.7071067811865476)
            act[part, cols] = (pre * phi).astype(BF)
            slope = phi + pre * (jnp.exp(-0.5 * pre * pre) * 0.3989422804014327)
            gp[part, cols] = slope.astype(BF)
            return carry

        lax.fori_loop(0, ff // width, expand, 0, unroll=True)
        mlp = dot_nn(act[part, :], wfc2[...]) + bias(5)
        mb[part, :] = mlp.astype(BF)
        fout[part, :] = (rb[part, :] + gains[0, 3:4, :] * mlp).astype(BF)

    def forward_block(j, carry):
        part = aligned(j * blk, blk)

        feats = segf[...]
        own_pen = ((segf[part, :].astype(F32) - 1.0) * penalty_row).astype(BF) * first_row

        def attend(trio, carry):
            items = [trio * 3 + i for i in range(3)]
            spans = [aligned(pair * 128, 128) for pair in items]
            scores = []
            for pair, cols in zip(items, spans):
                query = jnp.concatenate(
                    [
                        jnp.concatenate([qaug[2 * pair, part, :] * first_row, own_pen], 1),
                        jnp.concatenate([qaug[2 * pair + 1, part, :] * second_row, own_pen], 1),
                    ],
                    0,
                )
                scores.append(dot_nt(query, jnp.concatenate([kall[:, cols], feats], 1)))
            for pair, cols, score in zip(items, spans, scores):
                peak = jnp.max(score, -1, keepdims=True)
                expo = jnp.exp(score - peak).astype(BF)
                mixed = dot_nn(expo, jnp.concatenate([vall[:, cols], feats], 1))
                total = mixed[:, 132:133]
                outs = mixed[:, 0:128] / total
                log_total = peak + jnp.log(total)
                for i in range(2):
                    base = 64 * (1 - i)
                    extra = three_parts(-log_total[i * blk : (i + 1) * blk], lane_row, base + 4)
                    query = qaug[2 * pair + i, part, :]
                    qaug[2 * pair + i, part, :] = (query.astype(F32) + extra).astype(BF)
                ob[part, cols] = jnp.where(lane_row < 64, outs[:blk], outs[blk:]).astype(BF)
            return carry

        lax.fori_loop(0, pairs // 3, attend, 0, unroll=True)

        @pl.when(j == 0)
        def _():
            for copy in weight_copies[1:]:
                copy.wait()

        @pl.when(is_first)
        def _():
            def feed_half(half, carry):
                feed_forward(aligned(half * half_blk, half_blk))
                x_half(half).start()
                return carry

            lax.fori_loop(2 * j, 2 * j + 2, feed_half, 0)

        @pl.when(is_second)
        def _():
            feed_forward(part)

        return carry

    lax.fori_loop(0, chunks, forward_block, 0)

    n_fc2 = 2 * (width // 128)
    n_fc1 = ff // SLOT_COLS
    n_proj = width // SLOT_COLS
    n_qkv = 3 * width // SLOT_COLS
    lo_fc1 = n_fc2
    lo_proj = lo_fc1 + n_fc1
    lo_qkv = lo_proj + n_proj
    slots = lo_qkv + n_qkv
    mine = jnp.where(is_first, slots - LENT, slots + LENT)
    vslot = slots - LENT - 6
    lent_from = slots - LENT - 1

    def slot_at(m):
        return jnp.where(is_first, m + jnp.minimum(m // (LEND_EVERY - 1), LENT), m)

    def place_of(p):
        return jnp.where(is_first, p - jnp.minimum(p // LEND_EVERY, LENT), p)

    def lent_before(m):
        return jnp.minimum(jnp.maximum(m - lent_from, 0), LENT)

    def own_slot(m):
        return jnp.where(is_first, slot_at(m), m - lent_before(m))

    def is_borrowed(m):
        return is_second & (m >= lent_from) & (m < lent_from + LENT)

    def is_lent(p):
        return is_first & (p % LEND_EVERY == LEND_EVERY - 1) & (p < LENT * LEND_EVERY)

    def core_copy(t):
        at = t % RING
        return pltpu.make_async_remote_copy(
            src_ref=csend.at[at], dst_ref=crecv.at[at],
            send_sem=c_ssem.at[at], recv_sem=c_rsem.at[at],
            device_id=sib, device_id_type=MESH,
        )

    def y_copy(t):
        at = t % YRING
        return pltpu.make_async_remote_copy(
            src_ref=ysend.at[at], dst_ref=yrecv.at[at],
            send_sem=y_ssem.at[at], recv_sem=y_rsem.at[at],
            device_id=ynb, device_id_type=MESH,
        )

    def z_copy(way, t):
        return pltpu.make_async_remote_copy(
            src_ref=zsend.at[way, t % RING], dst_ref=zrecv.at[way, t % ZRING],
            send_sem=z_ssem.at[way, t % RING], recv_sem=z_rsem.at[way, t % ZRING],
            device_id=(zright, zleft)[way], device_id_type=MESH,
        )

    def v_copy(stage, peer):
        return pltpu.make_async_remote_copy(
            src_ref=vsend.at[stage], dst_ref=vrecv.at[stage],
            send_sem=v_ssem.at[stage], recv_sem=v_rsem.at[stage],
            device_id=peer, device_id_type=MESH,
        )

    def lend_copy(e):
        return pltpu.make_async_remote_copy(
            src_ref=lent.at[e], dst_ref=lent.at[e],
            send_sem=l_ssem.at[e], recv_sem=l_rsem.at[e],
            device_id=xnb, device_id_type=MESH,
        )

    def give(which, t, depth, peer, count=None):
        @pl.when(t + depth < (mine if count is None else count))
        def _():
            pl.semaphore_signal(credit.at[which], inc=1, device_id=peer, device_id_type=MESH)

    def take(which, t, depth):
        @pl.when(t >= depth)
        def _():
            pl.semaphore_wait(credit.at[which], 1)

    def out_parts(p, src, act):
        @pl.when(p < lo_fc1)
        def _():
            row = (p // (width // 128)) * (2 * SLOT_ROWS)
            cols = aligned((p % (width // 128)) * 128, 128)
            for i in range(2):
                rows_of = pl.ds(pl.multiple_of(row + i * SLOT_ROWS, SLOT_ROWS), SLOT_ROWS)
                act(src.at[:, i * 128 : (i + 1) * 128], g_fc2.at[rows_of, cols], i)

        for lo, count, ref in ((lo_fc1, n_fc1, g_fc1), (lo_proj, n_proj, g_proj), (lo_qkv, n_qkv, g_qkv)):
            @pl.when((p >= lo) & (p < lo + count))
            def _():
                act(src, ref.at[:, aligned((p - lo) * SLOT_COLS, SLOT_COLS)], 0)

    def own_out(m, method):
        def act(src, dst, i):
            getattr(pltpu.make_async_copy(src, dst, o_sem.at[m % 4, i]), method)()

        out_parts(own_slot(m), ostage.at[m % 4], act)

    def lent_out(e, method):
        def act(src, dst, i):
            copy = pltpu.make_async_remote_copy(
                src_ref=src, dst_ref=dst,
                send_sem=l_ssem.at[LENT + 2 * e + i], recv_sem=l_rsem.at[LENT + 2 * e + i],
                device_id=xnb, device_id_type=MESH,
            )
            getattr(copy, method)()

        out_parts(e * LEND_EVERY + LEND_EVERY - 1, ostage.at[(lent_from + e) % 4], act)

    def out_start(m):
        @pl.when(jnp.logical_not(is_borrowed(m)))
        def _():
            own_out(m, "start")

        @pl.when(is_borrowed(m))
        def _():
            lent_out(m - lent_from, "start")

    def out_wait(m):
        @pl.when(jnp.logical_not(is_borrowed(m)))
        def _():
            own_out(m, "wait")

        @pl.when(is_borrowed(m))
        def _():
            lent_out(m - lent_from, "wait_send")

    def result_stay():
        return pltpu.make_async_copy(fout.at[aligned(yy * blk, blk)], results.at[yy], res_sem.at[0])

    def result_move():
        return pltpu.make_async_remote_copy(
            src_ref=fout.at[aligned((1 - yy) * blk, blk)], dst_ref=results.at[yy],
            send_sem=res_sem.at[1], recv_sem=res_sem.at[2],
            device_id=ynb, device_id_type=MESH,
        )

    def own_terms(q):
        @pl.when(q * 3 >= RING)
        def _():
            for i in range(3):
                core_copy(q * 3 + i - RING).wait_send()

        ring = (q % 2) * 3

        @pl.when(q < lo_fc1 // 3)
        def _():
            row = (q // 2) * (2 * SLOT_ROWS)
            cols = aligned((q % 2) * 384, 384)

            def share(dest, carry):
                got = dot_tn(act[:, aligned(dest * width + row, 2 * SLOT_ROWS)], dmb[:, cols])

                def place(ref, kind):
                    for i in range(3):
                        for half in range(2):
                            ref[ring + i, dest // 2, :, half * 128 : half * 128 + 128] = got[
                                half * SLOT_ROWS : (half + 1) * SLOT_ROWS, i * 128 : (i + 1) * 128
                            ].astype(kind)

                @pl.when(cc == dest % 2)
                def _():
                    place(ckeep, BF)

                @pl.when(cc != dest % 2)
                def _():
                    place(csend, BF)

                return carry

            lax.fori_loop(0, 4, share, 0)

        @pl.when(q >= lo_fc1 // 3)
        def _():
            cols = aligned((q * 3 - lo_fc1) * SLOT_COLS, 3 * SLOT_COLS)
            left = jnp.where(q * 3 < lo_proj, 0, jnp.where(q * 3 < lo_qkv, 1, 2))

            def share(side, carry):
                got = dot_tn(lhs[left, :, aligned(side * 2 * SLOT_ROWS, 2 * SLOT_ROWS)], rhs[:, cols])
                for core in range(2):
                    @pl.when(cc == core)
                    def _():
                        for i in range(3):
                            span = slice(i * SLOT_COLS, (i + 1) * SLOT_COLS)
                            mine, theirs = slice(0, SLOT_ROWS), slice(SLOT_ROWS, 2 * SLOT_ROWS)
                            if core:
                                mine, theirs = theirs, mine
                            ckeep[ring + i, side] = got[mine, span].astype(BF)
                            csend[ring + i, side] = got[theirs, span].astype(BF)

                return carry

            lax.fori_loop(0, 2, share, 0)

    def stage_own(t, carry):
        @pl.when(t % 3 == 0)
        def _():
            own_terms(t // 3)

        take(0, t, RING)
        core_copy(t).start()

        @pl.when(t == own_slot(vslot))
        def _():
            vsend[0, :, 0:width] = vec[...]
            vsend[0, :, width : width + 256] = dcf[...]
            v_copy(0, sib).start()

        return carry

    def stage_chip(p, carry):
        own = jnp.where(is_first, p, p - lent_before(p))
        borrowed = is_borrowed(p)
        at = own % RING
        away = 1 - yy
        t = place_of(p)
        keeps = jnp.logical_not(is_lent(p))

        @pl.when(jnp.logical_not(borrowed))
        def _():
            core_copy(own).wait_recv()

        @pl.when(keeps)
        def _():
            take(1, t, YRING)

            @pl.when(t >= YRING)
            def _():
                y_copy(t - YRING).wait_send()

            @pl.when(jnp.logical_not(borrowed))
            def _():
                ysend[t % YRING] = (ckeep[at, away].astype(F32) + crecv[at, away].astype(F32)).astype(BF)
                rown[t % OWN_RING] = (ckeep[at, yy].astype(F32) + crecv[at, yy].astype(F32)).astype(BF)

            @pl.when(borrowed)
            def _():
                lend_copy(p - lent_from).wait_recv()
                ysend[t % YRING] = lent[p - lent_from, away]
                rown[t % OWN_RING] = lent[p - lent_from, yy]

            y_copy(t).start()

            @pl.when(t == vslot)
            def _():
                v_copy(0, sib).wait()
                vsend[1] = vsend[0] + vrecv[0]
                v_copy(1, ynb).start()

        @pl.when(is_lent(p))
        def _():
            e = p // LEND_EVERY
            for side in range(2):
                lent[e, side] = (ckeep[at, side].astype(F32) + crecv[at, side].astype(F32)).astype(BF)
            lend_copy(e).start()

        @pl.when(jnp.logical_not(borrowed))
        def _():
            give(0, own, RING, sib, slots)

        return carry

    def stage_group(t, carry):
        y_copy(t).wait_recv()
        at = t % OWN_RING
        rown[at] = (rown[at].astype(F32) + yrecv[t % YRING].astype(F32)).astype(BF)
        give(1, t, YRING, ynb)

        @pl.when(t == vslot + 1)
        def _():
            v_copy(1, ynb).wait()
            vsend[2] = vsend[1] + vrecv[1]

        return carry

    def stage_line(way, t, carry):
        has_before = (has_left, has_right)[way]
        has_after = (has_right, has_left)[way]
        behind = (zleft, zright)[way]
        ahead = (zright, zleft)[way]

        @pl.when(has_before)
        def _():
            z_copy(way, t).wait_recv()

        @pl.when(has_after)
        def _():
            take(2 + way, t, ZRING)

            @pl.when(t >= RING)
            def _():
                z_copy(way, t - RING).wait_send()

            @pl.when(has_before)
            def _():
                zsend[way, t % RING] = (
                    rown[t % OWN_RING].astype(F32) + zrecv[way, t % ZRING].astype(F32)
                ).astype(BF)

            @pl.when(jnp.logical_not(has_before))
            def _():
                zsend[way, t % RING] = rown[t % OWN_RING]

            z_copy(way, t).start()

        @pl.when(t == vslot + 1 + (grp if way == 0 else groups - 1 - grp))
        def _():
            @pl.when(has_before)
            def _():
                v_copy(2 + way, behind).wait_recv()

            @pl.when(has_after)
            def _():
                @pl.when(has_before)
                def _():
                    vsend[3 + way] = vsend[2] + vrecv[2 + way]

                @pl.when(jnp.logical_not(has_before))
                def _():
                    vsend[3 + way] = vsend[2]

                v_send(way, ahead).start()

        return carry

    def stage_whole(t, carry):
        at = t % ZRING
        own = rown[t % OWN_RING].astype(F32)

        @pl.when(t >= 4)
        def _():
            out_wait(t - 4)

        @pl.when(has_left & has_right)
        def _():
            ostage[t % 4] = (own + zrecv[0, at].astype(F32) + zrecv[1, at].astype(F32)).astype(BF)

        @pl.when(has_left & jnp.logical_not(has_right))
        def _():
            ostage[t % 4] = (own + zrecv[0, at].astype(F32)).astype(BF)

        @pl.when(has_right & jnp.logical_not(has_left))
        def _():
            ostage[t % 4] = (own + zrecv[1, at].astype(F32)).astype(BF)

        out_start(t)

        @pl.when(has_left)
        def _():
            give(2, t, ZRING, zleft)

        @pl.when(has_right)
        def _():
            give(3, t, ZRING, zright)

        return carry

    def v_send(way, peer):
        return pltpu.make_async_remote_copy(
            src_ref=vsend.at[3 + way], dst_ref=vrecv.at[2 + way],
            send_sem=v_ssem.at[2 + way], recv_sem=v_rsem.at[2 + way],
            device_id=peer, device_id_type=MESH,
        )

    @pl.when(is_second)
    def _():
        result_stay().start()
        result_move().start()
        own_block(cot).wait()
        swap_half(cot, 0).wait()
        swap_half(cot, 1).wait()

    def scale_back(j):
        part = aligned(j * blk, blk)

        @pl.when(is_first)
        def _():
            x_send(cot, dout, j, xb_ssem, xb_rsem).wait_recv()

        grad = cot[part, :].astype(F32)
        vec[3:4, :] += jnp.sum(grad * mb[part, :].astype(F32), 0, keepdims=True)
        low = (gains[0, 3:4, :] * grad).astype(BF)
        dmb[part, :] = low
        vec[9:10, :] += jnp.sum(low.astype(F32), 0, keepdims=True)

    def shrink_back(j):
        part = aligned(j * blk, blk)
        for t in range(ff // width):
            cols = slice(t * width, (t + 1) * width)
            back = dot_nt(dmb[part, :], wfc2[cols, :])
            low = (gp[part, cols].astype(F32) * back).astype(BF)
            du[part, cols] = low
            sums = jnp.sum(low.astype(F32), 0, keepdims=True)
            for i in range(width // 256):
                row = t * (width // 256) + i
                dcf[row : row + 1, :] += sums[:, i * 256 : (i + 1) * 256]

    def middle_back(j):
        part = aligned(j * blk, blk)
        grad_two = dot_nt(du[part, :], wfc1[...])
        hat, rstd = norm_stats(rb[part, :])
        vec[2:3, :] += jnp.sum(grad_two * hat, 0, keepdims=True)
        vec[8:9, :] += jnp.sum(grad_two, 0, keepdims=True)
        middle = cot[part, :].astype(F32) + norm_back(grad_two, hat, rstd, gains[0, 2:3, :])
        drb[part, :] = middle
        vec[1:2, :] += jnp.sum(middle * zb[part, :].astype(F32), 0, keepdims=True)
        low = (gains[0, 1:2, :] * middle).astype(BF)
        dzb[part, :] = low
        vec[7:8, :] += jnp.sum(low.astype(F32), 0, keepdims=True)

    def heads_back(j):
        part = aligned(j * blk, blk)
        grad_o = dot_nt(dzb[part, :], wproj[...]).astype(BF).astype(F32)
        for i in range(pairs):
            cols = slice(i * 128, (i + 1) * 128)
            pair = grad_o[:, cols]
            both = pair * ob[part, cols].astype(F32)
            inner_a = jnp.sum(jnp.where(lane_row < 64, both, 0.0), -1, keepdims=True)
            inner_b = jnp.sum(jnp.where(lane_row < 64, 0.0, both), -1, keepdims=True)
            extra_a = three_parts(-inner_a, lane_row, 68)
            extra_b = three_parts(-inner_b, lane_row, 4)
            doaug[2 * i, part, :] = jnp.where(lane_row < 64, pair, extra_a).astype(BF)
            doaug[2 * i + 1, part, :] = jnp.where(lane_row < 64, extra_b, pair).astype(BF)

    def dkv_copy(index, j):
        part = aligned(j * blk, blk)
        return pltpu.make_async_remote_copy(
            src_ref=dkv_send.at[index, part],
            dst_ref=dkv_recv.at[index, part],
            send_sem=dkv_ssem.at[index, j],
            recv_sem=dkv_rsem.at[index, j],
            device_id=sib,
            device_id_type=MESH,
        )

    def stacked(ref, pair, part):
        first, second = ref[2 * pair, part], ref[2 * pair + 1, part]
        return jnp.concatenate(
            [
                jnp.concatenate([first * first_row, first * second_row], 1),
                jnp.concatenate([second * second_row, second * first_row], 1),
            ],
            0,
        )

    def quadrant(pair, j, part):
        cols = aligned(pair * 128, 128)

        def key_block(ref):
            return jnp.concatenate(
                [ref[j * blk : (j + 1) * blk, cols], ref[rows + j * blk : rows + (j + 1) * blk, cols]], 0
            )

        feats = jnp.concatenate([segf[j * blk : (j + 1) * blk], segf[rows + j * blk : rows + (j + 1) * blk]], 0)
        keys, values = key_block(kall), key_block(vall)
        query, outer = stacked(qaug, pair, part), stacked(doaug, pair, part)
        prob = jnp.exp(dot_nt(jnp.concatenate([keys, feats], 1), query))
        diff = dot_nt(jnp.concatenate([values, feats], 1), outer)
        slope = (prob * diff).astype(BF)
        dq = dot_tn(slope, keys)
        count = dq.shape[0] // 2
        return (
            jnp.where(lane_row < 64, dq[:count], dq[count:]),
            dot_nn(slope, query[:, 0:128]),
            dot_nn(prob.astype(BF), outer[:, 0:128]),
        )

    def pair_spans(pair):
        return [aligned(third * width + pair * 128, 128) for third in range(3)]

    def attend_back_first(pair):
        dq_w, dk_w, dv_w = quadrant(pair, 0, slice(0, rows))
        dq_n, dk_n, dv_n = quadrant(pair, 1, slice(0, blk))
        q_cols, k_cols, v_cols = pair_spans(pair)
        dkv_send[pair, 0:blk] = dk_w[blk:].astype(BF)
        dkv_send[pairs + pair, 0:blk] = dv_w[blk:].astype(BF)
        dkv_copy(pair, 0).start()
        dkv_copy(pairs + pair, 0).start()
        dkv_send[pair, blk:] = dk_n[blk:].astype(BF)
        dkv_send[pairs + pair, blk:] = dv_n[blk:].astype(BF)
        dqkv[0:blk, q_cols] = ((dq_w[0:blk] + dq_n) * 0.125).astype(BF)
        dqkv[blk:, q_cols] = (dq_w[blk:] * 0.125).astype(BF)
        dqkv[0:blk, k_cols] = dk_w[0:blk].astype(BF)
        dqkv[blk:, k_cols] = dk_n[0:blk].astype(BF)
        dqkv[0:blk, v_cols] = dv_w[0:blk].astype(BF)
        dqkv[blk:, v_cols] = dv_n[0:blk].astype(BF)

    def attend_back_second(duo):
        found = [quadrant(2 * duo + i, 1, slice(blk, rows)) for i in range(2)]
        for i in range(2):
            second_sums(2 * duo + i, *found[i])

    def second_sums(pair, dq, dk, dv):
        q_cols, k_cols, v_cols = pair_spans(pair)
        for index, term in ((pair, dk), (pairs + pair, dv)):
            dkv_send[index, blk:] = (dkv_send[index, blk:].astype(F32) + term[blk:]).astype(BF)
            dkv_copy(index, 1).start()
        for cols, term in ((q_cols, dq * 0.125), (k_cols, dk[0:blk]), (v_cols, dv[0:blk])):
            dqkv[blk:, cols] = (dqkv[blk:, cols].astype(F32) + term).astype(BF)

    def finish_back(j):
        part = aligned(j * blk, blk)

        for index in range(2 * pairs):
            dkv_copy(index, j).wait()
        for index in range(2 * pairs):
            cols = slice(width + index * 128, width + (index + 1) * 128)
            dqkv[part, cols] = (dqkv[part, cols].astype(F32) + dkv_recv[index, part].astype(F32)).astype(BF)

        @pl.when(is_first & (j == 0))
        def _():
            for half in range(4):
                x_half(half).wait_send()

        @pl.when(is_second & (j == 0))
        def _():
            result_stay().wait()
            result_move().wait_send()

        grad_one = dot_nt(dqkv[part, :], wqkv[...])
        hat, rstd = norm_stats(hin[part, :].astype(F32))
        total = drb[part, :] + norm_back(grad_one, hat, rstd, gains[0, 0:1, :])
        dout[part, :] = total.astype(BF)

        @pl.when(is_second)
        def _():
            x_send(cot, dout, j, xb_ssem, xb_rsem).start()

        vec[0:1, :] += jnp.sum(grad_one * hat, 0, keepdims=True)
        vec[4:5, :] += jnp.sum(grad_one, 0, keepdims=True)
        vec[5:6, :] += jnp.sum(dqkv[part, 0:width].astype(F32), 0, keepdims=True)
        vec[6:7, :] += jnp.sum(dqkv[part, 2 * width : 3 * width].astype(F32), 0, keepdims=True)

    per_block = 4
    dense = chunks * per_block
    first_end = dense + pairs
    second_end = first_end + 1 + pairs // 2

    beside = 22

    def pieces_done(v):
        total = second_end + 1
        first = per_block + 1
        spread = jnp.minimum(first + (v * (total - first) + beside - 1) // beside, total)
        return jnp.where(v < 0, 0, jnp.where(is_first, spread, total))

    def advance(stage, lag, count, v, at=lambda m: m):
        def done(v):
            return jnp.minimum(jnp.maximum(v + 1 - lag, 0), count)

        lax.fori_loop(at(done(v - 1)), at(done(v)), stage, 0)

    late = jnp.maximum(grp, groups - 1 - grp)
    chip_lag, group_lag, hop_lag = 2, 4, 2
    visits = mine + group_lag + hop_lag * (groups - 1)

    def piece(w, carry):
        @pl.when(w < dense)
        def _():
            j, r = w // per_block, w % per_block

            @pl.when(r == 0)
            def _():
                scale_back(j)

            @pl.when(r == 1)
            def _():
                shrink_back(j)

            @pl.when(r == 2)
            def _():
                middle_back(j)

            @pl.when(r == 3)
            def _():
                heads_back(j)

        @pl.when((w >= dense) & (w < first_end))
        def _():
            attend_back_first(w - dense)

        @pl.when((w > first_end) & (w < second_end))
        def _():
            attend_back_second(w - first_end - 1)

        @pl.when((w == first_end) | (w == second_end))
        def _():
            finish_back((w - first_end) // (pairs // 2 + 1))

        return carry

    def visit(v, carry):
        lax.fori_loop(pieces_done(v - 1), pieces_done(v), piece, 0)
        advance(stage_own, 0, mine, v, own_slot)
        advance(stage_chip, chip_lag, mine, v, slot_at)
        advance(stage_group, group_lag, mine, v)
        for way in range(2):
            place = grp if way == 0 else groups - 1 - grp
            advance(functools.partial(stage_line, way), group_lag + hop_lag * place, mine, v)
        advance(stage_whole, group_lag + hop_lag * late, mine, v)

        @pl.when(is_first & (v == mine + 1))
        def _():
            result_stay().start()
            result_move().start()

        return carry

    lax.fori_loop(0, visits, visit, 0)

    def drain(i, carry):
        y_copy(mine - YRING + i).wait_send()

        @pl.when(i < 4)
        def _():
            out_wait(mine - 4 + i)

        @pl.when(i < RING)
        def _():
            core_copy(slots - RING + i).wait_send()

            @pl.when(has_right)
            def _():
                z_copy(0, mine - RING + i).wait_send()

            @pl.when(has_left)
            def _():
                z_copy(1, mine - RING + i).wait_send()

        return carry

    lax.fori_loop(0, YRING, drain, 0)

    @pl.when(is_first)
    def _():
        for e in range(LENT):
            lend_copy(e).wait_send()
            lent_out(e, "wait_recv")

    @pl.when(has_right)
    def _():
        v_send(0, zright).wait_send()

    @pl.when(has_left)
    def _():
        v_send(1, zleft).wait_send()

    total = vsend[2]
    vec_out[...] = total

    @pl.when(has_left)
    def _():
        vec_out[...] = vec_out[...] + vrecv[2]

    @pl.when(has_right)
    def _():
        vec_out[...] = vec_out[...] + vrecv[3]

    @pl.when(is_first)
    def _():
        result_stay().wait()
        result_move().wait_send()

    @pl.when(is_second)
    def _():
        for j in range(chunks):
            x_send(cot, dout, j, xb_ssem, xb_rsem).wait_send()

    result_move().wait_recv()

HEADS = 12
HDIM = 64


def from_behind(block, axis, distance):
    devices = range(lax.axis_size(axis))
    route = [(i - distance, i) for i in devices if i - distance in devices]
    return lax.ppermute(block, axis, route)


def normalize(values, scale_vec, shift_vec):
    row_mean = jnp.mean(values, -1, keepdims=True)
    centered = values - row_mean
    variance = jnp.mean(centered * centered, -1, keepdims=True)
    return centered * lax.rsqrt(variance + 1e-06) * scale_vec + shift_vec


def gelu_exact(values):
    return jax.nn.gelu(values, approximate=False)


def back_dot(left, weight):
    return lax.dot_general(
        left, weight, (((1,), (1,)), ((), ())), preferred_element_type=jnp.float32
    )


def row_contract(left, right):
    return lax.dot_general(
        left, right, (((0,), (0,)), ((), ())), preferred_element_type=jnp.float32
    )


def masked_scores(query, keys_all, seg_row):
    row_count = query.shape[0]
    length = keys_all.shape[0]
    start = lax.axis_index("narrow") * row_count
    own_seg = lax.dynamic_slice_in_dim(seg_row, start, row_count)
    same = own_seg[:, None] == seg_row[None, :]
    raw = (
        jnp.einsum(
            "qhd,khd->hqk",
            query.reshape(row_count, HEADS, HDIM),
            keys_all.reshape(length, HEADS, HDIM),
            preferred_element_type=jnp.float32,
        )
        * 0.125
    )
    return jnp.where(same[None], raw, -1e30)


def forward_layer(inputs, seg_row, weights):
    qkv_w, proj_w, fc1_w, fc2_w, gain_rows, bias_rows, fc1_b = weights
    row_count, model_width = inputs.shape
    normed = normalize(inputs, gain_rows[0], bias_rows[0]).astype(jnp.bfloat16)
    qkv = jnp.dot(normed, qkv_w, preferred_element_type=jnp.float32)
    query = (qkv[:, :model_width] + bias_rows[1]).astype(jnp.bfloat16)
    key_rows = qkv[:, model_width : 2 * model_width].astype(jnp.bfloat16)
    value_rows = (qkv[:, 2 * model_width :] + bias_rows[2]).astype(jnp.bfloat16)
    keys_all, values_all = (
        lax.all_gather(key_rows, "narrow", axis=0, tiled=True),
        lax.all_gather(value_rows, "narrow", axis=0, tiled=True),
    )
    length = keys_all.shape[0]
    scores = masked_scores(query, keys_all, seg_row)
    peak = jnp.max(scores, -1, keepdims=True)
    log_total = peak + jnp.log(jnp.sum(jnp.exp(scores - peak), -1, keepdims=True))
    probs = jnp.exp(scores - log_total).astype(jnp.bfloat16)
    mixed = jnp.einsum(
        "hqk,khd->qhd",
        probs,
        values_all.reshape(length, HEADS, HDIM),
        preferred_element_type=jnp.float32,
    )
    attended = mixed.reshape(row_count, model_width).astype(jnp.bfloat16)
    branch = jnp.dot(attended, proj_w, preferred_element_type=jnp.float32) + bias_rows[3]
    middle = inputs + gain_rows[1] * branch
    normed_two = normalize(middle, gain_rows[2], bias_rows[4]).astype(jnp.bfloat16)
    hidden_pre = jnp.dot(normed_two, fc1_w, preferred_element_type=jnp.float32) + fc1_b
    activated = gelu_exact(hidden_pre).astype(jnp.bfloat16)
    mlp_out = jnp.dot(activated, fc2_w, preferred_element_type=jnp.float32) + bias_rows[5]
    output = middle + gain_rows[3] * mlp_out
    saved = (
        inputs,
        query,
        keys_all,
        values_all,
        log_total,
        attended,
        branch,
        middle,
        hidden_pre,
        mlp_out,
    )
    return (output, saved)


def backward_layer(grad_out, saved, seg_row, weights):
    qkv_w, proj_w, fc1_w, fc2_w, gain_rows, bias_rows, fc1_b = weights
    (
        inputs,
        query,
        keys_all,
        values_all,
        log_total,
        attended,
        branch,
        middle,
        hidden_pre,
        mlp_out,
    ) = saved
    row_count, model_width = inputs.shape
    length = keys_all.shape[0]
    scale_two = jnp.sum(grad_out * mlp_out, 0)
    mlp_grad = (gain_rows[3] * grad_out).astype(jnp.bfloat16)
    activated, gelu_pull = jax.vjp(gelu_exact, hidden_pre)
    grad_fc2 = row_contract(activated.astype(jnp.bfloat16), mlp_grad)
    shift_five = jnp.sum(mlp_grad.astype(jnp.float32), 0)
    pre_grad = gelu_pull(back_dot(mlp_grad, fc2_w))[0].astype(jnp.bfloat16)
    normed_two, norm_pull_two = jax.vjp(normalize, middle, gain_rows[2], bias_rows[4])
    grad_fc1 = row_contract(normed_two.astype(jnp.bfloat16), pre_grad)
    grad_fc1b = jnp.sum(pre_grad.astype(jnp.float32), 0)
    middle_part, gain_two, shift_four = norm_pull_two(back_dot(pre_grad, fc1_w))
    middle_grad = grad_out + middle_part
    scale_one = jnp.sum(middle_grad * branch, 0)
    branch_grad = (gain_rows[1] * middle_grad).astype(jnp.bfloat16)
    grad_proj = row_contract(attended, branch_grad)
    shift_three = jnp.sum(branch_grad.astype(jnp.float32), 0)
    heads_grad = back_dot(branch_grad, proj_w).astype(jnp.bfloat16).reshape(row_count, HEADS, HDIM)
    scores = masked_scores(query, keys_all, seg_row)
    probs = jnp.exp(scores - log_total)
    keys_heads = keys_all.reshape(length, HEADS, HDIM)
    prob_grad = jnp.einsum(
        "qhd,khd->hqk",
        heads_grad,
        values_all.reshape(length, HEADS, HDIM),
        preferred_element_type=jnp.float32,
    )
    inner = jnp.sum(probs * prob_grad, -1, keepdims=True)
    score_grad = (probs * (prob_grad - inner)).astype(jnp.bfloat16)
    query_grad = (
        (
            jnp.einsum("hqk,khd->qhd", score_grad, keys_heads, preferred_element_type=jnp.float32)
            * 0.125
        )
        .reshape(row_count, model_width)
        .astype(jnp.bfloat16)
    )
    key_part = (
        jnp.einsum(
            "hqk,qhd->khd",
            score_grad,
            query.reshape(row_count, HEADS, HDIM),
            preferred_element_type=jnp.float32,
        )
        * 0.125
    ).reshape(length, model_width)
    value_part = jnp.einsum(
        "hqk,qhd->khd", probs.astype(jnp.bfloat16), heads_grad, preferred_element_type=jnp.float32
    ).reshape(length, model_width)
    key_sum, value_sum = (
        lax.psum_scatter(
            key_part.astype(jnp.bfloat16), "narrow", scatter_dimension=0, tiled=True
        ).astype(jnp.float32),
        lax.psum_scatter(
            value_part.astype(jnp.bfloat16), "narrow", scatter_dimension=0, tiled=True
        ).astype(jnp.float32),
    )
    key_grad = key_sum.astype(jnp.bfloat16)
    value_grad = value_sum.astype(jnp.bfloat16)
    qkv_grad = jnp.concatenate([query_grad, key_grad, value_grad], 1)
    normed, norm_pull_one = jax.vjp(normalize, inputs, gain_rows[0], bias_rows[0])
    grad_qkv = row_contract(normed.astype(jnp.bfloat16), qkv_grad)
    input_part, gain_one, shift_zero = norm_pull_one(back_dot(qkv_grad, qkv_w))
    input_grad = middle_grad + input_part
    gain_grads = jnp.stack([gain_one, scale_one, gain_two, scale_two])
    shift_grads = jnp.stack(
        [
            shift_zero,
            jnp.sum(query_grad.astype(jnp.float32), 0),
            jnp.sum(value_grad.astype(jnp.float32), 0),
            shift_three,
            shift_four,
            shift_five,
        ]
    )
    return (
        input_grad,
        (grad_qkv, grad_proj, grad_fc1, grad_fc2, gain_grads, shift_grads, grad_fc1b),
    )


def general_body(
    boundary, segments, qkv_weight, proj_weight, fc1_weight, fc2_weight, gains, biases, fc1_bias
):
    weights = (
        qkv_weight[0],
        proj_weight[0],
        fc1_weight[0],
        fc2_weight[0],
        gains[0],
        biases[0],
        fc1_bias[0],
    )
    local_ends = boundary[0]
    micro_count = local_ends.shape[0]
    first_section = lax.axis_index("section") == 0
    arrived = jnp.zeros(local_ends.shape[1:], jnp.bfloat16)
    stored = []
    outputs = []
    for step_index in range(micro_count + 1):
        lower = min(step_index, micro_count - 1)
        upper = max(step_index - 1, 0)
        inputs = jnp.where(
            first_section, local_ends[lower].astype(jnp.float32), arrived.astype(jnp.float32)
        )
        seg_row = jnp.where(first_section, segments[lower], segments[upper])
        output, saved = forward_layer(inputs, seg_row, weights)
        stored.append((saved, seg_row))
        outputs.append(output)
        if step_index < micro_count:
            arrived = from_behind(output.astype(jnp.bfloat16), "section", 1)
    totals = tuple((jnp.zeros(w.shape, jnp.float32) for w in weights))
    returned = jnp.zeros(local_ends.shape[1:], jnp.bfloat16)
    input_grads = []
    for step_index in range(micro_count + 1):
        lower = min(step_index, micro_count - 1)
        upper = max(step_index - 1, 0)
        picked = jax.tree.map(
            lambda early, later: jnp.where(first_section, early, later),
            stored[upper],
            stored[lower + 1],
        )
        cotangent = jnp.where(
            first_section, returned.astype(jnp.float32), local_ends[lower].astype(jnp.float32)
        )
        is_valid = jnp.where(first_section, step_index >= 1, step_index < micro_count)
        cotangent = jnp.where(is_valid, cotangent, 0.0)
        grad_in, pieces = backward_layer(cotangent, picked[0], picked[1], weights)
        totals = tuple((acc + part for acc, part in zip(totals, pieces)))
        input_grads.append(grad_in)
        if step_index < micro_count:
            returned = from_behind(grad_in.astype(jnp.bfloat16), "section", -1)
    results = jnp.stack(
        [jnp.where(first_section, input_grads[j + 1], outputs[j + 1]) for j in range(micro_count)]
    )
    results = results.astype(jnp.bfloat16)
    within = (
        lax.psum_scatter(
            totals[0].astype(jnp.bfloat16), "narrow", scatter_dimension=0, tiled=True
        ).astype(jnp.float32),
        lax.psum_scatter(
            totals[1].astype(jnp.bfloat16), "narrow", scatter_dimension=0, tiled=True
        ).astype(jnp.float32),
        lax.psum_scatter(
            totals[2].astype(jnp.bfloat16), "narrow", scatter_dimension=0, tiled=True
        ).astype(jnp.float32),
        lax.psum_scatter(
            totals[3].astype(jnp.bfloat16), "narrow", scatter_dimension=0, tiled=True
        ).astype(jnp.float32),
        lax.psum_scatter(
            totals[4].astype(jnp.bfloat16), "narrow", scatter_dimension=1, tiled=True
        ).astype(jnp.float32),
        lax.psum_scatter(
            totals[5].astype(jnp.bfloat16), "narrow", scatter_dimension=1, tiled=True
        ).astype(jnp.float32),
        lax.psum_scatter(
            totals[6].astype(jnp.bfloat16), "narrow", scatter_dimension=0, tiled=True
        ).astype(jnp.float32),
    )
    final = (
        lax.psum(within[0].astype(jnp.bfloat16), "group").astype(jnp.float32),
        lax.psum(within[1].astype(jnp.bfloat16), "group").astype(jnp.float32),
        lax.psum(within[2].astype(jnp.bfloat16), "group").astype(jnp.float32),
        lax.psum(within[3].astype(jnp.bfloat16), "group").astype(jnp.float32),
        lax.psum(within[4].astype(jnp.bfloat16), "group").astype(jnp.float32),
        lax.psum(within[5].astype(jnp.bfloat16), "group").astype(jnp.float32),
        lax.psum(within[6].astype(jnp.bfloat16), "group").astype(jnp.float32),
    )
    return (
        results[None],
        final[0][None],
        final[1][None],
        final[2][None],
        final[3][None],
        final[4][None],
        final[5][None],
        final[6][None],
    )


def fused_body(
    groups, boundary, segments, qkv_weight, proj_weight, fc1_weight, fc2_weight, gains, biases, fc1_bias
):
    blk, width = boundary.shape[2:]
    rows, keys = 2 * blk, 4 * blk
    ff = fc1_weight.shape[2]
    heads = width // HDIM
    nar = lax.axis_index(NARROW)

    def bf(*shape):
        return pltpu.VMEM(shape, BF)

    def f32(*shape):
        return pltpu.VMEM(shape, F32)

    dma = pltpu.SemaphoreType.DMA
    slot = (SLOT_ROWS, SLOT_COLS)
    scratch = [
        bf(width, 3 * width), bf(width, width), bf(width, ff), bf(ff, width),
        bf(rows, width), bf(rows, width), bf(3, rows, width), bf(heads, rows, 128),
        bf(keys, width), bf(keys, width), bf(rows, width), f32(rows, width),
        bf(rows, ff + 4 * width), bf(rows, ff), bf(rows, width), bf(rows, width),
        bf(rows, width), bf(heads, rows, 128), bf(heads, rows, 128), bf(heads, rows, 128),
        bf(keys, 128), bf(RING, 2, *slot), bf(RING, 2, *slot), bf(RING, 2, *slot),
        bf(YRING, *slot), bf(YRING, *slot), bf(OWN_RING, *slot), bf(2, RING, *slot), bf(2, ZRING, *slot), bf(4, *slot),
        f32(16, width), f32(16, 256), f32(5, 16, width + 256), f32(4, 16, width + 256), bf(LENT, 2, *slot),
        dma((4,)), dma(()), dma((2, 2)), dma((2, 4)), dma((2, 4)), dma((4,)), dma((4,)), dma((2,)), dma((2,)),
        dma((heads, 2)), dma((heads, 2)), dma((3,)),
        dma((RING,)), dma((RING,)), dma((YRING,)), dma((YRING,)), dma((2, RING)), dma((2, ZRING)), dma((4, 2)),
        dma((4,)), dma((4,)), dma((3 * LENT,)), dma((3 * LENT,)), pltpu.SemaphoreType.REGULAR((4,)),
    ]
    hbm = pl.BlockSpec(memory_space=pl.ANY)
    vmem = pl.BlockSpec(memory_space=pltpu.VMEM)
    out = pl.pallas_call(
        functools.partial(kernel, groups),
        out_shape=(
            jax.ShapeDtypeStruct((2, blk, width), BF),
            jax.ShapeDtypeStruct((width // 4, 3 * width), BF),
            jax.ShapeDtypeStruct((width // 4, width), BF),
            jax.ShapeDtypeStruct((width // 4, ff), BF),
            jax.ShapeDtypeStruct((ff // 4, width), BF),
            jax.ShapeDtypeStruct((16, width + 256), F32),
        ),
        in_specs=[hbm, vmem, hbm, hbm, hbm, hbm, vmem, vmem, vmem],
        out_specs=(hbm, hbm, hbm, hbm, hbm, vmem),
        scratch_shapes=scratch,
        compiler_params=pltpu.CompilerParams(
            collective_id=0, has_side_effects=True, vmem_limit_bytes=63 * 2**20
        ),
        name="two_layers",
    )(boundary, segments, qkv_weight, proj_weight, fc1_weight, fc2_weight, gains, biases.reshape(1, -1), fc1_bias)
    results, qkv, proj, fc1, fc2, vecs = out
    return widen(results, qkv, proj, fc1, fc2, vecs)


def widen_kernel(results, qkv, proj, fc1, fc2, vecs, *outs):
    o_results, o_qkv, o_proj, o_fc1, o_fc2, o_gains, o_biases, o_fc1b = outs
    o_results[0] = results[...]
    for src, dst in ((qkv, o_qkv), (proj, o_proj), (fc1, o_fc1), (fc2, o_fc2)):
        dst[0] = src[...].astype(F32)

    @pl.when(pl.program_id(0) == 0)
    def _():
        nar = lax.axis_index(NARROW)
        share = o_gains.shape[2]
        parts = o_fc1b.shape[1] // 256
        for i in range(4):
            @pl.when(nar == i)
            def _():
                cols = slice(i * share, (i + 1) * share)
                o_gains[0] = vecs[0:4, cols]
                for row in range(6):
                    o_biases[row] = vecs[4 + row : 5 + row, cols]
                for part in range(parts):
                    o_fc1b[:, part * 256 : (part + 1) * 256] = vecs[
                        i * parts + part : i * parts + part + 1, 4 * share :
                    ]


def widen(results, qkv, proj, fc1, fc2, vecs):
    steps = 2

    def block(shape, lead):
        size = (shape[0] // steps,) + shape[1:]
        rest = (0,) * (len(shape) - 1)
        if lead:
            return pl.BlockSpec((1,) + size, lambda i: (0, i) + rest)
        return pl.BlockSpec(size, lambda i: (i,) + rest)

    def whole(shape):
        return pl.BlockSpec(shape, lambda i: (0,) * len(shape))

    halves, rows, width = results.shape
    flat = results.reshape(halves * rows, width)
    flats = (flat, qkv, proj, fc1, fc2)
    share = width // 4
    small = ((1, 4, share), (6, 1, share), (1, fc2.shape[0]))
    out = pl.pallas_call(
        widen_kernel,
        grid=(steps,),
        in_specs=[block(a.shape, False) for a in flats] + [whole(vecs.shape)],
        out_specs=[block(a.shape, True) for a in flats] + [whole(s) for s in small],
        out_shape=[jax.ShapeDtypeStruct((1,) + a.shape, BF if i == 0 else F32) for i, a in enumerate(flats)]
        + [jax.ShapeDtypeStruct(s, F32) for s in small],
        name="widen",
    )(*flats, vecs)
    return (
        out[0].reshape(1, halves, rows, width),
        *out[1:6],
        out[6].transpose(1, 0, 2),
        out[7],
    )


def solution(mesh):
    sections, groups, narrow = (mesh.shape[name] for name in (SECTION, GROUP, NARROW))
    placed = (
        P("section", "group", "narrow", None),
        P("group", None),
        P("section", None, None),
        P("section", None, None),
        P("section", None, None),
        P("section", None, None),
        P("section", None, None),
        P("section", None, None),
        P("section", None),
    )
    fused = sections == 2 and narrow == 4 and groups > 1
    body = functools.partial(fused_body, groups) if fused else general_body
    return jax.shard_map(
        body,
        mesh=mesh,
        in_specs=placed,
        out_specs=(
            P("section", "group", "narrow", None),
            P("section", "narrow", None),
            P("section", "narrow", None),
            P("section", "narrow", None),
            P("section", "narrow", None),
            P("section", None, "narrow"),
            P("section", None, "narrow"),
            P("section", "narrow"),
        ),
        check_vma=False,
    )
```
